128 devices in a mesh: row: 16 (over x, z), col: 8 (over y, core).
Axes of the slice: x: 4, y: 4, z: 4, core: 2. Of those that a mesh axis runs over, the one named last changes fastest.
Arguments:
- winter: bfloat16 [256, 256, 1024], P(None, 'row', 'col'), may hold values from -6 to 6
- summer: bfloat16 [256, 256, 1024], P(None, 'row', 'col'), may hold values from -6 to 6
- offsets: int32 [2, 16, 8], replicated, may hold values from -1 to 1, as said below
- feat_weight: bfloat16 [256, 2304], replicated, may hold values from -0.125 to 0.125
- bn_gain: float32 [81], replicated, may hold values from 0.5 to 1.5
- bn_shift: float32 [81], replicated, may hold values from -3 to 3
- w_first: bfloat16 [64, 729], replicated, may hold values from -0.21875 to 0.21875
- w_second: bfloat16 [32, 576], replicated, may hold values from -0.25 to 0.25
- cotangent: bfloat16 [32, 256, 1024], P(None, 'row', 'col'), may hold values from -6 to 6
Outputs:
- refined: bfloat16 [32, 256, 1024], P(None, 'row', 'col')
- grad_winter: bfloat16 [256, 256, 1024], P(None, 'row', 'col')
- grad_summer: bfloat16 [256, 256, 1024], P(None, 'row', 'col')
- grad_feat: float32 [256, 2304], replicated
- grad_first: float32 [64, 729], replicated
- grad_second: float32 [32, 576], replicated
- grad_gain: float32 [81], replicated
- grad_shift: float32 [81], replicated
The draws below stay inside these ranges and needn't reach their ends.
Inputs may be any that keep to these rules, and one draw needn't show every extreme that they name: `offsets`: each offset keeps the summer tile inside the scene.
All inputs are finite; a program needn't handle non-finite values.
Results may differ from the reference program's by a relative error of at most 0.02.
Values may be sent and summed in bfloat16 or wider, within the bound.
A program may use at most 384 MiB of HBM per device.

```python
import math
import jax
import jax.numpy as jnp
from jax import lax

C = 256
D1 = 64
D2 = 32
RADIUS = 4
DISP = 81
TR = 16
TC = 128
NH = 256
NW = 1024
N_ROW = 16
N_COL = 8


def draw_offsets(key, part):
    steps = jax.random.randint(key, (2, N_ROW, N_COL), -1, 2).astype(jnp.int32)
    row_ids = jnp.arange(N_ROW, dtype=jnp.int32)[:, None] + jnp.zeros((1, N_COL), jnp.int32)
    col_ids = jnp.arange(N_COL, dtype=jnp.int32)[None, :] + jnp.zeros((N_ROW, 1), jnp.int32)
    row_target = row_ids + steps[0]
    col_target = col_ids + steps[1]
    row_steps = jnp.where((row_target < 0) | (row_target >= N_ROW), -steps[0], steps[0])
    col_steps = jnp.where((col_target < 0) | (col_target >= N_COL), -steps[1], steps[1])
    offsets = jnp.stack([row_steps, col_steps])
    offsets = offsets.at[:, 0, 0].set(1)
    offsets = offsets.at[:, N_ROW - 1, N_COL - 1].set(-1)
    return offsets.astype(jnp.int32)


def block_scale(key, dims, cuts, smallest, high):
    def one(dim, shards_of):
        steps = jax.random.uniform(jax.random.fold_in(jax.random.fold_in(key, 6), dim), (shards_of,), jnp.float32, smallest / len(cuts), high / len(cuts))
        return jnp.repeat(jnp.exp(steps), dims[dim] // shards_of).reshape((-1,) + (1,) * (len(dims) - dim - 1))

    level = one(*cuts[0])
    for cut in cuts[1:]:
        level = level * one(*cut)
    return level


def noise(key, shape, scale, limit, cuts=(), kind=jnp.bfloat16):
    values = scale * jax.random.normal(key, shape, jnp.float32)
    if cuts:
        values = values * block_scale(key, shape, cuts, -0.22, 0.18)
    return jnp.clip(values, -limit, limit).astype(kind)


def setup_inputs(seed: int = 0) -> dict:
    splits = jax.random.split(jax.random.key(seed), 10)
    winter = noise(splits[0], (C, NH, NW), 1.0, 6.0, ((1, 16), (2, 8)))
    summer = noise(splits[1], (C, NH, NW), 1.0, 6.0, ((1, 16), (2, 8)))
    offsets = draw_offsets(jax.random.fold_in(splits[9], 71), 0)
    feat_weight = noise(splits[3], (C, 9 * C), (9 * C) ** -0.5, 0.125)
    bn_gain = jnp.clip(1.0 + 0.1 * jax.random.normal(splits[4], (DISP,), jnp.float32), 0.5, 1.5)
    bn_shift = noise(splits[5], (DISP,), 0.5, 3.0, (), jnp.float32)
    w_first = noise(splits[6], (D1, 9 * DISP), (9 * DISP) ** -0.5, 0.21875)
    w_second = noise(splits[7], (D2, 9 * D1), (9 * D1) ** -0.5, 0.25)
    cotangent = noise(splits[8], (D2, NH, NW), 1.0, 6.0, ((1, 16), (2, 8)))
    return {"winter": winter, "summer": summer, "offsets": offsets, "feat_weight": feat_weight, "bn_gain": bn_gain, "bn_shift": bn_shift, "w_first": w_first, "w_second": w_second, "cotangent": cotangent}


def silu_slope(value):
    sigma = jax.nn.sigmoid(value)
    return sigma * (1.0 + value * (1.0 - sigma))

def conv_valid(padded, weight):
    out_channels = weight.shape[0]
    in_channels = padded.shape[1]
    kernel = weight.reshape(out_channels, 3, 3, in_channels).transpose(0, 3, 1, 2)
    return lax.conv_general_dilated(padded, kernel, (1, 1), 'VALID', dimension_numbers=('NCHW', 'OIHW', 'NCHW'), preferred_element_type=jnp.float32)

def flip_weight(weight, in_channels):
    out_channels = weight.shape[0]
    return weight.reshape(out_channels, 9, in_channels)[:, ::-1, :].transpose(2, 1, 0).reshape(in_channels, 9 * out_channels)

def weight_term(grad, padded):
    height = grad.shape[2]
    wide_cols = grad.shape[3]
    grad_wide = grad.astype(jnp.float32)
    products_list = []
    for shift_row in range(3):
        for shift_col in range(3):
            window = padded[:, :, shift_row:shift_row + height, shift_col:shift_col + wide_cols].astype(jnp.float32)
            products_list.append(jnp.einsum('nchw,ndhw->cd', grad_wide, window))
    return jnp.stack(products_list, 1).reshape(grad.shape[1], -1)

def pad_plane(field, rim_cells):
    return jnp.pad(field, ((0, 0), (rim_cells, rim_cells), (rim_cells, rim_cells)))

def correlate(winter_tile, matched):
    channels, height, tile_cols = winter_tile.shape
    disp_side = 2 * RADIUS + 1
    wide_cols = tile_cols + 2 * RADIUS
    corr_scale = 1.0 / math.sqrt(channels)
    features = winter_tile.astype(jnp.float32)
    pieces = []
    for row_shift in range(disp_side):
        strip_rows = matched[:, row_shift:row_shift + height, :].astype(jnp.float32)
        products = jnp.einsum('cij,cim->ijm', features, strip_rows)
        flattened = jnp.pad(products.reshape(height, tile_cols * wide_cols), ((0, 0), (0, tile_cols)))
        band_cut = flattened.reshape(height, tile_cols, wide_cols + 1)[:, :, :disp_side]
        pieces.append(band_cut.transpose(2, 0, 1))
    return jnp.concatenate(pieces, 0) * corr_scale

def correlate_back(grad_volume, winter_tile, matched):
    channels, height, tile_cols = winter_tile.shape
    disp_side = 2 * RADIUS + 1
    wide_cols = tile_cols + 2 * RADIUS
    corr_scale = 1.0 / math.sqrt(channels)
    features = winter_tile.astype(jnp.float32)
    grad_feat = jnp.zeros(winter_tile.shape, jnp.float32)
    grad_block = jnp.zeros(matched.shape, jnp.float32)
    for row_shift in range(disp_side):
        band_cut = grad_volume[row_shift * disp_side:(row_shift + 1) * disp_side].astype(jnp.float32).transpose(1, 2, 0)
        placed = jnp.pad(band_cut, ((0, 0), (0, 0), (0, tile_cols)))
        placed = placed.reshape(height, tile_cols * (wide_cols + 1))[:, :tile_cols * wide_cols].reshape(height, tile_cols, wide_cols)
        strip_rows = matched[:, row_shift:row_shift + height, :].astype(jnp.float32)
        grad_feat = grad_feat + jnp.einsum('ijm,cim->cij', placed, strip_rows)
        grad_block = grad_block.at[:, row_shift:row_shift + height, :].add(jnp.einsum('ijm,cij->cim', placed, features))
    return (grad_feat * corr_scale, grad_block * corr_scale)

def reference(winter, summer, offsets, feat_weight, bn_gain, bn_shift, w_first, w_second, cotangent):
    channels = winter.shape[0]
    height = NH
    full_width = NW
    tile_count = N_ROW * N_COL
    rim_width = RADIUS + 1
    pixel_count = float(height * full_width)

    def tile_view(field):
        layers = field.shape[0]
        return field.reshape(layers, N_ROW, TR, N_COL, TC).transpose(1, 3, 0, 2, 4).reshape(tile_count, layers, TR, TC)

    def plane_view(stacked):
        layers = stacked.shape[1]
        return stacked.reshape(N_ROW, N_COL, layers, TR, TC).transpose(2, 0, 3, 1, 4).reshape(layers, height, full_width)
    winter_pad = pad_plane(winter, 1)
    winter_feat = conv_valid(winter_pad[None], feat_weight)[0].astype(jnp.bfloat16)
    summer_pad = pad_plane(summer, rim_width)
    summer_tiles = jnp.stack([summer_pad[:, tile_row * TR:tile_row * TR + TR + 2 * rim_width, tile_col * TC:tile_col * TC + TC + 2 * rim_width] for tile_row in range(N_ROW) for tile_col in range(N_COL)])
    row_pos = jnp.arange(N_ROW, dtype=jnp.int32)[:, None] * TR - RADIUS + jnp.arange(TR + 2 * RADIUS, dtype=jnp.int32)[None, :]
    col_pos = jnp.arange(N_COL, dtype=jnp.int32)[:, None] * TC - RADIUS + jnp.arange(TC + 2 * RADIUS, dtype=jnp.int32)[None, :]
    row_inside = (row_pos >= 0) & (row_pos < height)
    col_inside = (col_pos >= 0) & (col_pos < full_width)
    inside = (row_inside[:, None, :, None] & col_inside[None, :, None, :]).reshape(tile_count, 1, TR + 2 * RADIUS, TC + 2 * RADIUS)
    summer_feat = jnp.where(inside, conv_valid(summer_tiles, feat_weight), 0.0).astype(jnp.bfloat16)
    grid_row = jnp.arange(N_ROW, dtype=jnp.int32)[:, None] + jnp.zeros((1, N_COL), jnp.int32)
    grid_col = jnp.arange(N_COL, dtype=jnp.int32)[None, :] + jnp.zeros((N_ROW, 1), jnp.int32)
    source = ((grid_row + offsets[0]) * N_COL + grid_col + offsets[1]).reshape(tile_count).astype(jnp.int32)
    matched = jnp.take(summer_feat, source, axis=0)
    winter_tiles = tile_view(winter_feat)
    cost_volume = jax.vmap(correlate)(winter_tiles, matched)
    channel_sum = lax.optimization_barrier(jnp.sum(cost_volume, axis=(0, 2, 3)))
    channel_sq = lax.optimization_barrier(jnp.sum(cost_volume * cost_volume, axis=(0, 2, 3)))
    channel_mean = channel_sum / pixel_count
    channel_var = channel_sq / pixel_count - channel_mean * channel_mean
    inv_std = lax.rsqrt(channel_var + 1e-05)
    centred = (cost_volume - channel_mean[None, :, None, None]) * inv_std[None, :, None, None]
    pre_norm = bn_gain[None, :, None, None] * centred + bn_shift[None, :, None, None]
    normed = jax.nn.silu(pre_norm).astype(jnp.bfloat16)
    normed_pad = pad_plane(plane_view(normed), 1)
    hidden_pre = conv_valid(normed_pad[None], w_first)[0]
    hidden = jax.nn.silu(hidden_pre).astype(jnp.bfloat16)
    hidden_pad = pad_plane(hidden, 1)
    refined = conv_valid(hidden_pad[None], w_second)[0].astype(jnp.bfloat16)
    grad_second = weight_term(cotangent[None], hidden_pad[None])
    grad_hidden = (conv_valid(pad_plane(cotangent, 1)[None], flip_weight(w_second, hidden.shape[0]))[0] * silu_slope(hidden_pre)).astype(jnp.bfloat16)
    grad_first = weight_term(grad_hidden[None], normed_pad[None])
    grad_normed = conv_valid(pad_plane(grad_hidden, 1)[None], flip_weight(w_first, normed.shape[1]))[0]
    grad_pre = tile_view(grad_normed) * silu_slope(pre_norm)
    grad_shift = lax.optimization_barrier(jnp.sum(grad_pre, axis=(0, 2, 3)))
    grad_gain = lax.optimization_barrier(jnp.sum(grad_pre * centred, axis=(0, 2, 3)))
    grad_volume = (bn_gain[None, :, None, None] * inv_std[None, :, None, None] * (grad_pre - grad_shift[None, :, None, None] / pixel_count - centred * grad_gain[None, :, None, None] / pixel_count)).astype(jnp.bfloat16)
    grad_wtiles, grad_blocks = jax.vmap(correlate_back)(grad_volume, winter_tiles, matched)
    grad_wfeat = plane_view(grad_wtiles.astype(jnp.bfloat16))
    grad_winter = conv_valid(pad_plane(grad_wfeat, 1)[None], flip_weight(feat_weight, channels))[0].astype(jnp.bfloat16)
    grad_feat = weight_term(grad_wfeat[None], winter_pad[None])
    rounded_blocks = lax.optimization_barrier(grad_blocks.astype(jnp.bfloat16)).astype(jnp.float32)
    returned = jax.ops.segment_sum(rounded_blocks, source, num_segments=tile_count)
    grad_sfeat = jnp.where(inside, returned, 0.0).astype(jnp.bfloat16)
    grad_feat = grad_feat + weight_term(grad_sfeat, summer_tiles)
    grad_sext = conv_valid(jnp.pad(grad_sfeat, ((0, 0), (0, 0), (2, 2), (2, 2))), flip_weight(feat_weight, channels))

    def add_tile(tile_index, accumulated):
        tile_row = (tile_index // N_COL).astype(jnp.int32)
        tile_col = (tile_index % N_COL).astype(jnp.int32)
        corner = (jnp.zeros((), jnp.int32), tile_row * TR, tile_col * TC)
        updated = lax.dynamic_slice(accumulated, corner, grad_sext.shape[1:]) + grad_sext[tile_index]
        return lax.dynamic_update_slice(accumulated, updated, corner)
    accumulated = lax.fori_loop(jnp.int32(0), jnp.int32(tile_count), add_tile, jnp.zeros((channels, height + 2 * rim_width, full_width + 2 * rim_width), jnp.float32))
    grad_summer = accumulated[:, rim_width:rim_width + height, rim_width:rim_width + full_width].astype(jnp.bfloat16)
    return (refined, grad_winter, grad_summer, grad_feat, grad_first, grad_second, grad_gain, grad_shift)
```

```python
import functools

import jax
import jax.numpy as jnp
from jax import lax
from jax.experimental import pallas as pl
from jax.experimental.pallas import tpu as pltpu
from jax.sharding import PartitionSpec as P

MESH = pl.DeviceIdType.MESH
C = 256
TR = 16
TC = 128
CH = 144
NROW = 16
NCOL = 8
PIXELS = 262144.0
F32 = jnp.float32
BF16 = jnp.bfloat16
VMEM_LIMIT = 58 * 1024 * 1024
AROUND = [(a, b) for a in (-1, 0, 1) for b in (-1, 0, 1) if (a, b) != (0, 0)]
NT = (((1,), (1,)), ((), ()))


def vspec():
    return pl.BlockSpec(memory_space=pltpu.VMEM)


def anyspec():
    return pl.BlockSpec(memory_space=pl.ANY)


def sspec():
    return pl.BlockSpec(memory_space=pltpu.SMEM)


def sds(shape, dtype):
    return jax.ShapeDtypeStruct(shape, dtype)


def call(kernel, outs, ins, scratch=(), in_specs=None, out_specs=None, **params):
    results = pl.pallas_call(
        kernel,
        out_shape=outs,
        in_specs=in_specs or [vspec() for _ in ins],
        out_specs=out_specs or [vspec() for _ in outs],
        scratch_shapes=list(scratch),
        compiler_params=pltpu.CompilerParams(vmem_limit_bytes=VMEM_LIMIT, **params),
    )(*ins)
    return list(results)


def rl(value, shift, axis):
    shift %= value.shape[axis]
    return value if shift == 0 else pltpu.roll(value, shift, axis)


def lane_of(shape):
    return lax.broadcasted_iota(jnp.int32, shape, 1)


def dot(a, b):
    return jnp.dot(a, b, preferred_element_type=F32)


def dot_nt(a, b):
    return lax.dot_general(a, b, NT, preferred_element_type=F32)


def pack_cols(row, cols, count=TR):
    total = None
    for y in range(count):
        value = row(y)
        lane = lane_of(value.shape)
        if total is None:
            total = jnp.zeros(value.shape, F32)
        for col, base in cols:
            total = jnp.where(lane == base + y, rl(value, base + y - col, 1), total)
    return total


ONE = [(0, 0), (127, 64)]
TWO = [(0, 0), (1, 16), (126, 64), (127, 80)]


def device_at(drow, dcol):
    row = lax.rem(lax.axis_index("row") + drow + NROW, NROW)
    col = lax.rem(lax.axis_index("col") + dcol + NCOL, NCOL)
    return (row, col)


def greet(steps):
    both = sorted(set(steps) | {(-a, -b) for a, b in steps})
    barrier = pltpu.get_barrier_semaphore()
    for step in both:
        pl.semaphore_signal(barrier, inc=1, device_id=device_at(*step), device_id_type=MESH)
    pl.semaphore_wait(barrier, len(both))


def exchange_kernel(moves, n_in, *refs):
    ins = refs[:n_in]
    outs = refs[n_in : n_in + len(moves)]
    send, recv = refs[n_in + len(moves) :]
    greet([m[3] for m in moves])
    copies = []
    for k, (which, start, size, step) in enumerate(moves):
        copies.append(
            pltpu.make_async_remote_copy(
                src_ref=ins[which].at[pl.ds(start, size)],
                dst_ref=outs[k],
                send_sem=send.at[k],
                recv_sem=recv.at[k],
                device_id=device_at(*step),
                device_id_type=MESH,
            )
        )
    for copy in copies:
        copy.start()
    for copy in copies:
        copy.wait()


def exchange(arrays, moves, collective_id):
    outs = [sds((size,) + arrays[which].shape[1:], arrays[which].dtype) for which, _, size, _ in moves]
    return call(
        functools.partial(exchange_kernel, moves, len(arrays)),
        outs,
        arrays,
        [pltpu.SemaphoreType.DMA((len(moves),)), pltpu.SemaphoreType.DMA((len(moves),))],
        in_specs=[anyspec() for _ in arrays],
        out_specs=[anyspec() for _ in moves],
        collective_id=collective_id,
        has_side_effects=True,
    )


def load_rows(x_ref, wide):
    wide[...] = x_ref[...].astype(F32)


def strided(wide, y, channels):
    return wide[pl.ds(y, channels, stride=TR), :]


def edges_kernel(w_ref, s_ref, c_ref, rows_out, pack_out, crows_out, cpack_out, wide, cwide):
    for k, ref in enumerate((w_ref, s_ref)):
        wide[...] = ref[...].astype(F32)
        rows_out[k] = strided(wide, 0, C).astype(BF16)
        rows_out[2 + k] = strided(wide, TR - 1, C).astype(BF16)
        pack_out[k] = pack_cols(lambda y: strided(wide, y, C), ONE).astype(BF16)
    cwide[...] = c_ref[...].astype(F32)
    for k, y in enumerate((0, 1, 14, 15)):
        crows_out[k] = strided(cwide, y, 32).astype(BF16)
    cpack_out[0] = pack_cols(lambda y: strided(cwide, y, 32), TWO).astype(BF16)


def edges2_kernel(w_ref, s_ref, rows_out, pack_out):
    for k, ref in enumerate((w_ref, s_ref)):
        rows_out[k] = ref[:, 0:TC]
        rows_out[2 + k] = ref[:, (TR - 1) * TC : TR * TC]
        pack_out[k] = pack_cols(
            lambda y: ref[:, y * TC : (y + 1) * TC].astype(F32), ONE
        ).astype(BF16)


def halo_moves(base):
    return [(0, 2, 2, (1, 0)), (0, 0, 2, (-1, 0))] + [(1, 0, 2, step) for step in AROUND if step[1] != 0]


SIDE_STEPS = [step for step in AROUND if step[1] != 0]


def halo_cols(packs, k):
    first_row = lax.axis_index("row") == 0
    last_row = lax.axis_index("row") == NROW - 1
    first_col = lax.axis_index("col") == 0
    last_col = lax.axis_index("col") == NCOL - 1
    get = lambda a, b: packs[(a, b)][k].astype(F32)
    total = jnp.zeros((C, TC), F32)
    lane = lane_of((C, TC))
    for side, source_base, dest, gone in ((-1, 64, 0, first_col), (1, 0, 64, last_col)):
        keep = jnp.logical_not(gone)
        up = keep & jnp.logical_not(first_row)
        down = keep & jnp.logical_not(last_row)
        mid = (lane >= dest + 1) & (lane < dest + 17) & keep
        total = jnp.where(mid, rl(get(0, side), dest + 1 - source_base, 1), total)
        total = jnp.where((lane == dest) & up, rl(get(-1, side), dest - source_base - 15, 1), total)
        total = jnp.where((lane == dest + 17) & down, rl(get(1, side), dest + 17 - source_base, 1), total)
    return total


def build_x3(x3, row, halo, count, channels, first_lane=0):
    for k in range(count):
        value = row(k)
        lane = lane_of(value.shape)
        at = slice(k * TC, (k + 1) * TC)
        left = jnp.where(lane == 0, rl(halo, -(first_lane + k), 1), rl(value, 1, 1))
        right = jnp.where(lane == TC - 1, rl(halo, TC - 1 - (64 + first_lane + k), 1), rl(value, -1, 1))
        x3[0:channels, at] = left.astype(BF16)
        x3[channels : 2 * channels, at] = value.astype(BF16)
        x3[2 * channels : 3 * channels, at] = right.astype(BF16)


def end_row(ref, gone):
    return jnp.where(gone, 0.0, ref.astype(F32))


def conv_chunk(w_ref, x3, start, width):
    total = None
    depth = x3.shape[0]
    for a in range(3):
        term = dot(w_ref[:, a * depth : (a + 1) * depth], x3[:, start + a * TC : start + a * TC + width])
        total = term if total is None else total + term
    return total


PACK_PLACES = [(-a, -b) for a, b in SIDE_STEPS]


def feat_kernel(k, summer, x_ref, top, bottom, p0, p1, p2, p3, p4, p5, w_ref, *rest):
    if summer:
        f_out, x3_out, wide = rest
    else:
        f_out, x3_out, wide = rest
    packs = dict(zip(PACK_PLACES, (p0, p1, p2, p3, p4, p5)))
    wide[...] = x_ref[...].astype(F32)
    first_row = lax.axis_index("row") == 0
    last_row = lax.axis_index("row") == NROW - 1

    def row(j):
        if j == 0:
            return end_row(top[k], first_row)
        if j == TR + 1:
            return end_row(bottom[k], last_row)
        return strided(wide, j - 1, C)

    build_x3(x3_out, row, halo_cols(packs, k), TR + 2, C)
    for n in range(4):
        value = conv_chunk(w_ref, x3_out, n * 512, 512)
        if summer:
            for j in range(4):
                wide[(n * 4 + j) * C : (n * 4 + j + 1) * C, :] = value[:, j * TC : (j + 1) * TC]
                f_out[n * 4 + j] = value[:, j * TC : (j + 1) * TC].astype(BF16)
        else:
            f_out[:, n * 512 : (n + 1) * 512] = value.astype(BF16)
    if summer:
        lane = lane_of((C, TC))
        total = jnp.zeros((C, TC), F32)
        for y in range(TR):
            value = wide[y * C : (y + 1) * C, :]
            low = (lane >= y * 8) & (lane < y * 8 + 4)
            high = (lane >= y * 8 + 4) & (lane < y * 8 + 8)
            total = jnp.where(low, rl(value, y * 8, 1), total)
            total = jnp.where(high, rl(value, y * 8 + 4 - 124, 1), total)
        f_out[TR] = total.astype(BF16)


def offset_of(off, part, row, col):
    return off[part * NROW * NCOL + row * NCOL + col]


def match_kernel(off, fp, out, strip, pstrip, send_buf, trio, ptrio, psend, lsem, sems, rsems):
    row = lax.axis_index("row")
    col = lax.axis_index("col")
    steps = [(1, 0), (-1, 0), (2, 0), (-2, 0), (0, 1), (0, -1), (0, 2), (0, -2)]
    own = [
        pltpu.make_async_copy(fp.at[pl.ds(0, TR)], strip.at[pl.ds(20, TR)], lsem.at[0]),
        pltpu.make_async_copy(fp.at[pl.ds(TR, 1)], pstrip.at[pl.ds(2, 1)], lsem.at[1]),
    ]
    for copy in own:
        copy.start()
    greet(steps)

    def remote(k, src, dst, step):
        return pltpu.make_async_remote_copy(
            src_ref=src,
            dst_ref=dst,
            send_sem=sems.at[k],
            recv_sem=rsems.at[k],
            device_id=device_at(*step),
            device_id_type=MESH,
        )

    stage = [
        remote(0, fp.at[pl.ds(0, TR)], strip.at[pl.ds(4, TR)], (1, 0)),
        remote(1, fp.at[pl.ds(0, TR)], strip.at[pl.ds(36, TR)], (-1, 0)),
        remote(2, fp.at[pl.ds(12, 4)], strip.at[pl.ds(0, 4)], (2, 0)),
        remote(3, fp.at[pl.ds(0, 4)], strip.at[pl.ds(52, 4)], (-2, 0)),
        remote(4, fp.at[pl.ds(TR, 1)], pstrip.at[pl.ds(1, 1)], (1, 0)),
        remote(5, fp.at[pl.ds(TR, 1)], pstrip.at[pl.ds(3, 1)], (-1, 0)),
        remote(6, fp.at[pl.ds(TR, 1)], pstrip.at[pl.ds(0, 1)], (2, 0)),
        remote(7, fp.at[pl.ds(TR, 1)], pstrip.at[pl.ds(4, 1)], (-2, 0)),
    ]
    for copy in stage:
        copy.start()
    for copy in own:
        copy.wait()
    for copy in stage:
        copy.wait()

    def pick_of(dcol):
        return offset_of(off, 0, row, lax.rem(col + dcol + NCOL, NCOL)) + 1

    second = []
    for k, dcol in enumerate((-1, 1)):
        pick = pick_of(dcol)

        def fill(j, carry, k=k, pick=pick):
            send_buf[k, j] = strip[16 * pick + j]
            return carry

        lax.fori_loop(0, 24, fill, 0)
        copy = remote(8 + k, send_buf.at[k], trio.at[1 - dcol], (0, dcol))
        copy.start()
        second.append(copy)
    for k, dcol in enumerate((-2, -1, 1, 2)):
        pick = pick_of(dcol)
        for j in range(3):
            psend[k, j] = pstrip[pick + j]
        copy = remote(10 + k, psend.at[k], ptrio.at[2 - dcol], (0, dcol))
        copy.start()
        second.append(copy)
    pick = pick_of(0)

    def fill(j, carry):
        trio[1, j] = strip[16 * pick + j]
        return carry

    lax.fori_loop(0, 24, fill, 0)
    for j in range(3):
        ptrio[2, j] = pstrip[pick + j]
    for copy in second:
        copy.wait()
    my_row = row + offset_of(off, 0, row, col)
    my_col = col + offset_of(off, 1, row, col)
    dcol = my_col - col + 1
    zero = jnp.zeros((C, TC), BF16)
    for j in range(24):
        value = trio[dcol, j]
        if j < 4:
            value = jnp.where(my_row == 0, zero, value)
        if j >= 20:
            value = jnp.where(my_row == NROW - 1, zero, value)
        out[:, j * TC : (j + 1) * TC] = value
    low = lax.rem(lane_of((C, TC)), 8) < 4
    for j in range(3):
        right = jnp.where(my_col == NCOL - 1, zero, ptrio[dcol + 2, j]).astype(F32)
        left = jnp.where(my_col == 0, zero, ptrio[dcol, j]).astype(F32)
        value = jnp.where(low, right, left)
        if j == 0:
            value = jnp.where(my_row == 0, 0.0, value)
        if j == 2:
            value = jnp.where(my_row == NROW - 1, 0.0, value)
        out[:, (24 + j) * TC : (25 + j) * TC] = value.astype(BF16)


def match(offsets, fp):
    return call(
        match_kernel,
        [sds((C, 27 * TC), BF16)],
        [offsets, fp],
        [
            pltpu.VMEM((56, C, TC), BF16),
            pltpu.VMEM((5, C, TC), BF16),
            pltpu.VMEM((2, 24, C, TC), BF16),
            pltpu.VMEM((3, 24, C, TC), BF16),
            pltpu.VMEM((5, 3, C, TC), BF16),
            pltpu.VMEM((4, 3, C, TC), BF16),
            pltpu.SemaphoreType.DMA((2,)),
            pltpu.SemaphoreType.DMA((14,)),
            pltpu.SemaphoreType.DMA((14,)),
        ],
        in_specs=[sspec(), vspec()],
        collective_id=1,
        has_side_effects=True,
    )[0]


def bit_off(lane, bit):
    return (lane & bit) == 0


def shear(main, rim):
    low = lane_of((80, TC)) < 64
    w = jnp.where(low, jnp.concatenate([rim, main[0:72]], 0), jnp.concatenate([main[56:128], rim], 0))
    w = jnp.where(bit_off(lane_of((48, TC)), 32), w[0:48], w[32:80])
    w = jnp.where(bit_off(lane_of((32, TC)), 16), w[0:32], w[16:48])
    w = jnp.where(bit_off(lane_of((24, TC)), 8), w[0:24], w[8:32])
    lane = lane_of((16, TC))
    w = jnp.where(bit_off(lane, 4), rl(w, -4, 0)[0:16], w[8:24])
    w = jnp.where(bit_off(lane, 2), w, rl(w, -2, 0))
    w = jnp.where(bit_off(lane, 1), w, rl(w, -1, 0))
    return jnp.where(lax.broadcasted_iota(jnp.int32, (16, TC), 0) < 9, w, 0.0)


def unshear(value):
    lane = lane_of((16, TC))
    w = jnp.where(bit_off(lane, 1), value, rl(value, 1, 0))
    w = jnp.where(bit_off(lane, 2), w, rl(w, 2, 0))
    zeros = lambda n: jnp.zeros((n, TC), F32)
    padded = jnp.concatenate([w, zeros(8)], 0)
    w = jnp.where(bit_off(lane_of((24, TC)), 4), rl(padded, 4, 0), jnp.concatenate([zeros(8), w], 0))
    for n, bit in ((24, 8), (32, 16), (48, 32)):
        w = jnp.where(
            bit_off(lane_of((n + bit, TC)), bit),
            jnp.concatenate([w, zeros(bit)], 0),
            jnp.concatenate([zeros(bit), w], 0),
        )
    low = lambda n: lane_of((n, TC)) < 64
    main = jnp.concatenate(
        [
            jnp.where(low(56), w[8:64], 0.0),
            jnp.where(low(16), w[64:80], w[0:16]),
            jnp.where(low(56), 0.0, w[16:72]),
        ],
        0,
    )
    return main, jnp.where(low(8), w[0:8], w[72:80])


def row_sums(first, second):
    ones = jnp.ones((8, TC), F32)
    a = lax.dot_general(ones, first, NT, precision=lax.Precision.HIGHEST, preferred_element_type=F32)
    b = lax.dot_general(ones, second, NT, precision=lax.Precision.HIGHEST, preferred_element_type=F32)
    return jnp.where(lax.broadcasted_iota(jnp.int32, a.shape, 0) == 0, a, b)


def correlate_kernel(fw, m, cv, pack, sums, mt, rt, grim, s1, s2):
    for r in range(24):
        mt[r * TC : (r + 1) * TC, :] = m[:, r * TC : (r + 1) * TC].T
    for q in range(3):
        rt[q * TC : (q + 1) * TC, :] = m[:, (24 + q) * TC : (25 + q) * TC].T
    for n in range(4):
        grim[:, n * 512 : (n + 1) * 512] = dot(rt[...], fw[:, n * 512 : (n + 1) * 512])
    s1[...] = jnp.zeros_like(s1)
    s2[...] = jnp.zeros_like(s2)

    def at_row(y, carry):
        lanes = pl.ds(pl.multiple_of(y * TC, TC), TC)
        feat = fw[:, lanes]
        for a in range(9):
            main = dot(mt[pl.ds(pl.multiple_of((y + a) * TC, TC), TC), :], feat)
            rim = grim[pl.ds(pl.multiple_of((y + a + 12) * 8, 8), 8), lanes]
            value = shear(main, rim) * 0.0625
            rows = slice(a * 16, (a + 1) * 16)
            cv[y, rows, :] = value
            s1[rows, :] += value
            s2[rows, :] += value * value
        return carry

    lax.fori_loop(0, TR, at_row, 0)
    pack[0] = pack_cols(lambda y: cv[y], TWO)
    sums[...] = jnp.zeros_like(sums)
    sums[:, 0:CH] = row_sums(s1[...], s2[...])


def reduce_phases(value_ref, gather_col, gather_row, out, csend, crecv, rsend, rrecv, base=0):
    for count, axis, src, dst, send, recv in (
        (NCOL, "col", value_ref, gather_col, csend, crecv),
        (NROW, "row", out, gather_row, rsend, rrecv),
    ):
        copies = []
        for d in range(1, count):
            step = (0, d) if axis == "col" else (d, 0)
            copies.append(
                pltpu.make_async_remote_copy(
                    src_ref=src,
                    dst_ref=dst.at[d],
                    send_sem=send.at[d],
                    recv_sem=recv.at[d],
                    device_id=device_at(*step),
                    device_id_type=MESH,
                )
            )
        for copy in copies:
            copy.start()
        for copy in copies:
            copy.wait()
        dst[0] = src[...]
        me = lax.axis_index(axis)
        total = None
        for d in range(count):
            value = dst[lax.rem(me - d + count, count)]
            total = value if total is None else total + value
        out[...] = total


RING = [(0, d) for d in range(1, NCOL)] + [(d, 0) for d in range(1, NROW)]


def stats_kernel(moves, n_in, *refs):
    value = refs[0]
    ins = refs[1 : 1 + n_in]
    out = refs[1 + n_in]
    outs = refs[2 + n_in : 2 + n_in + len(moves)]
    gcol, grow, csend, crecv, rsend, rrecv, send, recv = refs[2 + n_in + len(moves) :]
    greet(RING + [m[3] for m in moves])
    copies = [
        pltpu.make_async_remote_copy(
            src_ref=ins[which].at[pl.ds(start, size)],
            dst_ref=outs[k],
            send_sem=send.at[k],
            recv_sem=recv.at[k],
            device_id=device_at(*step),
            device_id_type=MESH,
        )
        for k, (which, start, size, step) in enumerate(moves)
    ]
    for copy in copies:
        copy.start()
    reduce_phases(value, gcol, grow, out, csend, crecv, rsend, rrecv)
    for copy in copies:
        copy.wait()


def stats(value, arrays, moves, collective_id):
    outs = [sds(value.shape, F32)] + [
        sds((size,) + arrays[which].shape[1:], arrays[which].dtype) for which, _, size, _ in moves
    ]
    dma = pltpu.SemaphoreType.DMA
    return call(
        functools.partial(stats_kernel, moves, len(arrays)),
        outs,
        [value] + arrays,
        [
            pltpu.VMEM((NCOL,) + value.shape, F32),
            pltpu.VMEM((NROW,) + value.shape, F32),
            dma((NCOL,)),
            dma((NCOL,)),
            dma((NROW,)),
            dma((NROW,)),
            dma((max(1, len(moves)),)),
            dma((max(1, len(moves)),)),
        ],
        in_specs=[vspec()] + [anyspec() for _ in arrays],
        out_specs=[vspec()] + [anyspec() for _ in moves],
        collective_id=collective_id,
        has_side_effects=True,
    )


def two_tiles(packs):
    tiles = []
    for b in (-1, 0, 1):
        total = None
        for dest, col in ((0, b - 1), (64, 128 + b)):
            place = -1 if col < 0 else (1 if col > 127 else 0)
            local = col - place * TC
            base = dict(TWO)[local]
            for drow, first, last in ((-1, 0, 2), (0, 2, 18), (1, 18, 20)):
                value = rl(packs[(drow, place)], dest + 2 + 16 * drow - base, 1)
                lane = lane_of(value.shape)
                if total is None:
                    total = jnp.zeros(value.shape, F32)
                total = jnp.where((lane >= dest + first) & (lane < dest + last), value, total)
        tiles.append(total)
    return tiles


def tile_inside(b, shape):
    lane = lane_of(shape)
    row = lax.axis_index("row")
    col = lax.axis_index("col")
    local = jnp.where(lane < 64, lane, lane - 64)
    y = row * TR - 2 + local
    x = jnp.where(lane < 64, col * TC - 1 + b, col * TC + TC + b)
    return (y >= 0) & (y < NROW * TR) & (x >= 0) & (x < NCOL * TC) & (local < 20)


def rim_patches(tiles, a):
    return jnp.concatenate([rl(t, -a, 1) for t in tiles], 0).astype(BF16)


def silu_parts(value):
    sigma = jax.nn.sigmoid(value)
    return value * sigma, sigma * (1.0 + value * (1.0 - sigma))


def refine_kernel(
    cv, cvtop, cvbot, n0, n1, n2, n3, n4, n5, n6, n7, pack,
    cot, ctop, cbot, m0, m1, m2, m3, m4, m5, m6, m7, cpack,
    coef, w1, w1f, w2, w2f,
    refined, gpre, gfirst, gsecond, sums,
    cwide, n3x, c3x, h3, gh3, hpre, gmain, s1, s2, rwide,
):
    places = [(-a, -b) for a, b in AROUND]
    row = lax.axis_index("row")
    first = row == 0
    last = row == NROW - 1
    scale, bias, inv, mid = (coef[k] for k in range(4))
    packs = {place: ref[0] for place, ref in zip(places, (n0, n1, n2, n3, n4, n5, n6, n7))}
    packs[(0, 0)] = pack[0]
    cpacks = {place: ref[0].astype(F32) for place, ref in zip(places, (m0, m1, m2, m3, m4, m5, m6, m7))}
    cpacks[(0, 0)] = cpack[0].astype(F32)

    def outer(k):
        return first if k < 2 else last

    def normed_of(value):
        return silu_parts(value * scale + bias)[0]

    ntiles = [
        jnp.where(tile_inside(b - 1, (CH, TC)), normed_of(t), 0.0) for b, t in enumerate(two_tiles(packs))
    ]

    def nrow(k):
        if k < 2:
            return jnp.where(first, 0.0, normed_of(cvtop[k]))
        if k >= 18:
            return jnp.where(last, 0.0, normed_of(cvbot[k - 18]))
        return normed_of(cv[k - 2])

    build_x3(n3x, nrow, ntiles[1], 20, CH)
    ctiles = [
        jnp.where(tile_inside(b - 1, (32, TC)), t, 0.0) for b, t in enumerate(two_tiles(cpacks))
    ]
    cwide[...] = cot[...].astype(F32)

    def crow(k):
        if k < 2:
            return jnp.where(first, 0.0, ctop[k].astype(F32))
        if k >= 18:
            return jnp.where(last, 0.0, cbot[k - 18].astype(F32))
        return strided(cwide, k - 2, 32)

    build_x3(c3x, crow, ctiles[1], 20, 32)

    def both(w_ref, x3, tiles):
        depth = x3.shape[0]
        rim = None
        for a in range(3):
            term = dot(w_ref[:, a * depth : (a + 1) * depth], rim_patches(tiles, a))
            rim = term if rim is None else rim + term
        return rim

    lane = lane_of((64, TC))
    local = jnp.where(lane < 64, lane, lane - 64)
    ypos = row * TR - 1 + local
    col = lax.axis_index("col")
    xpos = jnp.where(lane < 64, col * TC - 1, col * TC + TC)
    rim_in = (ypos >= 0) & (ypos < NROW * TR) & (local < 18) & (xpos >= 0) & (xpos < NCOL * TC)
    rim_h, rim_slope = silu_parts(both(w1, n3x, ntiles))
    rim_g = both(w2f, c3x, ctiles)
    rim_h = jnp.where(rim_in, rim_h, 0.0)
    rim_g = jnp.where(rim_in, rim_g * rim_slope, 0.0)
    for n in range(6):
        hpre[:, n * 384 : (n + 1) * 384] = conv_chunk(w1, n3x, n * 384, 384)
        gmain[:, n * 384 : (n + 1) * 384] = conv_chunk(w2f, c3x, n * 384, 384)

    def edge(k):
        return first if k == 0 else (last if k == 17 else None)

    def hrow(k):
        value, slope = silu_parts(hpre[:, k * TC : (k + 1) * TC])
        grad = gmain[:, k * TC : (k + 1) * TC] * slope
        gone = edge(k)
        if gone is not None:
            value = jnp.where(gone, 0.0, value)
            grad = jnp.where(gone, 0.0, grad)
        gmain[:, k * TC : (k + 1) * TC] = grad
        return value

    build_x3(h3, hrow, rim_h, 18, 64)
    build_x3(gh3, lambda k: gmain[:, k * TC : (k + 1) * TC], rim_g, 18, 64)
    for n in range(4):
        value = conv_chunk(w2, h3, n * 512, 512)
        for j in range(4):
            rwide[pl.ds(n * 4 + j, 32, stride=TR), :] = value[:, j * TC : (j + 1) * TC]
    refined[...] = rwide[...].astype(BF16)
    own = slice(TC, 17 * TC)
    mine = slice(2 * TC, 18 * TC)
    for a in range(3):
        gsecond[:, a * 192 : (a + 1) * 192] = dot_nt(c3x[32:64, mine], h3[:, a * TC : (a + 16) * TC])
        gfirst[:, a * 432 : (a + 1) * 432] = dot_nt(gh3[64:128, own], n3x[:, (a + 1) * TC : (a + 17) * TC])
    s1[...] = jnp.zeros_like(s1)
    s2[...] = jnp.zeros_like(s2)
    for n in range(4):
        value = conv_chunk(w1f, gh3, n * 512, 512)
        for j in range(4):
            y = n * 4 + j
            volume = cv[y]
            grad = value[:, j * TC : (j + 1) * TC] * silu_parts(volume * scale + bias)[1]
            gpre[y] = grad
            s1[...] += grad
            s2[...] += grad * (volume * inv - mid)
    sums[...] = jnp.zeros_like(sums)
    sums[:, 0:CH] = row_sums(s1[...], s2[...])


def correlate_back_kernel(cv, gpre, coef, fw, m, gfw, gm, q, qrim):
    def at_row(y, carry):
        lanes = pl.ds(pl.multiple_of(y * TC, TC), TC)
        grad = coef[0] * gpre[y] + coef[1] + coef[2] * cv[y]
        grad = grad.astype(BF16).astype(F32)
        for a in range(9):
            main, rim = unshear(grad[a * 16 : (a + 1) * 16])
            q[pl.ds(pl.multiple_of((y + a) * TC, TC), TC), lanes] = main.astype(BF16)
            qrim[pl.ds(pl.multiple_of((y + a + 12) * 8, 8), 8), lanes] = rim
        return carry

    qrim[...] = jnp.zeros_like(qrim)
    lax.fori_loop(0, TR, at_row, 0)
    for y in range(TR):
        at = slice(y * TC, (y + 1) * TC)
        value = dot(m[:, y * TC : (y + 9) * TC], q[y * TC : (y + 9) * TC, at])
        value = value + dot(m[:, 24 * TC : 27 * TC], qrim[:, at].astype(BF16))
        gfw[:, at] = (value * 0.0625).astype(BF16)
    for r in range(24):
        at = slice(max(0, r - 8) * TC, (min(15, r) + 1) * TC)
        value = dot_nt(fw[:, at], q[r * TC : (r + 1) * TC, at])
        gm[r] = (value * 0.0625).astype(BF16)
    for k in range(3):
        value = dot_nt(fw[...], qrim[k * TC : (k + 1) * TC, :].astype(BF16))
        gm[24 + k] = (value * 0.0625).astype(BF16)


def return_kernel(off, gm, out, trio, strip, pstrip, ab, be, ab2, be2, pab, pfar, mine, side, lsem, sems, rsems):
    row = lax.axis_index("row")
    col = lax.axis_index("col")
    steps = [(1, 0), (-1, 0), (2, 0), (-2, 0), (0, 1), (0, -1)]
    own = pltpu.make_async_copy(gm, trio.at[1, pl.ds(0, 27)], lsem.at[0])
    own.start()
    for k in range(3):
        trio[k, 27] = jnp.zeros((C, TC), BF16)
    greet(steps)

    def remote(k, src, dst, step):
        return pltpu.make_async_remote_copy(
            src_ref=src,
            dst_ref=dst,
            send_sem=sems.at[k],
            recv_sem=rsems.at[k],
            device_id=device_at(*step),
            device_id_type=MESH,
        )

    stage = [
        remote(0, gm, trio.at[0, pl.ds(0, 27)], (0, 1)),
        remote(1, gm, trio.at[2, pl.ds(0, 27)], (0, -1)),
    ]
    for copy in stage:
        copy.start()
    own.wait()
    for copy in stage:
        copy.wait()
    sources = []
    for k in range(3):
        place = col + k - 1
        there = lax.rem(place + NCOL, NCOL)
        drow = offset_of(off, 0, row, there)
        dcol = offset_of(off, 1, row, there)
        good = (dcol == 1 - k) & (place >= 0) & (place < NCOL)
        sources.append((drow, good))

    def gather(p, carry):
        total = jnp.zeros((C, TC), F32)
        for k, (drow, good) in enumerate(sources):
            j = p - 16 * (drow + 1)
            fits = good & (j >= 0) & (j < 24)
            total = total + trio[k, jnp.where(fits, j, 27)].astype(F32)
        strip[p] = total.astype(BF16)
        return carry

    lax.fori_loop(0, 56, gather, 0)
    for p in range(5):
        total = jnp.zeros((C, TC), F32)
        for k, (drow, good) in enumerate(sources):
            j = p - (drow + 1)
            fits = good & (j >= 0) & (j < 3)
            total = total + trio[k, jnp.where(fits, 24 + j, 27)].astype(F32)
        pstrip[p] = total.astype(BF16)
    stage = [
        remote(2, strip.at[pl.ds(4, TR)], be, (-1, 0)),
        remote(3, strip.at[pl.ds(36, TR)], ab, (1, 0)),
        remote(4, strip.at[pl.ds(0, 4)], be2, (-2, 0)),
        remote(5, strip.at[pl.ds(52, 4)], ab2, (2, 0)),
        remote(6, pstrip.at[pl.ds(1, 1)], pab.at[pl.ds(1, 1)], (-1, 0)),
        remote(7, pstrip.at[pl.ds(3, 1)], pab.at[pl.ds(0, 1)], (1, 0)),
        remote(8, pstrip.at[pl.ds(0, 1)], pfar.at[pl.ds(1, 1)], (-2, 0)),
        remote(9, pstrip.at[pl.ds(4, 1)], pfar.at[pl.ds(0, 1)], (2, 0)),
    ]
    for copy in stage:
        copy.start()
    for copy in stage:
        copy.wait()
    up1, up2 = row >= 1, row >= 2
    down1, down2 = row < NROW - 1, row < NROW - 2
    zero = jnp.zeros((C, TC), F32)

    def only(flag, ref):
        return jnp.where(flag, ref.astype(F32), zero)

    total = pstrip[2].astype(F32) + only(up1, pab[0]) + only(down1, pab[1])
    total = total + only(up2, pfar[0]) + only(down2, pfar[1])
    mine[...] = total.astype(BF16)
    stage = [
        remote(10, mine, side.at[0], (0, 1)),
        remote(11, mine, side.at[1], (0, -1)),
    ]
    for copy in stage:
        copy.start()
    for copy in stage:
        copy.wait()
    lane = lane_of((C, TC))
    left = only(col > 0, side[0])
    right = only(col < NCOL - 1, side[1])
    for y in range(TR):
        total = strip[20 + y].astype(F32) + only(up1, ab[y]) + only(down1, be[y])
        if y < 4:
            total = total + only(up2, ab2[y])
        if y >= 12:
            total = total + only(down2, be2[y - 12])
        total = total + jnp.where(lane < 4, rl(left, -y * 8, 1), 0.0)
        total = total + jnp.where(lane >= 124, rl(right, 124 - (y * 8 + 4), 1), 0.0)
        out[:, y * TC : (y + 1) * TC] = total.astype(BF16)


def give_back(offsets, gm):
    return call(
        return_kernel,
        [sds((C, TR * TC), BF16)],
        [offsets, gm],
        [
            pltpu.VMEM((3, 28, C, TC), BF16),
            pltpu.VMEM((56, C, TC), BF16),
            pltpu.VMEM((5, C, TC), BF16),
            pltpu.VMEM((TR, C, TC), BF16),
            pltpu.VMEM((TR, C, TC), BF16),
            pltpu.VMEM((4, C, TC), BF16),
            pltpu.VMEM((4, C, TC), BF16),
            pltpu.VMEM((2, C, TC), BF16),
            pltpu.VMEM((2, C, TC), BF16),
            pltpu.VMEM((C, TC), BF16),
            pltpu.VMEM((2, C, TC), BF16),
            pltpu.SemaphoreType.DMA((1,)),
            pltpu.SemaphoreType.DMA((12,)),
            pltpu.SemaphoreType.DMA((12,)),
        ],
        in_specs=[sspec(), vspec()],
        collective_id=4,
        has_side_effects=True,
    )[0]


def last_kernel(k, g, top, bottom, p0, p1, p2, p3, p4, p5, w_ref, out, x3, wide):
    packs = dict(zip(PACK_PLACES, (p0, p1, p2, p3, p4, p5)))
    first_row = lax.axis_index("row") == 0
    last_row = lax.axis_index("row") == NROW - 1

    def row(j):
        if j == 0:
            return end_row(top[k], first_row)
        if j == TR + 1:
            return end_row(bottom[k], last_row)
        return g[:, (j - 1) * TC : j * TC].astype(F32)

    build_x3(x3, row, halo_cols(packs, k), TR + 2, C)
    for n in range(4):
        value = conv_chunk(w_ref, x3, n * 512, 512)
        for j in range(4):
            wide[pl.ds(n * 4 + j, C, stride=TR), :] = value[:, j * TC : (j + 1) * TC]
    out[...] = wide[...].astype(BF16)


def weight_kernel(gw, gs, xw, xs, out):
    for a in range(3):
        at = slice(a * TC, (a + 16) * TC)
        for n in range(3):
            part = slice(n * C, (n + 1) * C)
            value = dot_nt(gw[...], xw[part, at]) + dot_nt(gs[...], xs[part, at])
            out[:, a * 768 + n * C : a * 768 + (n + 1) * C] = value


def flip_weight(weight, in_channels):
    out_channels = weight.shape[0]
    return (
        weight.reshape(out_channels, 9, in_channels)[:, ::-1, :]
        .transpose(2, 1, 0)
        .reshape(in_channels, 9 * out_channels)
    )


def spread(vector):
    return jnp.pad(vector.reshape(9, 9), ((0, 0), (0, 7))).reshape(CH)


def gathered(vector):
    return vector.reshape(9, 16)[:, :9].reshape(81)


def across(*vectors):
    return jnp.stack([jnp.broadcast_to(v[:, None], (CH, TC)) for v in vectors])


def body(winter, summer, offsets, feat_weight, bn_gain, bn_shift, w_first, w_second, cotangent):
    w2 = winter.reshape(C * TR, TC)
    s2 = summer.reshape(C * TR, TC)
    c2 = cotangent.reshape(32 * TR, TC)
    flat = offsets.reshape(-1)
    rows, pack, crows, cpack = call(
        edges_kernel,
        [sds((4, C, TC), BF16), sds((2, C, TC), BF16), sds((4, 32, TC), BF16), sds((1, 32, TC), BF16)],
        [w2, s2, c2],
        [pltpu.VMEM((C * TR, TC), F32), pltpu.VMEM((32 * TR, TC), F32)],
    )
    moves = halo_moves(0)
    got = exchange(
        [rows, pack, crows, cpack],
        moves + [(2, 2, 2, (1, 0)), (2, 0, 2, (-1, 0))] + [(3, 0, 1, step) for step in AROUND],
        0,
    )
    halo = got[:8]
    chalo = got[8:]

    def feat(k, x):
        summer_side = k == 1
        out = sds((TR + 1, C, TC), BF16) if summer_side else sds((C, TR * TC), BF16)
        return call(
            functools.partial(feat_kernel, k, summer_side),
            [out, sds((3 * C, 18 * TC), BF16)],
            [x] + halo + [feat_weight],
            [pltpu.VMEM((C * TR, TC), F32)],
        )

    fs, xs = feat(1, s2)
    fw, xw = feat(0, w2)
    m = match(flat, fs)
    cv, cvpack, sums = call(
        correlate_kernel,
        [sds((TR, CH, TC), F32), sds((1, CH, TC), F32), sds((8, 256), F32)],
        [fw, m],
        [
            pltpu.VMEM((24 * TC, C), BF16),
            pltpu.VMEM((3 * TC, C), BF16),
            pltpu.VMEM((3 * TC, TR * TC), F32),
            pltpu.VMEM((CH, TC), F32),
            pltpu.VMEM((CH, TC), F32),
        ],
    )
    got = stats(
        sums,
        [cv, cvpack],
        [(0, 14, 2, (1, 0)), (0, 0, 2, (-1, 0))] + [(1, 0, 1, step) for step in AROUND],
        2,
    )
    sums, vhalo = got[0], got[1:]
    mean = sums[0, :CH] / PIXELS
    inv = lax.rsqrt(sums[1, :CH] / PIXELS - mean * mean + 1e-05)
    gain = spread(bn_gain)
    scale = gain * inv
    coef = across(scale, spread(bn_shift) - mean * scale, inv, mean * inv)
    w1 = jnp.pad(w_first.reshape(64, 9, 9, 9), ((0, 0), (0, 0), (0, 0), (0, 7))).reshape(64, 9 * CH)
    dma = pltpu.SemaphoreType.DMA
    refined, gpre, gfirst, gsecond, gsums = call(
        refine_kernel,
        [
            sds((32 * TR, TC), BF16),
            sds((TR, CH, TC), F32),
            sds((64, 9 * CH), F32),
            sds((32, 576), F32),
            sds((8, 256), F32),
        ],
        [cv] + vhalo + [cvpack] + [c2] + chalo + [cpack]
        + [coef, w1, flip_weight(w1, CH), w_second, flip_weight(w_second, 64)],
        [
            pltpu.VMEM((32 * TR, TC), F32),
            pltpu.VMEM((3 * CH, 20 * TC), BF16),
            pltpu.VMEM((96, 20 * TC), BF16),
            pltpu.VMEM((192, 18 * TC), BF16),
            pltpu.VMEM((192, 18 * TC), BF16),
            pltpu.VMEM((64, 18 * TC), F32),
            pltpu.VMEM((64, 18 * TC), F32),
            pltpu.VMEM((CH, TC), F32),
            pltpu.VMEM((CH, TC), F32),
            pltpu.VMEM((32 * TR, TC), F32),
        ],
    )
    gsums = stats(gsums, [], [], 3)[0]
    grad_shift = gsums[0, :CH]
    grad_gain = gsums[1, :CH]
    slope = -scale * grad_gain / PIXELS
    coef = across(scale, -scale * grad_shift / PIXELS - slope * mean * inv, slope * inv)
    gfw, gm = call(
        correlate_back_kernel,
        [sds((C, TR * TC), BF16), sds((27, C, TC), BF16)],
        [cv, gpre, coef, fw, m],
        [pltpu.VMEM((24 * TC, TR * TC), BF16), pltpu.VMEM((3 * TC, TR * TC), F32)],
    )
    gfs = give_back(flat, gm)
    rows, pack = call(
        edges2_kernel, [sds((4, C, TC), BF16), sds((2, C, TC), BF16)], [gfw, gfs]
    )
    ghalo = exchange([rows, pack], moves, 5)
    flipped = flip_weight(feat_weight, C)

    def last(k, g):
        return call(
            functools.partial(last_kernel, k),
            [sds((C * TR, TC), BF16)],
            [g] + ghalo + [flipped],
            [pltpu.VMEM((3 * C, 18 * TC), BF16), pltpu.VMEM((C * TR, TC), F32)],
        )[0].reshape(C, TR, TC)

    grad_feat = call(weight_kernel, [sds((C, 9 * C), F32)], [gfw, gfs, xw, xs])[0]
    sums3 = lax.psum((grad_feat, gfirst, gsecond), ("row", "col"))
    grad_winter = last(0, gfw)
    grad_summer = last(1, gfs)
    return (
        refined.reshape(32, TR, TC),
        grad_winter,
        grad_summer,
        sums3[0],
        sums3[1].reshape(64, 9, 9, 16)[:, :, :, :9].reshape(64, 729),
        sums3[2],
        gathered(grad_gain),
        gathered(grad_shift),
    )


def solution(mesh):
    tile = P(None, "row", "col")
    return jax.shard_map(
        body,
        mesh=mesh,
        in_specs=(tile, tile, P(), P(), P(), P(), P(), P(), tile),
        out_specs=(tile, tile, tile, P(), P(), P(), P(), P()),
        check_vma=False,
    )
```

```python
import functools

import jax
import jax.numpy as jnp
from jax import lax
from jax.experimental import pallas as pl
from jax.experimental.pallas import tpu as pltpu
from jax.sharding import PartitionSpec as P

MESH = pl.DeviceIdType.MESH
C = 256
TR = 16
TC = 128
CH = 144
NROW = 16
NCOL = 8
PIXELS = 262144.0
F32 = jnp.float32
BF16 = jnp.bfloat16
VMEM_LIMIT = 58 * 1024 * 1024
NT = (((1,), (1,)), ((), ()))


def vspec():
    return pl.BlockSpec(memory_space=pltpu.VMEM)


def sspec():
    return pl.BlockSpec(memory_space=pltpu.SMEM)


def sds(shape, dtype):
    return jax.ShapeDtypeStruct(shape, dtype)


def call(kernel, outs, ins, scratch=(), in_specs=None, out_specs=None, **params):
    results = pl.pallas_call(
        kernel,
        out_shape=outs,
        in_specs=in_specs or [vspec() for _ in ins],
        out_specs=out_specs or [vspec() for _ in outs],
        scratch_shapes=list(scratch),
        compiler_params=pltpu.CompilerParams(vmem_limit_bytes=VMEM_LIMIT, **params),
    )(*ins)
    return list(results)


def rl(value, shift, axis):
    shift %= value.shape[axis]
    return value if shift == 0 else pltpu.roll(value, shift, axis)


def lane_of(shape):
    return lax.broadcasted_iota(jnp.int32, shape, 1)


def dot(a, b):
    return jnp.dot(a, b, preferred_element_type=F32)


def dot_nt(a, b):
    return lax.dot_general(a, b, NT, preferred_element_type=F32)


def pack_cols(row, cols, count=TR):
    total = None
    for y in range(count):
        value = row(y)
        lane = lane_of(value.shape)
        if total is None:
            total = jnp.zeros(value.shape, F32)
        for col, base in cols:
            total = jnp.where(lane == base + y, rl(value, base + y - col, 1), total)
    return total


TWO = [(0, 0), (1, 32), (126, 64), (127, 96)]


def two_cols(first_lane):
    return [(0, first_lane), (127, 64 + first_lane)]


def put_col(total, value, cols, k):
    lane = lane_of(value.shape)
    for col, base in cols:
        total = jnp.where(lane == base + k, rl(value, base + k - col, 1), total)
    return total


def other_side(left, right):
    lane = lane_of(left.shape)
    col = lax.axis_index("col")
    both = jnp.where(lane >= 64, jnp.where(col > 0, left, 0.0), jnp.where(col < NCOL - 1, right, 0.0))
    return rl(both, 64, 1)


def three_tiles(left, own, right):
    low = lane_of(own.shape) < 64
    return [
        jnp.where(low, rl(left, -64, 1), rl(own, -32, 1)),
        jnp.where(low, rl(left, -96, 1), rl(right, 64, 1)),
        jnp.where(low, own, rl(right, 32, 1)),
    ]


def device_at(drow, dcol):
    row = lax.rem(lax.axis_index("row") + drow + NROW, NROW)
    col = lax.rem(lax.axis_index("col") + dcol + NCOL, NCOL)
    return (row, col)


def greet(steps):
    both = sorted(set(steps) | {(-a, -b) for a, b in steps})
    barrier = pltpu.get_barrier_semaphore()
    for step in both:
        pl.semaphore_signal(barrier, inc=1, device_id=device_at(*step), device_id_type=MESH)
    pl.semaphore_wait(barrier, len(both))


def remote_in(sems, rsems):
    def remote(k, src, dst, step):
        return pltpu.make_async_remote_copy(
            src_ref=src,
            dst_ref=dst,
            send_sem=sems.at[k],
            recv_sem=rsems.at[k],
            device_id=device_at(*step),
            device_id_type=MESH,
        )

    return remote


def start_all(copies):
    for copy in copies:
        copy.start()


def wait_all(copies):
    for copy in copies:
        copy.wait()


def strided(wide, y, channels):
    return wide[pl.ds(y, channels, stride=TR), :]


def start_kernel(
    w_ref, s_ref, c_ref,
    wrows, srows, crows, hw, hs, ct,
    wide, wide2, cwide, sw, ss, sc, rw, rs, rc, kw, ks, kc, iw, is_, ic, sems, rsems,
):
    row = lax.axis_index("row")
    first = row == 0
    last = row == NROW - 1
    remote = remote_in(sems, rsems)
    wide[...] = s_ref[...].astype(F32)
    for k in range(5):
        ss[k] = strided(wide, 11 + k, C).astype(BF16)
        ss[5 + k] = strided(wide, k, C).astype(BF16)
    greet([(1, 0), (0, 1)])
    stage = [
        remote(0, ss.at[pl.ds(0, 5)], rs.at[pl.ds(0, 5)], (1, 0)),
        remote(1, ss.at[pl.ds(5, 5)], rs.at[pl.ds(5, 5)], (-1, 0)),
    ]
    start_all(stage)
    wide2[...] = w_ref[...].astype(F32)
    sw[0] = strided(wide2, TR - 1, C).astype(BF16)
    sw[1] = strided(wide2, 0, C).astype(BF16)
    cwide[...] = c_ref[...].astype(F32)
    for k in range(2):
        sc[k] = strided(cwide, 14 + k, 32).astype(BF16)
        sc[2 + k] = strided(cwide, k, 32).astype(BF16)
    more = [
        remote(2, sw.at[pl.ds(0, 1)], rw.at[pl.ds(0, 1)], (1, 0)),
        remote(3, sw.at[pl.ds(1, 1)], rw.at[pl.ds(1, 1)], (-1, 0)),
        remote(4, sc.at[pl.ds(0, 2)], rc.at[pl.ds(0, 2)], (1, 0)),
        remote(5, sc.at[pl.ds(2, 2)], rc.at[pl.ds(2, 2)], (-1, 0)),
    ]
    start_all(more)
    pack_s = pack_cols(lambda y: strided(wide, y, C), two_cols(5))
    pack_w = pack_cols(lambda y: strided(wide2, y, C), two_cols(1))
    pack_c = pack_cols(lambda y: strided(cwide, y, 32), [(c, b + 2) for c, b in TWO])
    wait_all(stage + more)
    for k in range(10):
        value = jnp.where(first if k < 5 else last, 0.0, rs[k].astype(F32))
        srows[k] = value.astype(BF16)
        pack_s = put_col(pack_s, value, two_cols(0), k if k < 5 else 16 + k)
    ks[...] = pack_s.astype(BF16)
    for k in range(2):
        value = jnp.where(first if k < 1 else last, 0.0, rw[k].astype(F32))
        wrows[k] = value.astype(BF16)
        pack_w = put_col(pack_w, value, two_cols(0), 17 * k)
    kw[...] = pack_w.astype(BF16)
    for k in range(4):
        value = jnp.where(first if k < 2 else last, 0.0, rc[k].astype(F32))
        crows[k] = value.astype(BF16)
        pack_c = put_col(pack_c, value, TWO, k if k < 2 else 16 + k)
    kc[...] = pack_c.astype(BF16)
    stage = []
    for n, (src, dst) in enumerate(((ks, is_), (kw, iw), (kc, ic))):
        stage.append(remote(6 + 2 * n, src, dst.at[0], (0, 1)))
        stage.append(remote(7 + 2 * n, src, dst.at[1], (0, -1)))
    start_all(stage)
    wait_all(stage)
    hs[...] = other_side(is_[0].astype(F32), is_[1].astype(F32)).astype(BF16)
    hw[...] = other_side(iw[0].astype(F32), iw[1].astype(F32)).astype(BF16)
    col = lax.axis_index("col")
    left = jnp.where(col > 0, ic[0].astype(F32), 0.0)
    right = jnp.where(col < NCOL - 1, ic[1].astype(F32), 0.0)
    for k, tile in enumerate(three_tiles(left, kc[...].astype(F32), right)):
        ct[k] = tile.astype(BF16)


def start(w2, s2, c2):
    tile = lambda n, c: pltpu.VMEM((n, c, TC), BF16)
    one = lambda c: pltpu.VMEM((c, TC), BF16)
    return call(
        start_kernel,
        [
            sds((2, C, TC), BF16), sds((10, C, TC), BF16), sds((4, 32, TC), BF16),
            sds((C, TC), BF16), sds((C, TC), BF16), sds((3, 32, TC), BF16),
        ],
        [w2, s2, c2],
        [
            pltpu.VMEM((C * TR, TC), F32), pltpu.VMEM((C * TR, TC), F32), pltpu.VMEM((32 * TR, TC), F32),
            tile(2, C), tile(10, C), tile(4, 32), tile(2, C), tile(10, C), tile(4, 32),
            one(C), one(C), one(32), tile(2, C), tile(2, C), tile(2, 32),
            pltpu.SemaphoreType.DMA((12,)), pltpu.SemaphoreType.DMA((12,)),
        ],
        collective_id=0,
        has_side_effects=True,
    )


def build_x3(x3, row, halo, count, channels, first_lane=0):
    for k in range(count):
        value = row(k)
        lane = lane_of(value.shape)
        at = slice(k * TC, (k + 1) * TC)
        left = jnp.where(lane == 0, rl(halo, -(first_lane + k), 1), rl(value, 1, 1))
        right = jnp.where(lane == TC - 1, rl(halo, TC - 1 - (64 + first_lane + k), 1), rl(value, -1, 1))
        x3[0:channels, at] = left.astype(BF16)
        x3[channels : 2 * channels, at] = value.astype(BF16)
        x3[2 * channels : 3 * channels, at] = right.astype(BF16)


def conv_chunk(w_ref, x3, start, width):
    total = None
    depth = x3.shape[0]
    for a in range(3):
        term = dot(w_ref[:, a * depth : (a + 1) * depth], x3[:, start + a * TC : start + a * TC + width])
        total = term if total is None else total + term
    return total


def winter_kernel(x_ref, ends, halo, w_ref, f_out, x3_out, wide):
    wide[...] = x_ref[...].astype(F32)

    def row(j):
        if j == 0 or j == TR + 1:
            return ends[j // (TR + 1)].astype(F32)
        return strided(wide, j - 1, C)

    build_x3(x3_out, row, halo[...].astype(F32), TR + 2, C)
    for n in range(4):
        f_out[:, n * 512 : (n + 1) * 512] = conv_chunk(w_ref, x3_out, n * 512, 512).astype(BF16)


def summer_kernel(x_ref, ends, halo, w_ref, f_out, x3_out, wide):
    wide[...] = x_ref[...].astype(F32)
    first = lax.axis_index("row") == 0
    last = lax.axis_index("row") == NROW - 1

    def row(j):
        if j < 5:
            return ends[j].astype(F32)
        if j >= 21:
            return ends[j - 16].astype(F32)
        return strided(wide, j - 5, C)

    build_x3(x3_out, row, halo[...].astype(F32), TR + 10, C)
    packs = [jnp.zeros((C, TC), F32), jnp.zeros((C, TC), F32)]
    lane = lane_of((C, TC))
    for n in range(6):
        value = conv_chunk(w_ref, x3_out, n * 512, 512)
        for j in range(4):
            k = n * 4 + j
            part = value[:, j * TC : (j + 1) * TC]
            if k < 4:
                part = jnp.where(first, 0.0, part)
            if k >= 20:
                part = jnp.where(last, 0.0, part)
            f_out[k] = part.astype(BF16)
            for p, at in ((0, k), (1, k - 8)):
                if 0 <= at < 16:
                    low = (lane >= at * 8) & (lane < at * 8 + 4)
                    high = (lane >= at * 8 + 4) & (lane < at * 8 + 8)
                    packs[p] = jnp.where(low, rl(part, at * 8, 1), packs[p])
                    packs[p] = jnp.where(high, rl(part, at * 8 + 4 - 124, 1), packs[p])
    f_out[24] = packs[0].astype(BF16)
    f_out[25] = packs[1].astype(BF16)


def offset_of(off, part, row, col):
    return off[part * NROW * NCOL + row * NCOL + col]


PARTS = 4
WIDE = C // PARTS


def part_of(q):
    return pl.ds(q * WIDE, WIDE)


def match_kernel(off, fp, out, pin, cand, send_buf, ptrio, psend, lsem, sems, rsems, *parts):
    strips, trios = parts[:PARTS], parts[PARTS:]
    row = lax.axis_index("row")
    col = lax.axis_index("col")
    owns = [
        pltpu.make_async_copy(fp.at[pl.ds(0, 24), part_of(q)], strips[q].at[pl.ds(16, 24)], lsem.at[q])
        for q in range(PARTS)
    ]
    start_all(owns)
    greet([(1, 0), (0, 1), (0, 2)])
    remote = remote_in(sems, rsems)
    pstage = [
        remote(0, fp.at[24], pin.at[0], (1, 0)),
        remote(1, fp.at[25], pin.at[1], (-1, 0)),
    ]
    start_all(pstage)
    stages = []
    for q in range(PARTS):
        cs = part_of(q)
        stages.append(
            [
                remote(2 + 2 * q, fp.at[pl.ds(0, 16), cs], strips[q].at[pl.ds(0, 16)], (1, 0)),
                remote(3 + 2 * q, fp.at[pl.ds(8, 16), cs], strips[q].at[pl.ds(40, 16)], (-1, 0)),
            ]
        )
    start_all(stages[0])
    start_all(stages[1])
    wait_all(owns)

    def pick_of(dcol):
        return offset_of(off, 0, row, lax.rem(col + dcol + NCOL, NCOL)) + 1

    wait_all(pstage)
    lane = lane_of((C, TC))
    low = lane < 64
    p0, p1 = fp[24].astype(F32), fp[25].astype(F32)
    above, below = pin[0].astype(F32), pin[1].astype(F32)
    cand[0, 0] = above.astype(BF16)
    cand[0, 1] = jnp.where(low, p0, 0.0).astype(BF16)
    cand[1, 0] = p0.astype(BF16)
    cand[1, 1] = jnp.where(low, rl(p1, 64, 1), 0.0).astype(BF16)
    cand[2, 0] = rl(jnp.where(low, below, p1), 64, 1).astype(BF16)
    cand[2, 1] = jnp.where(low, rl(below, 64, 1), 0.0).astype(BF16)
    second = []
    base = 2 + 2 * PARTS
    for k, dcol in enumerate((-2, -1, 1, 2)):
        pick = pick_of(dcol)
        for j in range(2):
            psend[k, j] = cand[pick, j]
        second.append(remote(base + k, psend.at[k], ptrio.at[2 - dcol], (0, dcol)))
    start_all(second)
    pick = pick_of(0)
    for j in range(2):
        ptrio[2, j] = cand[pick, j]
    base += 4
    picks = [pick_of(-1), pick_of(1)]
    mine = pick_of(0)
    my_row = row + offset_of(off, 0, row, col)
    my_col = col + offset_of(off, 1, row, col)
    dcol = my_col - col + 1
    thirds = []
    for q in range(PARTS):
        cs = part_of(q)
        wait_all(stages[q])
        if q + 2 < PARTS:
            start_all(stages[q + 2])

        def fill(j, carry, cs=cs, q=q):
            send_buf[0, j, cs] = strips[q][16 * picks[0] + j]
            send_buf[1, j, cs] = strips[q][16 * picks[1] + j]
            return carry

        lax.fori_loop(0, 24, fill, 0)
        third = [
            remote(base + 2 * q, send_buf.at[0, :, cs], trios[q].at[2], (0, -1)),
            remote(base + 2 * q + 1, send_buf.at[1, :, cs], trios[q].at[0], (0, 1)),
        ]
        start_all(third)
        thirds.append(third)

        def keep(j, carry, q=q):
            trios[q][1, j] = strips[q][16 * mine + j]
            return carry

        lax.fori_loop(0, 24, keep, 0)
    wait_all(second)
    low = lax.rem(lane, 8) < 4
    for j in range(2):
        right = jnp.where(my_col == NCOL - 1, 0.0, ptrio[dcol + 2, j].astype(F32))
        left = jnp.where(my_col == 0, 0.0, ptrio[dcol, j].astype(F32))
        out[:, (24 + j) * TC : (25 + j) * TC] = jnp.where(low, right, left).astype(BF16)
    for q in range(PARTS):
        wait_all(thirds[q])
        cs = part_of(q)
        for j in range(24):
            out[cs, j * TC : (j + 1) * TC] = trios[q][dcol, j]


def match(offsets, fp):
    dma = pltpu.SemaphoreType.DMA((6 + 4 * PARTS,))
    return call(
        match_kernel,
        [sds((C, 26 * TC), BF16)],
        [offsets, fp],
        [
            pltpu.VMEM((2, C, TC), BF16),
            pltpu.VMEM((3, 2, C, TC), BF16),
            pltpu.VMEM((2, 24, C, TC), BF16),
            pltpu.VMEM((5, 2, C, TC), BF16),
            pltpu.VMEM((4, 2, C, TC), BF16),
            pltpu.SemaphoreType.DMA((PARTS,)),
            dma,
            dma,
        ]
        + [pltpu.VMEM((56, WIDE, TC), BF16)] * PARTS
        + [pltpu.VMEM((3, 24, WIDE, TC), BF16)] * PARTS,
        in_specs=[sspec(), vspec()],
        collective_id=1,
        has_side_effects=True,
    )[0]


def bit_off(lane, bit):
    return (lane & bit) == 0


def shear(main, rim):
    low = lane_of((80, TC)) < 64
    w = jnp.where(low, jnp.concatenate([rim, main[0:72]], 0), jnp.concatenate([main[56:128], rim], 0))
    w = jnp.where(bit_off(lane_of((48, TC)), 32), w[0:48], w[32:80])
    w = jnp.where(bit_off(lane_of((32, TC)), 16), w[0:32], w[16:48])
    w = jnp.where(bit_off(lane_of((24, TC)), 8), w[0:24], w[8:32])
    lane = lane_of((16, TC))
    w = jnp.where(bit_off(lane, 4), rl(w, -4, 0)[0:16], w[8:24])
    w = jnp.where(bit_off(lane, 2), w, rl(w, -2, 0))
    w = jnp.where(bit_off(lane, 1), w, rl(w, -1, 0))
    return jnp.where(lax.broadcasted_iota(jnp.int32, (16, TC), 0) < 9, w, 0.0)


def unshear(value):
    lane = lane_of((16, TC))
    w = jnp.where(bit_off(lane, 1), value, rl(value, 1, 0))
    w = jnp.where(bit_off(lane, 2), w, rl(w, 2, 0))
    zeros = lambda n: jnp.zeros((n, TC), F32)
    padded = jnp.concatenate([w, zeros(8)], 0)
    w = jnp.where(bit_off(lane_of((24, TC)), 4), rl(padded, 4, 0), jnp.concatenate([zeros(8), w], 0))
    for n, bit in ((24, 8), (32, 16), (48, 32)):
        w = jnp.where(
            bit_off(lane_of((n + bit, TC)), bit),
            jnp.concatenate([w, zeros(bit)], 0),
            jnp.concatenate([zeros(bit), w], 0),
        )
    low = lambda n: lane_of((n, TC)) < 64
    main = jnp.concatenate(
        [
            jnp.where(low(56), w[8:64], 0.0),
            jnp.where(low(16), w[64:80], w[0:16]),
            jnp.where(low(56), 0.0, w[16:72]),
        ],
        0,
    )
    return main, jnp.where(low(8), w[0:8], w[72:80])


def row_sums(first, second):
    ones = jnp.ones((8, TC), F32)
    a = lax.dot_general(ones, first, NT, precision=lax.Precision.HIGHEST, preferred_element_type=F32)
    b = lax.dot_general(ones, second, NT, precision=lax.Precision.HIGHEST, preferred_element_type=F32)
    return jnp.where(lax.broadcasted_iota(jnp.int32, a.shape, 0) == 0, a, b)


def correlate_kernel(fw, m, cv, pack, sums, mt, rt, grim, s1, s2):
    for r in range(24):
        mt[r * TC : (r + 1) * TC, :] = m[:, r * TC : (r + 1) * TC].T
    for q in range(2):
        rt[q * TC : (q + 1) * TC, :] = m[:, (24 + q) * TC : (25 + q) * TC].T
    for n in range(4):
        grim[:, n * 512 : (n + 1) * 512] = dot(rt[...], fw[:, n * 512 : (n + 1) * 512])
    s1[...] = jnp.zeros_like(s1)
    s2[...] = jnp.zeros_like(s2)

    def at_row(y, carry):
        lanes = pl.ds(pl.multiple_of(y * TC, TC), TC)
        feat = fw[:, lanes]
        for a in range(9):
            main = dot(mt[pl.ds(pl.multiple_of((y + a) * TC, TC), TC), :], feat)
            rim = grim[pl.ds(pl.multiple_of((y + a) * 8, 8), 8), lanes]
            value = shear(main, rim) * 0.0625
            rows = slice(a * 16, (a + 1) * 16)
            cv[y, rows, :] = value
            s1[rows, :] += value
            s2[rows, :] += value * value
        return carry

    lax.fori_loop(0, TR, at_row, 0)
    pack[...] = pack_cols(lambda y: cv[y], [(c, b + 2) for c, b in TWO])
    sums[...] = jnp.zeros_like(sums)
    sums[:, 0:CH] = row_sums(s1[...], s2[...])


def reduce_one(src, dst, out, send, recv, axis, count):
    copies = []
    for d in range(1, count):
        step = (0, d) if axis == "col" else (d, 0)
        copies.append(
            pltpu.make_async_remote_copy(
                src_ref=src,
                dst_ref=dst.at[d],
                send_sem=send.at[d],
                recv_sem=recv.at[d],
                device_id=device_at(*step),
                device_id_type=MESH,
            )
        )
    start_all(copies)
    dst[0] = src[...]
    wait_all(copies)
    me = lax.axis_index(axis)
    total = None
    for d in range(count):
        value = dst[lax.rem(me - d + count, count)]
        total = value if total is None else total + value
    out[...] = total


RING = [(0, d) for d in range(1, NCOL)] + [(d, 0) for d in range(1, NROW)]


def stats_kernel(with_halo, *refs):
    if with_halo:
        value, cv, pack, out, vrows, own, sides, gcol, grow, csend, crecv, rsend, rrecv, sems, rsems = refs
    else:
        value, out, gcol, grow, csend, crecv, rsend, rrecv = refs
    greet(RING)
    if with_halo:
        remote = remote_in(sems, rsems)
        rows = [
            remote(0, cv.at[pl.ds(14, 2)], vrows.at[pl.ds(0, 2)], (1, 0)),
            remote(1, cv.at[pl.ds(0, 2)], vrows.at[pl.ds(2, 2)], (-1, 0)),
        ]
        start_all(rows)
    reduce_one(value, gcol, out, csend, crecv, "col", NCOL)
    if with_halo:
        wait_all(rows)
        total = pack[...]
        for k in range(4):
            total = put_col(total, vrows[k], TWO, k if k < 2 else 16 + k)
        own[...] = total
        cols = [remote(2, own, sides.at[0], (0, 1)), remote(3, own, sides.at[1], (0, -1))]
        start_all(cols)
    reduce_one(out, grow, out, rsend, rrecv, "row", NROW)
    if with_halo:
        wait_all(cols)


def stats(value, halo, collective_id):
    dma = pltpu.SemaphoreType.DMA
    outs = [sds(value.shape, F32)]
    if halo:
        outs += [sds((4, CH, TC), F32), sds((CH, TC), F32), sds((2, CH, TC), F32)]
    return call(
        functools.partial(stats_kernel, bool(halo)),
        outs,
        [value] + halo,
        [
            pltpu.VMEM((NCOL,) + value.shape, F32),
            pltpu.VMEM((NROW,) + value.shape, F32),
            dma((NCOL,)),
            dma((NCOL,)),
            dma((NROW,)),
            dma((NROW,)),
        ]
        + ([dma((4,)), dma((4,))] if halo else []),
        collective_id=collective_id,
        has_side_effects=True,
    )


def tile_inside(b, shape):
    lane = lane_of(shape)
    row = lax.axis_index("row")
    col = lax.axis_index("col")
    local = jnp.where(lane < 64, lane, lane - 64)
    y = row * TR - 2 + local
    x = jnp.where(lane < 64, col * TC - 1 + b, col * TC + TC + b)
    return (y >= 0) & (y < NROW * TR) & (x >= 0) & (x < NCOL * TC) & (local < 20)


def rim_patches(tiles, a):
    return jnp.concatenate([rl(t, -a, 1) for t in tiles], 0).astype(BF16)


def silu_parts(value):
    sigma = jax.nn.sigmoid(value)
    return value * sigma, sigma * (1.0 + value * (1.0 - sigma))


def refine_kernel(
    cv, vrows, own_pack, sides, cot, crows, ct,
    coef, w1, w1f, w2, w2f,
    refined, gpre, gfirst, gsecond, sums,
    cwide, n3x, c3x, h3, gh3, hpre, gmain, s1, s2, rwide,
):
    row = lax.axis_index("row")
    first = row == 0
    last = row == NROW - 1
    scale, bias, inv, mid = (coef[k] for k in range(4))

    def normed_of(value):
        return silu_parts(value * scale + bias)[0]

    ntiles = [
        jnp.where(tile_inside(b - 1, (CH, TC)), normed_of(t), 0.0) for b, t in enumerate(three_tiles(sides[0], own_pack[...], sides[1]))
    ]

    def nrow(k):
        if k < 2:
            return jnp.where(first, 0.0, normed_of(vrows[k]))
        if k >= 18:
            return jnp.where(last, 0.0, normed_of(vrows[k - 16]))
        return normed_of(cv[k - 2])

    build_x3(n3x, nrow, ntiles[1], 20, CH)
    ctiles = [ct[k].astype(F32) for k in range(3)]
    cwide[...] = cot[...].astype(F32)

    def crow(k):
        if k < 2:
            return crows[k].astype(F32)
        if k >= 18:
            return crows[k - 16].astype(F32)
        return strided(cwide, k - 2, 32)

    build_x3(c3x, crow, ctiles[1], 20, 32)

    def both(w_ref, x3, tiles):
        depth = x3.shape[0]
        rim = None
        for a in range(3):
            term = dot(w_ref[:, a * depth : (a + 1) * depth], rim_patches(tiles, a))
            rim = term if rim is None else rim + term
        return rim

    lane = lane_of((64, TC))
    local = jnp.where(lane < 64, lane, lane - 64)
    ypos = row * TR - 1 + local
    col = lax.axis_index("col")
    xpos = jnp.where(lane < 64, col * TC - 1, col * TC + TC)
    rim_in = (ypos >= 0) & (ypos < NROW * TR) & (local < 18) & (xpos >= 0) & (xpos < NCOL * TC)
    rim_h, rim_slope = silu_parts(both(w1, n3x, ntiles))
    rim_g = both(w2f, c3x, ctiles)
    rim_h = jnp.where(rim_in, rim_h, 0.0)
    rim_g = jnp.where(rim_in, rim_g * rim_slope, 0.0)
    for n in range(6):
        hpre[:, n * 384 : (n + 1) * 384] = conv_chunk(w1, n3x, n * 384, 384)
        gmain[:, n * 384 : (n + 1) * 384] = conv_chunk(w2f, c3x, n * 384, 384)

    def edge(k):
        return first if k == 0 else (last if k == 17 else None)

    def hrow(k):
        value, slope = silu_parts(hpre[:, k * TC : (k + 1) * TC])
        grad = gmain[:, k * TC : (k + 1) * TC] * slope
        gone = edge(k)
        if gone is not None:
            value = jnp.where(gone, 0.0, value)
            grad = jnp.where(gone, 0.0, grad)
        gmain[:, k * TC : (k + 1) * TC] = grad
        return value

    build_x3(h3, hrow, rim_h, 18, 64)
    build_x3(gh3, lambda k: gmain[:, k * TC : (k + 1) * TC], rim_g, 18, 64)
    for n in range(4):
        value = conv_chunk(w2, h3, n * 512, 512)
        for j in range(4):
            rwide[pl.ds(n * 4 + j, 32, stride=TR), :] = value[:, j * TC : (j + 1) * TC]
    refined[...] = rwide[...].astype(BF16)
    own = slice(TC, 17 * TC)
    mine = slice(2 * TC, 18 * TC)
    gfirst[:, 9 * CH :] = jnp.zeros((64, 1408 - 9 * CH), F32)
    gsecond[:, 576:] = jnp.zeros((32, 64), F32)
    for a in range(3):
        gsecond[:, a * 192 : (a + 1) * 192] = dot_nt(c3x[32:64, mine], h3[:, a * TC : (a + 16) * TC])
        gfirst[:, a * 432 : (a + 1) * 432] = dot_nt(gh3[64:128, own], n3x[:, (a + 1) * TC : (a + 17) * TC])
    s1[...] = jnp.zeros_like(s1)
    s2[...] = jnp.zeros_like(s2)
    for n in range(4):
        value = conv_chunk(w1f, gh3, n * 512, 512)
        for j in range(4):
            y = n * 4 + j
            volume = cv[y]
            grad = value[:, j * TC : (j + 1) * TC] * silu_parts(volume * scale + bias)[1]
            gpre[y] = grad
            s1[...] += grad
            s2[...] += grad * (volume * inv - mid)
    sums[...] = jnp.zeros_like(sums)
    sums[:, 0:CH] = row_sums(s1[...], s2[...])


def correlate_back_kernel(cv, gpre, coef, fw, m, gfw, gm, kw, q, qrim):
    def at_row(y, carry):
        lanes = pl.ds(pl.multiple_of(y * TC, TC), TC)
        grad = coef[0] * gpre[y] + coef[1] + coef[2] * cv[y]
        grad = grad.astype(BF16).astype(F32)
        for a in range(9):
            main, rim = unshear(grad[a * 16 : (a + 1) * 16])
            q[pl.ds(pl.multiple_of((y + a) * TC, TC), TC), lanes] = main.astype(BF16)
            qrim[pl.ds(pl.multiple_of((y + a) * 8, 8), 8), lanes] = rim
        return carry

    qrim[...] = jnp.zeros_like(qrim)
    lax.fori_loop(0, TR, at_row, 0)
    for y in range(TR):
        at = slice(y * TC, (y + 1) * TC)
        value = dot(m[:, y * TC : (y + 9) * TC], q[y * TC : (y + 9) * TC, at])
        value = value + dot(m[:, 24 * TC : 26 * TC], qrim[:, at].astype(BF16))
        gfw[:, at] = (value * 0.0625).astype(BF16)
    for r in range(24):
        at = slice(max(0, r - 8) * TC, (min(15, r) + 1) * TC)
        value = dot_nt(fw[:, at], q[r * TC : (r + 1) * TC, at])
        gm[r] = (value * 0.0625).astype(BF16)
    kw[...] = pack_cols(lambda y: gfw[:, y * TC : (y + 1) * TC].astype(F32), two_cols(1)).astype(BF16)
    for k in range(2):
        value = dot_nt(fw[...], qrim[k * TC : (k + 1) * TC, :].astype(BF16))
        gm[24 + k] = (value * 0.0625).astype(BF16)


def return_kernel(
    off, gm, gfw, kw0, ext, hs, wrows, hw,
    ptrio, strip, be, ab, pout, pin, g24, g5, pab, pq, pack, side, rw, kw, iw, lsem, sems, rsems, *trios,
):
    row = lax.axis_index("row")
    col = lax.axis_index("col")
    owns = [
        pltpu.make_async_copy(gm.at[pl.ds(0, 24), part_of(q)], trios[q].at[1, pl.ds(0, 24)], lsem.at[q])
        for q in range(PARTS)
    ]
    start_all(owns)
    for q in range(PARTS):
        for k in range(3):
            trios[q][k, 24] = jnp.zeros((WIDE, TC), BF16)
    greet([(1, 0), (0, 1)])
    remote = remote_in(sems, rsems)
    count = [0]

    def new(src, dst, step):
        count[0] += 1
        return remote(count[0] - 1, src, dst, step)

    pstage = [new(gm.at[pl.ds(24, 2)], ptrio.at[0], (0, 1)), new(gm.at[pl.ds(24, 2)], ptrio.at[2], (0, -1))]
    wstage = [
        new(gfw.at[:, pl.ds((TR - 1) * TC, TC)], rw.at[0], (1, 0)),
        new(gfw.at[:, pl.ds(0, TC)], rw.at[1], (-1, 0)),
    ]
    start_all(pstage + wstage)
    stages = []
    for q in range(PARTS):
        cs = part_of(q)
        stages.append(
            [
                new(gm.at[pl.ds(0, 24), cs], trios[q].at[0, pl.ds(0, 24)], (0, 1)),
                new(gm.at[pl.ds(0, 24), cs], trios[q].at[2, pl.ds(0, 24)], (0, -1)),
            ]
        )
    start_all(stages[0])
    start_all(stages[1])
    wait_all(owns)
    sources = []
    for k in range(3):
        place = col + k - 1
        there = lax.rem(place + NCOL, NCOL)
        drow = offset_of(off, 0, row, there)
        dcol = offset_of(off, 1, row, there)
        good = (dcol == 1 - k) & (place >= 0) & (place < NCOL)
        sources.append((drow, good))

    first, last = row == 0, row == NROW - 1
    zero = jnp.zeros((C, TC), F32)
    lane = lane_of((C, TC))
    low = lane < 64

    def only(flag, ref):
        return jnp.where(flag, ref.astype(F32), 0.0)

    wait_all(pstage)
    to_above, own0, own1, to_below = zero, zero, zero, zero
    for k, (drow, good) in enumerate(sources):
        t0, t1 = (gm[24], gm[25]) if k == 1 else (ptrio[k, 0], ptrio[k, 1])
        t0, t1 = t0.astype(F32), jnp.where(low, t1.astype(F32), 0.0)
        up, level, down = (good & (drow == v) for v in (-1, 0, 1))
        turned0, turned1 = rl(t0, 64, 1), rl(t1, 64, 1)
        to_above += jnp.where(up, t0, 0.0)
        own0 += jnp.where(up, t1, 0.0) + jnp.where(level, t0, 0.0)
        own1 += jnp.where(level, turned1, 0.0) + jnp.where(down & jnp.logical_not(low), turned0, 0.0)
        to_below += jnp.where(down, turned1 + jnp.where(low, turned0, 0.0), 0.0)
    pout[0] = to_above.astype(BF16)
    pout[1] = to_below.astype(BF16)
    pstage = [new(pout.at[0], pin.at[0], (-1, 0)), new(pout.at[1], pin.at[1], (1, 0))]
    start_all(pstage)

    wait_all(wstage)
    kpack = kw0[...].astype(F32)
    for k in range(2):
        value = only(jnp.logical_not(first if k == 0 else last), rw[k])
        wrows[k] = value.astype(BF16)
        kpack = put_col(kpack, value, two_cols(0), 17 * k)
    kw[...] = kpack.astype(BF16)
    wstage = [new(kw, iw.at[0], (0, 1)), new(kw, iw.at[1], (0, -1))]
    start_all(wstage)

    thirds = []
    for q in range(PARTS):
        cs = part_of(q)
        wait_all(stages[q])
        if q + 2 < PARTS:
            start_all(stages[q + 2])

        def gather(p, carry, cs=cs, q=q):
            total = None
            for k, (drow, good) in enumerate(sources):
                j = p - 16 * (drow + 1)
                fits = good & (j >= 0) & (j < 24)
                value = trios[q][k, jnp.where(fits, j, 24)].astype(F32)
                total = value if total is None else total + value
            strip[p, cs] = total.astype(BF16)
            return carry

        lax.fori_loop(0, 56, gather, 0)
        third = [
            new(strip.at[pl.ds(0, 16), cs], be.at[:, cs], (-1, 0)),
            new(strip.at[pl.ds(40, 16), cs], ab.at[:, cs], (1, 0)),
        ]
        start_all(third)
        thirds.append(third)
    wait_all(wstage)
    hw[...] = other_side(iw[0].astype(F32), iw[1].astype(F32)).astype(BF16)
    wait_all(pstage)
    not_first, not_last = row > 0, row < NROW - 1
    p0 = own0 + only(not_last, pin[0])
    p1 = own1 + only(not_first, pin[1])
    tile_a = p0 + jnp.where(low, 0.0, rl(p1, 64, 1))
    tile_b = jnp.where(low, rl(p1, 64, 1), 0.0)
    pab[0] = tile_a.astype(BF16)
    pab[1] = tile_b.astype(BF16)
    fourth = [new(pab.at[0], pq.at[0], (-1, 0)), new(pab.at[1], pq.at[1], (1, 0))]
    start_all(fourth)
    for q in range(PARTS):
        cs = part_of(q)
        wait_all(thirds[q])
        for k in range(24):
            total = strip[16 + k, cs].astype(F32)
            if k < 16:
                total = total + only(not_last, be[k, cs])
            if k >= 8:
                total = total + only(not_first, ab[k - 8, cs])
            g24[k, cs] = total.astype(BF16)
        more = [
            new(g24.at[pl.ds(0, 5), cs], g5.at[1, :, cs], (-1, 0)),
            new(g24.at[pl.ds(19, 5), cs], g5.at[0, :, cs], (1, 0)),
        ]
        start_all(more)
        fourth = fourth + more
    wait_all(fourth)
    tile_a = tile_a + jnp.where((lane >= 24) & (lane < 64), only(not_first, pq[1]), 0.0)
    tile_b = tile_b + jnp.where(lane < 40, only(not_last, pq[0]), 0.0)
    pack[0] = tile_a.astype(BF16)
    pack[1] = tile_b.astype(BF16)
    total = zero
    for k in range(18):
        value = g24[k + 3].astype(F32)
        if k < 5:
            value = value + only(not_first, g5[0, k])
        if k >= 13:
            value = value + only(not_last, g5[1, k - 13])
        if k == 0:
            value = only(not_first, value)
        if k == 17:
            value = only(not_last, value)
        strip[k] = value.astype(BF16)
        total = put_col(total, value, two_cols(0), k)
    pack[2] = total.astype(BF16)
    stage = [new(pack, side.at[0], (0, 1)), new(pack, side.at[1], (0, -1))]
    start_all(stage)
    source = lax.broadcasted_iota(jnp.int32, (2 * TC, TC), 0)
    target = lax.broadcasted_iota(jnp.int32, (2 * TC, TC), 1)
    take = ((target < 18) & (source == (target + 3) * 8 + 7)) | (
        (target >= 64) & (target < 82) & (source == (target - 61) * 8)
    )
    rims = dot(pack[0], take[0:TC].astype(F32).astype(BF16)) + dot(pack[1], take[TC:].astype(F32).astype(BF16))
    wait_all(stage)
    halo = other_side(side[0, 2].astype(F32), side[1, 2].astype(F32))
    halo = halo + jnp.where(low, only(col > 0, rims), only(col < NCOL - 1, rims))
    at = jnp.where(low, lane, lane - 64)
    gone = (first & (at == 0)) | (last & (at == 17))
    hs[...] = jnp.where(gone, 0.0, halo).astype(BF16)
    for k in range(18):
        p, base = ((0, (k + 3) * 8) if k + 3 < 16 else (1, (k - 13) * 8))
        value = strip[k].astype(F32)
        left = rl(only(col > 0, side[0, p]), -base, 1)
        right = rl(only(col < NCOL - 1, side[1, p]), 120 - base, 1)
        extra = jnp.where(lane < 4, left, 0.0) + jnp.where(lane >= 124, right, 0.0)
        if k == 0:
            extra = only(not_first, extra)
        if k == 17:
            extra = only(not_last, extra)
        ext[:, k * TC : (k + 1) * TC] = (value + extra).astype(BF16)


def give_back(offsets, gm, gfw, kw):
    tile = lambda *n: pltpu.VMEM(n + (C, TC), BF16)
    n = 14 + 6 * PARTS
    return call(
        return_kernel,
        [sds((C, 18 * TC), BF16), sds((C, TC), BF16), sds((2, C, TC), BF16), sds((C, TC), BF16)],
        [offsets, gm, gfw, kw],
        [
            tile(3, 2), tile(56), tile(16), tile(16), tile(2), tile(2), tile(24), tile(2, 5),
            tile(2), tile(2), tile(3), tile(2, 3), tile(2), tile(), tile(2),
            pltpu.SemaphoreType.DMA((PARTS,)), pltpu.SemaphoreType.DMA((n,)), pltpu.SemaphoreType.DMA((n,)),
        ]
        + [pltpu.VMEM((3, 25, WIDE, TC), BF16)] * PARTS,
        in_specs=[sspec(), vspec(), vspec(), vspec()],
        collective_id=4,
        has_side_effects=True,
    )


TILES = 384
HALF = TILES // 2
SHARE = TILES // 8
LEAST = SHARE // NROW


def finish_kernel(
    gw, wrows, hw, gs, hs, xw, xs, flipped, gfirst, gsecond,
    out_w, out_s, feat_out, first_out, second_out,
    x3, wide, buf, half_in, half, y_in, share, row_in, full, sems, rsems,
):
    row = lax.axis_index("row")
    col = lax.axis_index("col")
    core = lax.rem(col, 2)
    chip = lax.div(col, 2)
    greet(RING)
    count = [0]

    def new(src, dst, device):
        k = count[0]
        count[0] += 1
        return pltpu.make_async_remote_copy(
            src_ref=src,
            dst_ref=dst,
            send_sem=sems.at[k],
            recv_sem=rsems.at[k],
            device_id=device,
            device_id_type=MESH,
        )

    for a in range(3):
        xw_at = slice(a * TC, (a + 16) * TC)
        xs_at = slice((a + 4) * TC, (a + 20) * TC)
        for n in range(3):
            part = slice(n * C, (n + 1) * C)
            value = dot_nt(gw[...], xw[part, xw_at]) + dot_nt(gs[:, TC : 17 * TC], xs[part, xs_at])
            value = value.astype(BF16)
            for t in range(2):
                for g in range(16):
                    buf[(a * 6 + n * 2 + t) * 16 + g] = value[g * 16 : (g + 1) * 16, t * TC : (t + 1) * TC]
    for t in range(11):
        for g in range(4):
            buf[288 + t * 4 + g] = gfirst[g * 16 : (g + 1) * 16, t * TC : (t + 1) * TC].astype(BF16)
    for t in range(5):
        for g in range(2):
            buf[332 + t * 2 + g] = gsecond[g * 16 : (g + 1) * 16, t * TC : (t + 1) * TC].astype(BF16)
    for t in range(342, TILES):
        buf[t] = jnp.zeros((16, TC), BF16)
    partner = (row, col + 1 - 2 * core)
    pair = new(buf.at[pl.ds(HALF * (1 - core), HALF)], half_in, partner)
    pair.start()

    def w_row(k):
        if k == 0 or k == TR + 1:
            return wrows[k // (TR + 1)].astype(F32)
        return gw[:, (k - 1) * TC : k * TC].astype(F32)

    build_x3(x3, w_row, hw[...].astype(F32), TR + 2, C)
    pair.wait()

    def add_half(k, carry):
        half[k] = (buf[HALF * core + k].astype(F32) + half_in[k].astype(F32)).astype(BF16)
        return carry

    lax.fori_loop(0, HALF, add_half, 0)
    chips = []
    for d in range(1, 4):
        there = lax.rem(chip + d, 4)
        chips.append(
            new(half.at[pl.ds(SHARE * there, SHARE)], y_in.at[d - 1], (row, 2 * there + core))
        )
    start_all(chips)
    for n in range(4):
        value = conv_chunk(flipped, x3, n * 512, 512)
        for j in range(4):
            wide[pl.ds(n * 4 + j, C, stride=TR), :] = value[:, j * TC : (j + 1) * TC]
    out_w[...] = wide[...].astype(BF16)
    wait_all(chips)

    def add_share(k, carry):
        total = half[SHARE * chip + k].astype(F32)
        for d in range(3):
            total = total + y_in[d, k].astype(F32)
        share[k] = total.astype(BF16)
        return carry

    lax.fori_loop(0, SHARE, add_share, 0)
    rows = []
    for d in range(1, NROW):
        there = lax.rem(row + d, NROW)
        rows.append(new(share.at[pl.ds(LEAST * there, LEAST)], row_in.at[d - 1], (there, col)))
    start_all(rows)
    build_x3(x3, lambda k: gs[:, k * TC : (k + 1) * TC].astype(F32), hs[...].astype(F32), TR + 2, C)
    wait_all(rows)
    spot = HALF * core + SHARE * chip + LEAST * row
    for k in range(LEAST):
        total = share[LEAST * row + k].astype(F32)
        for d in range(NROW - 1):
            total = total + row_in[d, k].astype(F32)
        full[spot + k] = total.astype(BF16)
    mine = full.at[pl.ds(spot, LEAST)]
    rows = [new(mine, mine, (lax.rem(row + d, NROW), col)) for d in range(1, NROW)]
    start_all(rows)
    value = conv_chunk(flipped, x3, 0, 512)
    for j in range(4):
        wide[pl.ds(j, C, stride=TR), :] = value[:, j * TC : (j + 1) * TC]
    wait_all(rows)
    mine = full.at[pl.ds(HALF * core + SHARE * chip, SHARE)]
    chips = [new(mine, mine, (row, 2 * lax.rem(chip + d, 4) + core)) for d in range(1, 4)]
    start_all(chips)
    for n in range(1, 4):
        value = conv_chunk(flipped, x3, n * 512, 512)
        for j in range(4):
            wide[pl.ds(n * 4 + j, C, stride=TR), :] = value[:, j * TC : (j + 1) * TC]
    out_s[...] = wide[...].astype(BF16)
    wait_all(chips)
    mine = full.at[pl.ds(HALF * core, HALF)]
    pair = new(mine, mine, partner)
    pair.start()
    pair.wait()
    for t in range(18):
        for g in range(16):
            feat_out[g * 16 : (g + 1) * 16, t * TC : (t + 1) * TC] = full[t * 16 + g].astype(F32)
    for t in range(11):
        for g in range(4):
            first_out[g * 16 : (g + 1) * 16, t * TC : (t + 1) * TC] = full[288 + t * 4 + g].astype(F32)
    for t in range(5):
        for g in range(2):
            second_out[g * 16 : (g + 1) * 16, t * TC : (t + 1) * TC] = full[332 + t * 2 + g].astype(F32)


def finish(*ins):
    tile = lambda *n: pltpu.VMEM(n + (16, TC), BF16)
    n = 2 + 2 * 3 + 2 * (NROW - 1)
    return call(
        finish_kernel,
        [
            sds((C * TR, TC), BF16), sds((C * TR, TC), BF16),
            sds((C, 9 * C), F32), sds((64, 1408), F32), sds((32, 640), F32),
        ],
        list(ins),
        [
            pltpu.VMEM((3 * C, 18 * TC), BF16), pltpu.VMEM((C * TR, TC), F32),
            tile(TILES), tile(HALF), tile(HALF), tile(3, SHARE), tile(SHARE), tile(NROW - 1, LEAST), tile(TILES),
            pltpu.SemaphoreType.DMA((n,)), pltpu.SemaphoreType.DMA((n,)),
        ],
        collective_id=5,
        has_side_effects=True,
    )


def flip_weight(weight, in_channels):
    out_channels = weight.shape[0]
    return (
        weight.reshape(out_channels, 9, in_channels)[:, ::-1, :]
        .transpose(2, 1, 0)
        .reshape(in_channels, 9 * out_channels)
    )


def spread(vector):
    return jnp.pad(vector.reshape(9, 9), ((0, 0), (0, 7))).reshape(CH)


def gathered(vector):
    return vector.reshape(9, 16)[:, :9].reshape(81)


def across(*vectors):
    return jnp.stack([jnp.broadcast_to(v[:, None], (CH, TC)) for v in vectors])


def body(winter, summer, offsets, feat_weight, bn_gain, bn_shift, w_first, w_second, cotangent):
    w2 = winter.reshape(C * TR, TC)
    s2 = summer.reshape(C * TR, TC)
    c2 = cotangent.reshape(32 * TR, TC)
    flat = offsets.reshape(-1)
    wrows, srows, crows, hw, hs, ct = start(w2, s2, c2)
    fs, xs = call(
        summer_kernel,
        [sds((26, C, TC), BF16), sds((3 * C, 26 * TC), BF16)],
        [s2, srows, hs, feat_weight],
        [pltpu.VMEM((C * TR, TC), F32)],
    )
    fw, xw = call(
        winter_kernel,
        [sds((C, TR * TC), BF16), sds((3 * C, 18 * TC), BF16)],
        [w2, wrows, hw, feat_weight],
        [pltpu.VMEM((C * TR, TC), F32)],
    )
    m = match(flat, fs)
    cv, cvpack, sums = call(
        correlate_kernel,
        [sds((TR, CH, TC), F32), sds((CH, TC), F32), sds((8, 256), F32)],
        [fw, m],
        [
            pltpu.VMEM((24 * TC, C), BF16),
            pltpu.VMEM((2 * TC, C), BF16),
            pltpu.VMEM((2 * TC, TR * TC), F32),
            pltpu.VMEM((CH, TC), F32),
            pltpu.VMEM((CH, TC), F32),
        ],
    )
    sums, vrows, own_pack, sides = stats(sums, [cv, cvpack], 2)
    mean = sums[0, :CH] / PIXELS
    inv = lax.rsqrt(sums[1, :CH] / PIXELS - mean * mean + 1e-05)
    gain = spread(bn_gain)
    scale = gain * inv
    coef = across(scale, spread(bn_shift) - mean * scale, inv, mean * inv)
    w1 = jnp.pad(w_first.reshape(64, 9, 9, 9), ((0, 0), (0, 0), (0, 0), (0, 7))).reshape(64, 9 * CH)
    refined, gpre, gfirst, gsecond, gsums = call(
        refine_kernel,
        [
            sds((32 * TR, TC), BF16),
            sds((TR, CH, TC), F32),
            sds((64, 1408), F32),
            sds((32, 640), F32),
            sds((8, 256), F32),
        ],
        [cv, vrows, own_pack, sides, c2, crows, ct]
        + [coef, w1, flip_weight(w1, CH), w_second, flip_weight(w_second, 64)],
        [
            pltpu.VMEM((32 * TR, TC), F32),
            pltpu.VMEM((3 * CH, 20 * TC), BF16),
            pltpu.VMEM((96, 20 * TC), BF16),
            pltpu.VMEM((192, 18 * TC), BF16),
            pltpu.VMEM((192, 18 * TC), BF16),
            pltpu.VMEM((64, 18 * TC), F32),
            pltpu.VMEM((64, 18 * TC), F32),
            pltpu.VMEM((CH, TC), F32),
            pltpu.VMEM((CH, TC), F32),
            pltpu.VMEM((32 * TR, TC), F32),
        ],
    )
    gsums = stats(gsums, [], 3)[0]
    grad_shift = gsums[0, :CH]
    grad_gain = gsums[1, :CH]
    slope = -scale * grad_gain / PIXELS
    coef = across(scale, -scale * grad_shift / PIXELS - slope * mean * inv, slope * inv)
    gfw, gm, kw = call(
        correlate_back_kernel,
        [sds((C, TR * TC), BF16), sds((26, C, TC), BF16), sds((C, TC), BF16)],
        [cv, gpre, coef, fw, m],
        [pltpu.VMEM((24 * TC, TR * TC), BF16), pltpu.VMEM((2 * TC, TR * TC), F32)],
    )
    gs, ghs, gwrows, ghw = give_back(flat, gm, gfw, kw)
    grad_winter, grad_summer, gfeat, gfirst, gsecond = finish(
        gfw, gwrows, ghw, gs, ghs, xw, xs, flip_weight(feat_weight, C), gfirst, gsecond
    )
    return (
        refined.reshape(32, TR, TC),
        grad_winter.reshape(C, TR, TC),
        grad_summer.reshape(C, TR, TC),
        gfeat,
        gfirst[:, : 9 * CH].reshape(64, 9, 9, 16)[:, :, :, :9].reshape(64, 729),
        gsecond[:, :576],
        gathered(grad_gain),
        gathered(grad_shift),
    )


def solution(mesh):
    tile = P(None, "row", "col")
    return jax.shard_map(
        body,
        mesh=mesh,
        in_specs=(tile, tile, P(), P(), P(), P(), P(), P(), tile),
        out_specs=(tile, tile, tile, P(), P(), P(), P(), P()),
        check_vma=False,
    )
```

```python
import types

import jax
import jax.numpy as jnp
from jax import lax
from jax.experimental import pallas as pl
from jax.experimental.pallas import tpu as pltpu
from jax.sharding import PartitionSpec as P

MESH = pl.DeviceIdType.MESH
C = 256
TR = 16
TC = 128
CH = 144
NROW = 16
NCOL = 8
PIXELS = 262144.0
F32 = jnp.float32
BF16 = jnp.bfloat16
VMEM_LIMIT = 58 * 1024 * 1024
NT = (((1,), (1,)), ((), ()))


def vspec():
    return pl.BlockSpec(memory_space=pltpu.VMEM)


def sspec():
    return pl.BlockSpec(memory_space=pltpu.SMEM)


def sds(shape, dtype):
    return jax.ShapeDtypeStruct(shape, dtype)


def anyspec():
    return pl.BlockSpec(memory_space=pl.ANY)


def call(kernel, ins, outs, scratch, collective_id):
    names = list(ins) + list(outs) + list(scratch)

    def named(*refs):
        kernel(types.SimpleNamespace(**dict(zip(names, refs))))

    results = pl.pallas_call(
        named,
        out_shape=[shape for shape, _ in outs.values()],
        in_specs=[spec for _, spec in ins.values()],
        out_specs=[spec for _, spec in outs.values()],
        scratch_shapes=list(scratch.values()),
        compiler_params=pltpu.CompilerParams(
            vmem_limit_bytes=VMEM_LIMIT, collective_id=collective_id, has_side_effects=True
        ),
    )(*[array for array, _ in ins.values()])
    return types.SimpleNamespace(**dict(zip(outs, results)))


def tiles(*n):
    return pltpu.VMEM(n + (C, TC), BF16)


def dma(n):
    return pltpu.SemaphoreType.DMA((n,))


def numbered(sems, rsems):
    count = [0]

    def new(src, dst, step=None, device=None):
        k = count[0]
        count[0] += 1
        return pltpu.make_async_remote_copy(
            src_ref=src,
            dst_ref=dst,
            send_sem=sems.at[k],
            recv_sem=rsems.at[k],
            device_id=device_at(*step) if device is None else device,
            device_id_type=MESH,
        )

    return new


def rl(value, shift, axis):
    shift %= value.shape[axis]
    return value if shift == 0 else pltpu.roll(value, shift, axis)


def lane_of(shape):
    return lax.broadcasted_iota(jnp.int32, shape, 1)


def dot(a, b):
    return jnp.dot(a, b, preferred_element_type=F32)


def dot_nt(a, b):
    return lax.dot_general(a, b, NT, preferred_element_type=F32)


def pack_cols(row, cols, count=TR):
    total = None
    for y in range(count):
        value = row(y)
        lane = lane_of(value.shape)
        if total is None:
            total = jnp.zeros(value.shape, F32)
        for col, base in cols:
            total = jnp.where(lane == base + y, rl(value, base + y - col, 1), total)
    return total


TWO = [(0, 0), (1, 32), (126, 64), (127, 96)]


def two_cols(first_lane):
    return [(0, first_lane), (127, 64 + first_lane)]


def put_col(total, value, cols, k):
    lane = lane_of(value.shape)
    for col, base in cols:
        total = jnp.where(lane == base + k, rl(value, base + k - col, 1), total)
    return total


def other_side(left, right):
    lane = lane_of(left.shape)
    col = lax.axis_index("col")
    both = jnp.where(lane >= 64, jnp.where(col > 0, left, 0.0), jnp.where(col < NCOL - 1, right, 0.0))
    return rl(both, 64, 1)


def three_tiles(left, own, right):
    low = lane_of(own.shape) < 64
    return [
        jnp.where(low, rl(left, -64, 1), rl(own, -32, 1)),
        jnp.where(low, rl(left, -96, 1), rl(right, 64, 1)),
        jnp.where(low, own, rl(right, 32, 1)),
    ]


def device_at(drow, dcol):
    row = lax.rem(lax.axis_index("row") + drow + NROW, NROW)
    col = lax.rem(lax.axis_index("col") + dcol + NCOL, NCOL)
    return (row, col)


def greet(steps):
    both = sorted(set(steps) | {(-a, -b) for a, b in steps})
    barrier = pltpu.get_barrier_semaphore()
    for step in both:
        pl.semaphore_signal(barrier, inc=1, device_id=device_at(*step), device_id_type=MESH)
    return lambda: pl.semaphore_wait(barrier, len(both))


def start_all(copies):
    for copy in copies:
        copy.start()


def wait_all(copies):
    for copy in copies:
        copy.wait()


def strided(wide, y, channels):
    return wide[pl.ds(y, channels, stride=TR), :]


def build_x3(x3, row, halo, count, channels, first_lane=0):
    for k in range(count):
        value = row(k)
        lane = lane_of(value.shape)
        at = slice(k * TC, (k + 1) * TC)
        left = jnp.where(lane == 0, rl(halo, -(first_lane + k), 1), rl(value, 1, 1))
        right = jnp.where(lane == TC - 1, rl(halo, TC - 1 - (64 + first_lane + k), 1), rl(value, -1, 1))
        x3[0:channels, at] = left.astype(BF16)
        x3[channels : 2 * channels, at] = value.astype(BF16)
        x3[2 * channels : 3 * channels, at] = right.astype(BF16)


def conv_chunk(w_ref, x3, start, width):
    total = None
    depth = x3.shape[0]
    for a in range(3):
        term = dot(w_ref[:, a * depth : (a + 1) * depth], x3[:, start + a * TC : start + a * TC + width])
        total = term if total is None else total + term
    return total


def offset_of(off, part, row, col):
    return off[part * NROW * NCOL + row * NCOL + col]


PARTS = 4
WIDE = C // PARTS


def part_of(q):
    return pl.ds(q * WIDE, WIDE)


def forward_kernel(r):
    row = lax.axis_index("row")
    col = lax.axis_index("col")
    first = row == 0
    last = row == NROW - 1
    arrived = greet([(1, 0), (0, 1), (0, 2)])
    new = numbered(r.sems, r.rsems)
    wide, wide2, cwide = r.wide, r.wide2, r.cwide

    wide[...] = r.summer[...].astype(F32)
    for k in range(5):
        r.ss[k] = strided(wide, 11 + k, C).astype(BF16)
        r.ss[5 + k] = strided(wide, k, C).astype(BF16)
    arrived()
    stage = [
        new(r.ss.at[pl.ds(0, 5)], r.rs.at[pl.ds(0, 5)], (1, 0)),
        new(r.ss.at[pl.ds(5, 5)], r.rs.at[pl.ds(5, 5)], (-1, 0)),
    ]
    start_all(stage)
    pack_s = pack_cols(lambda y: strided(wide, y, C), two_cols(5))
    wide2[...] = r.winter[...].astype(F32)
    r.sw[0] = strided(wide2, TR - 1, C).astype(BF16)
    r.sw[1] = strided(wide2, 0, C).astype(BF16)
    cwide[...] = r.cot[...].astype(F32)
    for k in range(2):
        r.sc[k] = strided(cwide, 14 + k, 32).astype(BF16)
        r.sc[2 + k] = strided(cwide, k, 32).astype(BF16)
    pack_w = pack_cols(lambda y: strided(wide2, y, C), two_cols(1))
    wait_all(stage)
    other = [
        new(r.sw.at[pl.ds(0, 1)], r.rw.at[pl.ds(0, 1)], (1, 0)),
        new(r.sw.at[pl.ds(1, 1)], r.rw.at[pl.ds(1, 1)], (-1, 0)),
        new(r.sc.at[pl.ds(0, 2)], r.rc.at[pl.ds(0, 2)], (1, 0)),
        new(r.sc.at[pl.ds(2, 2)], r.rc.at[pl.ds(2, 2)], (-1, 0)),
    ]
    start_all(other)
    for k in range(10):
        value = jnp.where(first if k < 5 else last, 0.0, r.rs[k].astype(F32))
        pack_s = put_col(pack_s, value, two_cols(0), k if k < 5 else 16 + k)
    r.ks[...] = pack_s.astype(BF16)
    stage = [new(r.ks, r.is_.at[0], (0, 1)), new(r.ks, r.is_.at[1], (0, -1))]
    start_all(stage)
    pack_c = pack_cols(lambda y: strided(cwide, y, 32), [(c, b + 2) for c, b in TWO])
    wait_all(other)
    for k in range(2):
        value = jnp.where(first if k < 1 else last, 0.0, r.rw[k].astype(F32))
        r.sw2[k] = value.astype(BF16)
        pack_w = put_col(pack_w, value, two_cols(0), 17 * k)
    r.kw[...] = pack_w.astype(BF16)
    for k in range(4):
        value = jnp.where(first if k < 2 else last, 0.0, r.rc[k].astype(F32))
        r.crows[k] = value.astype(BF16)
        pack_c = put_col(pack_c, value, TWO, k if k < 2 else 16 + k)
    r.kc[...] = pack_c.astype(BF16)
    other = [
        new(r.kw, r.iw.at[0], (0, 1)),
        new(r.kw, r.iw.at[1], (0, -1)),
        new(r.kc, r.ic.at[0], (0, 1)),
        new(r.kc, r.ic.at[1], (0, -1)),
    ]
    start_all(other)
    wait_all(stage)

    def summer_row(j):
        if j < 5:
            return jnp.where(first, 0.0, r.rs[j].astype(F32))
        if j >= 21:
            return jnp.where(last, 0.0, r.rs[j - 16].astype(F32))
        return strided(wide, j - 5, C)

    halo = other_side(r.is_[0].astype(F32), r.is_[1].astype(F32))
    build_x3(r.x3s, summer_row, halo, TR + 10, C)
    save_s = pltpu.make_async_copy(r.x3s, r.xs, r.lsem.at[PARTS])
    save_s.start()
    packs = [jnp.zeros((C, TC), F32), jnp.zeros((C, TC), F32)]
    lane = lane_of((C, TC))
    fp = r.fp
    for n in range(6):
        value = conv_chunk(r.weight, r.x3s, n * 512, 512)
        for j in range(4):
            k = n * 4 + j
            part = value[:, j * TC : (j + 1) * TC]
            if k < 4:
                part = jnp.where(first, 0.0, part)
            if k >= 20:
                part = jnp.where(last, 0.0, part)
            fp[k] = part.astype(BF16)
            for p, at in ((0, k), (1, k - 8)):
                if 0 <= at < 16:
                    low = (lane >= at * 8) & (lane < at * 8 + 4)
                    high = (lane >= at * 8 + 4) & (lane < at * 8 + 8)
                    packs[p] = jnp.where(low, rl(part, at * 8, 1), packs[p])
                    packs[p] = jnp.where(high, rl(part, at * 8 + 4 - 124, 1), packs[p])
    fp[24] = packs[0].astype(BF16)
    fp[25] = packs[1].astype(BF16)

    strips = [getattr(r, f"strip{q}") for q in range(PARTS)]
    trios = [getattr(r, f"trio{q}") for q in range(PARTS)]
    pin, cand, psend, ptrio, send_buf = r.pin, r.cand, r.psend, r.ptrio, r.send_buf
    owns = [
        pltpu.make_async_copy(fp.at[pl.ds(0, 24), part_of(q)], strips[q].at[pl.ds(16, 24)], r.lsem.at[q])
        for q in range(PARTS)
    ]
    pstage = [new(fp.at[24], pin.at[0], (1, 0)), new(fp.at[25], pin.at[1], (-1, 0))]
    start_all(pstage)
    stages = []
    for q in range(PARTS):
        cs = part_of(q)
        stages.append(
            [
                new(fp.at[pl.ds(0, 16), cs], strips[q].at[pl.ds(0, 16)], (1, 0)),
                new(fp.at[pl.ds(8, 16), cs], strips[q].at[pl.ds(40, 16)], (-1, 0)),
            ]
        )
    start_all(stages[0])
    start_all(stages[1])
    start_all(owns)
    wait_all(other)
    whalo = other_side(r.iw[0].astype(F32), r.iw[1].astype(F32))
    left = jnp.where(col > 0, r.ic[0].astype(F32), 0.0)
    right = jnp.where(col < NCOL - 1, r.ic[1].astype(F32), 0.0)
    for k, tile in enumerate(three_tiles(left, r.kc[...].astype(F32), right)):
        r.ct[k] = tile.astype(BF16)

    def winter_row(j):
        if j == 0 or j == TR + 1:
            return r.sw2[j // (TR + 1)].astype(F32)
        return strided(wide2, j - 1, C)

    build_x3(r.x3w, winter_row, whalo, TR + 2, C)
    save_w = pltpu.make_async_copy(r.x3w, r.xw, r.lsem.at[PARTS + 1])
    save_w.start()
    wait_all(owns)
    off = r.off

    def pick_of(dcol):
        return offset_of(off, 0, row, lax.rem(col + dcol + NCOL, NCOL)) + 1

    wait_all(pstage)
    low = lane < 64
    p0, p1 = fp[24].astype(F32), fp[25].astype(F32)
    above, below = pin[0].astype(F32), pin[1].astype(F32)
    cand[0, 0] = above.astype(BF16)
    cand[0, 1] = jnp.where(low, p0, 0.0).astype(BF16)
    cand[1, 0] = p0.astype(BF16)
    cand[1, 1] = jnp.where(low, rl(p1, 64, 1), 0.0).astype(BF16)
    cand[2, 0] = rl(jnp.where(low, below, p1), 64, 1).astype(BF16)
    cand[2, 1] = jnp.where(low, rl(below, 64, 1), 0.0).astype(BF16)
    second = []
    for k, dcol in enumerate((-2, -1, 1, 2)):
        pick = pick_of(dcol)
        for j in range(2):
            psend[k, j] = cand[pick, j]
        second.append(new(psend.at[k], ptrio.at[2 - dcol], (0, dcol)))
    start_all(second)
    mine = pick_of(0)
    for j in range(2):
        ptrio[2, j] = cand[mine, j]
    picks = [pick_of(-1), pick_of(1)]
    my_row = row + offset_of(off, 0, row, col)
    my_col = col + offset_of(off, 1, row, col)
    dcol = my_col - col + 1
    thirds = []
    for q in range(PARTS):
        cs = part_of(q)
        wait_all(stages[q])
        if q + 2 < PARTS:
            start_all(stages[q + 2])

        def fill(j, carry, cs=cs, q=q):
            send_buf[0, j, cs] = strips[q][16 * picks[0] + j]
            send_buf[1, j, cs] = strips[q][16 * picks[1] + j]
            return carry

        lax.fori_loop(0, 24, fill, 0)
        third = [
            new(send_buf.at[0, :, cs], trios[q].at[2], (0, -1)),
            new(send_buf.at[1, :, cs], trios[q].at[0], (0, 1)),
        ]
        start_all(third)
        thirds.append(third)

        def keep(j, carry, q=q):
            trios[q][1, j] = strips[q][16 * mine + j]
            return carry

        lax.fori_loop(0, 24, keep, 0)
        for n in range(q * 4 // PARTS, (q + 1) * 4 // PARTS):
            at = slice(n * 512, (n + 1) * 512)
            r.fw[:, at] = conv_chunk(r.weight, r.x3w, n * 512, 512).astype(BF16)
    wait_all(second)
    m = r.m
    low = lax.rem(lane, 8) < 4
    for j in range(2):
        right = jnp.where(my_col == NCOL - 1, 0.0, ptrio[dcol + 2, j].astype(F32))
        left = jnp.where(my_col == 0, 0.0, ptrio[dcol, j].astype(F32))
        m[:, (24 + j) * TC : (25 + j) * TC] = jnp.where(low, right, left).astype(BF16)
    for q in range(PARTS):
        wait_all(thirds[q])
        cs = part_of(q)
        for j in range(24):
            m[cs, j * TC : (j + 1) * TC] = trios[q][dcol, j]
    correlate(r.fw, m, r.cv, r.cvpack, r.sums, r.mt, r.rt, r.grim, r.s1, r.s2)
    save_s.wait()
    save_w.wait()


def forward(offsets, summer, winter, cot, weight):
    one = lambda c: pltpu.VMEM((c, TC), BF16)
    some = lambda n, c: pltpu.VMEM((n, c, TC), BF16)
    n = 16 + 6 + 4 * PARTS
    scratch = dict(
        wide=pltpu.VMEM((C * TR, TC), F32), wide2=pltpu.VMEM((C * TR, TC), F32), cwide=pltpu.VMEM((32 * TR, TC), F32),
        ss=tiles(10), rs=tiles(10), sw=tiles(2), sw2=tiles(2), rw=tiles(2), sc=some(4, 32), rc=some(4, 32),
        ks=tiles(), kw=tiles(), kc=one(32), is_=tiles(2), iw=tiles(2), ic=some(2, 32),
        x3s=pltpu.VMEM((3 * C, 26 * TC), BF16), x3w=pltpu.VMEM((3 * C, 18 * TC), BF16), fp=tiles(26),
        pin=tiles(2), cand=tiles(3, 2), send_buf=tiles(2, 24), ptrio=tiles(5, 2), psend=tiles(4, 2),
        mt=pltpu.VMEM((24 * TC, C), BF16), rt=pltpu.VMEM((2 * TC, C), BF16), grim=pltpu.VMEM((2 * TC, TR * TC), F32),
        s1=pltpu.VMEM((CH, TC), F32), s2=pltpu.VMEM((CH, TC), F32),
        lsem=dma(PARTS + 2), sems=dma(n), rsems=dma(n),
    )
    for q in range(PARTS):
        scratch[f"strip{q}"] = pltpu.VMEM((56, WIDE, TC), BF16)
        scratch[f"trio{q}"] = pltpu.VMEM((3, 24, WIDE, TC), BF16)
    return call(
        forward_kernel,
        dict(
            off=(offsets, sspec()), summer=(summer, vspec()), winter=(winter, vspec()), cot=(cot, vspec()),
            weight=(weight, vspec()),
        ),
        dict(
            crows=(sds((4, 32, TC), BF16), vspec()), ct=(sds((3, 32, TC), BF16), vspec()),
            xs=(sds((3 * C, 26 * TC), BF16), anyspec()), xw=(sds((3 * C, 18 * TC), BF16), anyspec()),
            fw=(sds((C, TR * TC), BF16), vspec()), m=(sds((C, 26 * TC), BF16), vspec()),
            cv=(sds((TR, CH, TC), F32), vspec()), cvpack=(sds((CH, TC), F32), vspec()),
            sums=(sds((8, 256), F32), vspec()),
        ),
        scratch,
        0,
    )


def bit_off(lane, bit):
    return (lane & bit) == 0


def shear(main, rim):
    low = lane_of((80, TC)) < 64
    w = jnp.where(low, jnp.concatenate([rim, main[0:72]], 0), jnp.concatenate([main[56:128], rim], 0))
    w = jnp.where(bit_off(lane_of((48, TC)), 32), w[0:48], w[32:80])
    w = jnp.where(bit_off(lane_of((32, TC)), 16), w[0:32], w[16:48])
    w = jnp.where(bit_off(lane_of((24, TC)), 8), w[0:24], w[8:32])
    lane = lane_of((16, TC))
    w = jnp.where(bit_off(lane, 4), rl(w, -4, 0)[0:16], w[8:24])
    w = jnp.where(bit_off(lane, 2), w, rl(w, -2, 0))
    w = jnp.where(bit_off(lane, 1), w, rl(w, -1, 0))
    return jnp.where(lax.broadcasted_iota(jnp.int32, (16, TC), 0) < 9, w, 0.0)


def unshear(value):
    lane = lane_of((16, TC))
    w = jnp.where(bit_off(lane, 1), value, rl(value, 1, 0))
    w = jnp.where(bit_off(lane, 2), w, rl(w, 2, 0))
    zeros = lambda n: jnp.zeros((n, TC), F32)
    padded = jnp.concatenate([w, zeros(8)], 0)
    w = jnp.where(bit_off(lane_of((24, TC)), 4), rl(padded, 4, 0), jnp.concatenate([zeros(8), w], 0))
    for n, bit in ((24, 8), (32, 16), (48, 32)):
        w = jnp.where(
            bit_off(lane_of((n + bit, TC)), bit),
            jnp.concatenate([w, zeros(bit)], 0),
            jnp.concatenate([zeros(bit), w], 0),
        )
    low = lambda n: lane_of((n, TC)) < 64
    main = jnp.concatenate(
        [
            jnp.where(low(56), w[8:64], 0.0),
            jnp.where(low(16), w[64:80], w[0:16]),
            jnp.where(low(56), 0.0, w[16:72]),
        ],
        0,
    )
    return main, jnp.where(low(8), w[0:8], w[72:80])


def row_sums(first, second):
    ones = jnp.ones((8, TC), F32)
    a = lax.dot_general(ones, first, NT, precision=lax.Precision.HIGHEST, preferred_element_type=F32)
    b = lax.dot_general(ones, second, NT, precision=lax.Precision.HIGHEST, preferred_element_type=F32)
    return jnp.where(lax.broadcasted_iota(jnp.int32, a.shape, 0) == 0, a, b)


def correlate(fw, m, cv, pack, sums, mt, rt, grim, s1, s2):
    for r in range(24):
        mt[r * TC : (r + 1) * TC, :] = m[:, r * TC : (r + 1) * TC].T
    for q in range(2):
        rt[q * TC : (q + 1) * TC, :] = m[:, (24 + q) * TC : (25 + q) * TC].T
    for n in range(4):
        grim[:, n * 512 : (n + 1) * 512] = dot(rt[...], fw[:, n * 512 : (n + 1) * 512])
    s1[...] = jnp.zeros_like(s1)
    s2[...] = jnp.zeros_like(s2)

    def at_row(y, carry):
        lanes = pl.ds(pl.multiple_of(y * TC, TC), TC)
        feat = fw[:, lanes]
        for a in range(9):
            main = dot(mt[pl.ds(pl.multiple_of((y + a) * TC, TC), TC), :], feat)
            rim = grim[pl.ds(pl.multiple_of((y + a) * 8, 8), 8), lanes]
            value = shear(main, rim) * 0.0625
            rows = slice(a * 16, (a + 1) * 16)
            cv[y, rows, :] = value
            s1[rows, :] += value
            s2[rows, :] += value * value
        return carry

    lax.fori_loop(0, TR, at_row, 0)
    pack[...] = pack_cols(lambda y: cv[y], [(c, b + 2) for c, b in TWO])
    sums[...] = jnp.zeros_like(sums)
    sums[:, 0:CH] = row_sums(s1[...], s2[...])


def reduce_one(src, dst, out, send, recv, axis, count):
    copies = []
    for d in range(1, count):
        step = (0, d) if axis == "col" else (d, 0)
        copies.append(
            pltpu.make_async_remote_copy(
                src_ref=src,
                dst_ref=dst.at[d],
                send_sem=send.at[d],
                recv_sem=recv.at[d],
                device_id=device_at(*step),
                device_id_type=MESH,
            )
        )
    start_all(copies)
    dst[0] = src[...]
    wait_all(copies)
    me = lax.axis_index(axis)
    total = None
    for d in range(count):
        value = dst[lax.rem(me - d + count, count)]
        total = value if total is None else total + value
    out[...] = total


RING = [(0, d) for d in range(1, NCOL)] + [(d, 0) for d in range(1, NROW)]


def tile_inside(b, shape):
    lane = lane_of(shape)
    row = lax.axis_index("row")
    col = lax.axis_index("col")
    local = jnp.where(lane < 64, lane, lane - 64)
    y = row * TR - 2 + local
    x = jnp.where(lane < 64, col * TC - 1 + b, col * TC + TC + b)
    return (y >= 0) & (y < NROW * TR) & (x >= 0) & (x < NCOL * TC) & (local < 20)


def rim_patches(tiles, a):
    return jnp.concatenate([rl(t, -a, 1) for t in tiles], 0).astype(BF16)


def silu_parts(value):
    sigma = jax.nn.sigmoid(value)
    return value * sigma, sigma * (1.0 + value * (1.0 - sigma))


def columns(sums):
    turned = sums.T
    return turned[0:CH, 0:1], turned[0:CH, 1:2]


def refine(r, scale, bias, inv, mid):
    row = lax.axis_index("row")
    first = row == 0
    last = row == NROW - 1
    cv, vrows, own_pack, sides, cot, crows, ct = r.cv, r.vrows, r.own_pack, r.sides, r.cot, r.crows, r.ct
    w1, w1f, w2, w2f = r.w1, r.w1f, r.w2, r.w2f
    refined, gpre, gfirst, gsecond, sums = r.refined, r.gpre, r.gfirst, r.gsecond, r.gsums0
    cwide, n3x, c3x, h3, gh3, hpre, gmain = r.cwide, r.n3x, r.c3x, r.h3, r.gh3, r.hpre, r.gmain
    s1, s2, rwide = r.s1, r.s2, r.rwide

    def normed_of(value):
        return silu_parts(value * scale + bias)[0]

    ntiles = [
        jnp.where(tile_inside(b - 1, (CH, TC)), normed_of(t), 0.0) for b, t in enumerate(three_tiles(sides[0], own_pack[...], sides[1]))
    ]

    def nrow(k):
        if k < 2:
            return jnp.where(first, 0.0, normed_of(vrows[k]))
        if k >= 18:
            return jnp.where(last, 0.0, normed_of(vrows[k - 16]))
        return normed_of(cv[k - 2])

    build_x3(n3x, nrow, ntiles[1], 20, CH)
    ctiles = [ct[k].astype(F32) for k in range(3)]
    cwide[...] = cot[...].astype(F32)

    def crow(k):
        if k < 2:
            return crows[k].astype(F32)
        if k >= 18:
            return crows[k - 16].astype(F32)
        return strided(cwide, k - 2, 32)

    build_x3(c3x, crow, ctiles[1], 20, 32)

    def both(w_ref, x3, tiles):
        depth = x3.shape[0]
        rim = None
        for a in range(3):
            term = dot(w_ref[:, a * depth : (a + 1) * depth], rim_patches(tiles, a))
            rim = term if rim is None else rim + term
        return rim

    lane = lane_of((64, TC))
    local = jnp.where(lane < 64, lane, lane - 64)
    ypos = row * TR - 1 + local
    col = lax.axis_index("col")
    xpos = jnp.where(lane < 64, col * TC - 1, col * TC + TC)
    rim_in = (ypos >= 0) & (ypos < NROW * TR) & (local < 18) & (xpos >= 0) & (xpos < NCOL * TC)
    rim_h, rim_slope = silu_parts(both(w1, n3x, ntiles))
    rim_g = both(w2f, c3x, ctiles)
    rim_h = jnp.where(rim_in, rim_h, 0.0)
    rim_g = jnp.where(rim_in, rim_g * rim_slope, 0.0)
    for n in range(6):
        hpre[:, n * 384 : (n + 1) * 384] = conv_chunk(w1, n3x, n * 384, 384)
        gmain[:, n * 384 : (n + 1) * 384] = conv_chunk(w2f, c3x, n * 384, 384)

    def edge(k):
        return first if k == 0 else (last if k == 17 else None)

    def hrow(k):
        value, slope = silu_parts(hpre[:, k * TC : (k + 1) * TC])
        grad = gmain[:, k * TC : (k + 1) * TC] * slope
        gone = edge(k)
        if gone is not None:
            value = jnp.where(gone, 0.0, value)
            grad = jnp.where(gone, 0.0, grad)
        gmain[:, k * TC : (k + 1) * TC] = grad
        return value

    build_x3(h3, hrow, rim_h, 18, 64)
    build_x3(gh3, lambda k: gmain[:, k * TC : (k + 1) * TC], rim_g, 18, 64)
    for n in range(4):
        value = conv_chunk(w2, h3, n * 512, 512)
        for j in range(4):
            rwide[pl.ds(n * 4 + j, 32, stride=TR), :] = value[:, j * TC : (j + 1) * TC]
    refined[...] = rwide[...].astype(BF16)
    own = slice(TC, 17 * TC)
    mine = slice(2 * TC, 18 * TC)
    gfirst[:, 9 * CH :] = jnp.zeros((64, 1408 - 9 * CH), F32)
    gsecond[:, 576:] = jnp.zeros((32, 64), F32)
    for a in range(3):
        gsecond[:, a * 192 : (a + 1) * 192] = dot_nt(c3x[32:64, mine], h3[:, a * TC : (a + 16) * TC])
        gfirst[:, a * 432 : (a + 1) * 432] = dot_nt(gh3[64:128, own], n3x[:, (a + 1) * TC : (a + 17) * TC])
    s1[...] = jnp.zeros_like(s1)
    s2[...] = jnp.zeros_like(s2)
    for n in range(4):
        value = conv_chunk(w1f, gh3, n * 512, 512)
        for j in range(4):
            y = n * 4 + j
            volume = cv[y]
            grad = value[:, j * TC : (j + 1) * TC] * silu_parts(volume * scale + bias)[1]
            gpre[y] = grad
            s1[...] += grad
            s2[...] += grad * (volume * inv - mid)
    sums[...] = jnp.zeros_like(sums)
    sums[:, 0:CH] = row_sums(s1[...], s2[...])


def correlate_back(cv, gpre, coef, fw, m, gfw, gm, kw, q, qrim):
    def at_row(y, carry):
        lanes = pl.ds(pl.multiple_of(y * TC, TC), TC)
        grad = coef[0] * gpre[y] + coef[1] + coef[2] * cv[y]
        grad = grad.astype(BF16).astype(F32)
        for a in range(9):
            main, rim = unshear(grad[a * 16 : (a + 1) * 16])
            q[pl.ds(pl.multiple_of((y + a) * TC, TC), TC), lanes] = main.astype(BF16)
            qrim[pl.ds(pl.multiple_of((y + a) * 8, 8), 8), lanes] = rim
        return carry

    qrim[...] = jnp.zeros_like(qrim)
    lax.fori_loop(0, TR, at_row, 0)
    for y in range(TR):
        at = slice(y * TC, (y + 1) * TC)
        value = dot(m[:, y * TC : (y + 9) * TC], q[y * TC : (y + 9) * TC, at])
        value = value + dot(m[:, 24 * TC : 26 * TC], qrim[:, at].astype(BF16))
        gfw[:, at] = (value * 0.0625).astype(BF16)
    for r in range(24):
        at = slice(max(0, r - 8) * TC, (min(15, r) + 1) * TC)
        value = dot_nt(fw[:, at], q[r * TC : (r + 1) * TC, at])
        gm[r] = (value * 0.0625).astype(BF16)
    kw[...] = pack_cols(lambda y: gfw[:, y * TC : (y + 1) * TC].astype(F32), two_cols(1)).astype(BF16)
    for k in range(2):
        value = dot_nt(fw[...], qrim[k * TC : (k + 1) * TC, :].astype(BF16))
        gm[24 + k] = (value * 0.0625).astype(BF16)


def middle_kernel(r):
    arrived = greet(RING)
    new = numbered(r.sems, r.rsems)
    arrived()
    rows = [
        new(r.cv.at[pl.ds(14, 2)], r.vrows.at[pl.ds(0, 2)], (1, 0)),
        new(r.cv.at[pl.ds(0, 2)], r.vrows.at[pl.ds(2, 2)], (-1, 0)),
    ]
    start_all(rows)
    reduce_one(r.sums, r.gcol, r.total, r.csend, r.crecv, "col", NCOL)
    wait_all(rows)
    pack = r.cvpack[...]
    for k in range(4):
        pack = put_col(pack, r.vrows[k], TWO, k if k < 2 else 16 + k)
    r.own_pack[...] = pack
    cols = [new(r.own_pack, r.sides.at[0], (0, 1)), new(r.own_pack, r.sides.at[1], (0, -1))]
    start_all(cols)
    reduce_one(r.total, r.grow, r.total2, r.rsend, r.rrecv, "row", NROW)
    wait_all(cols)
    sum1, sum2 = columns(r.total2[...])
    mean = sum1 / PIXELS
    inv = lax.rsqrt(sum2 / PIXELS - mean * mean + 1e-05)
    shape = (CH, TC)
    gain, shift = r.norm[0], r.norm[1]
    scale = gain * inv
    mid = jnp.broadcast_to(mean * inv, shape)
    inv = jnp.broadcast_to(inv, shape)
    refine(r, scale, shift - mean * scale, inv, mid)
    reduce_one(r.gsums0, r.gcol2, r.total3, r.csend2, r.crecv2, "col", NCOL)
    reduce_one(r.total3, r.grow2, r.gsums, r.rsend2, r.rrecv2, "row", NROW)
    grad_shift, grad_gain = columns(r.gsums[...])
    slope = -scale * grad_gain / PIXELS
    coef = (scale, -scale * grad_shift / PIXELS - slope * mid, slope * inv)
    correlate_back(r.cv, r.gpre, coef, r.fw, r.m, r.gfw, r.gm, r.gkw, r.q, r.qrim)


def middle(fore, cot, norm, w1, w1f, w2, w2f):
    f32 = lambda *n: pltpu.VMEM(n, F32)
    bf16 = lambda *n: pltpu.VMEM(n, BF16)
    return call(
        middle_kernel,
        {
            name: (array, vspec())
            for name, array in dict(
                cv=fore.cv, cvpack=fore.cvpack, sums=fore.sums, crows=fore.crows, ct=fore.ct, fw=fore.fw, m=fore.m,
                cot=cot, norm=norm, w1=w1, w1f=w1f, w2=w2, w2f=w2f,
            ).items()
        },
        {
            name: (sds(shape, kind), vspec())
            for name, shape, kind in (
                ("refined", (32 * TR, TC), BF16),
                ("gfirst", (64, 1408), F32),
                ("gsecond", (32, 640), F32),
                ("gsums", (8, 256), F32),
                ("gfw", (C, TR * TC), BF16),
                ("gm", (26, C, TC), BF16),
                ("gkw", (C, TC), BF16),
            )
        },
        dict(
            vrows=f32(4, CH, TC), own_pack=f32(CH, TC), sides=f32(2, CH, TC),
            gcol=f32(NCOL, 8, 256), grow=f32(NROW, 8, 256), total=f32(8, 256), total2=f32(8, 256),
            gcol2=f32(NCOL, 8, 256), grow2=f32(NROW, 8, 256), gsums0=f32(8, 256), total3=f32(8, 256),
            cwide=f32(32 * TR, TC), n3x=bf16(3 * CH, 20 * TC), c3x=bf16(96, 20 * TC), h3=bf16(192, 18 * TC),
            gh3=bf16(192, 18 * TC), hpre=f32(64, 18 * TC), gmain=f32(64, 18 * TC), s1=f32(CH, TC), s2=f32(CH, TC),
            rwide=f32(32 * TR, TC), gpre=f32(TR, CH, TC), q=bf16(24 * TC, TR * TC), qrim=f32(2 * TC, TR * TC),
            sems=dma(4), rsems=dma(4),
            csend=dma(NCOL), crecv=dma(NCOL), rsend=dma(NROW), rrecv=dma(NROW),
            csend2=dma(NCOL), crecv2=dma(NCOL), rsend2=dma(NROW), rrecv2=dma(NROW),
        ),
        1,
    )


TILES = 384
HALF = TILES // 2
SHARE = TILES // 8
LEAST = SHARE // NROW


def final_kernel(r):
    row = lax.axis_index("row")
    col = lax.axis_index("col")
    core = lax.rem(col, 2)
    chip = lax.div(col, 2)
    off, gm, gfw = r.off, r.gm, r.gfw
    trios = [getattr(r, f"trio{q}") for q in range(PARTS)]
    ptrio, strip, be, ab, pout, pin, g24, g5 = r.ptrio, r.strip, r.be, r.ab, r.pout, r.pin, r.g24, r.g5
    pab, pq, pack, side, rw, kw, iw, kw0 = r.pab, r.pq, r.pack, r.side, r.rw, r.kw, r.iw, r.gkw
    ext, wrows, buf, half_in, half, y_in = r.ext, r.wrows, r.buf, r.half_in, r.half, r.y_in
    share, row_in, full, x3, wide, flipped = r.share, r.row_in, r.full, r.x3, r.wide, r.flipped
    xw, xs = r.xw_here, r.xs_here
    arrived = greet(RING)
    loads = [
        pltpu.make_async_copy(r.xw, xw, r.lsem.at[PARTS]),
        pltpu.make_async_copy(r.xs, xs, r.lsem.at[PARTS + 1]),
    ]
    owns = [
        pltpu.make_async_copy(gm.at[pl.ds(0, 24), part_of(q)], trios[q].at[1, pl.ds(0, 24)], r.lsem.at[q])
        for q in range(PARTS)
    ]
    start_all(owns)
    start_all(loads)
    new = numbered(r.sems, r.rsems)
    arrived()
    pstage = [new(gm.at[pl.ds(24, 2)], ptrio.at[0], (0, 1)), new(gm.at[pl.ds(24, 2)], ptrio.at[2], (0, -1))]
    wstage = [
        new(gfw.at[:, pl.ds((TR - 1) * TC, TC)], rw.at[0], (1, 0)),
        new(gfw.at[:, pl.ds(0, TC)], rw.at[1], (-1, 0)),
    ]
    start_all(pstage + wstage)
    stages = []
    for q in range(PARTS):
        cs = part_of(q)
        stages.append(
            [
                new(gm.at[pl.ds(0, 24), cs], trios[q].at[0, pl.ds(0, 24)], (0, 1)),
                new(gm.at[pl.ds(0, 24), cs], trios[q].at[2, pl.ds(0, 24)], (0, -1)),
            ]
        )
    start_all(stages[0])
    start_all(stages[1])
    for q in range(PARTS):
        for k in range(3):
            trios[q][k, 24] = jnp.zeros((WIDE, TC), BF16)
    for k in range(9):
        flipped[:, k * C : (k + 1) * C] = r.weight[:, (8 - k) * C : (9 - k) * C].T
    wait_all(owns)
    sources = []
    for k in range(3):
        place = col + k - 1
        there = lax.rem(place + NCOL, NCOL)
        drow = offset_of(off, 0, row, there)
        dcol = offset_of(off, 1, row, there)
        good = (dcol == 1 - k) & (place >= 0) & (place < NCOL)
        sources.append((drow, good))

    first, last = row == 0, row == NROW - 1
    zero = jnp.zeros((C, TC), F32)
    lane = lane_of((C, TC))
    low = lane < 64

    def only(flag, ref):
        return jnp.where(flag, ref.astype(F32), 0.0)

    wait_all(pstage)
    to_above, own0, own1, to_below = zero, zero, zero, zero
    for k, (drow, good) in enumerate(sources):
        t0, t1 = (gm[24], gm[25]) if k == 1 else (ptrio[k, 0], ptrio[k, 1])
        t0, t1 = t0.astype(F32), jnp.where(low, t1.astype(F32), 0.0)
        up, level, down = (good & (drow == v) for v in (-1, 0, 1))
        turned0, turned1 = rl(t0, 64, 1), rl(t1, 64, 1)
        to_above += jnp.where(up, t0, 0.0)
        own0 += jnp.where(up, t1, 0.0) + jnp.where(level, t0, 0.0)
        own1 += jnp.where(level, turned1, 0.0) + jnp.where(down & jnp.logical_not(low), turned0, 0.0)
        to_below += jnp.where(down, turned1 + jnp.where(low, turned0, 0.0), 0.0)
    pout[0] = to_above.astype(BF16)
    pout[1] = to_below.astype(BF16)
    pstage = [new(pout.at[0], pin.at[0], (-1, 0)), new(pout.at[1], pin.at[1], (1, 0))]
    start_all(pstage)

    wait_all(wstage)
    kpack = kw0[...].astype(F32)
    for k in range(2):
        value = only(jnp.logical_not(first if k == 0 else last), rw[k])
        wrows[k] = value.astype(BF16)
        kpack = put_col(kpack, value, two_cols(0), 17 * k)
    kw[...] = kpack.astype(BF16)
    wstage = [new(kw, iw.at[0], (0, 1)), new(kw, iw.at[1], (0, -1))]
    start_all(wstage)

    thirds = []
    for q in range(PARTS):
        cs = part_of(q)
        wait_all(stages[q])
        if q + 2 < PARTS:
            start_all(stages[q + 2])

        def gather(p, carry, cs=cs, q=q):
            total = None
            for k, (drow, good) in enumerate(sources):
                j = p - 16 * (drow + 1)
                fits = good & (j >= 0) & (j < 24)
                value = trios[q][k, jnp.where(fits, j, 24)].astype(F32)
                total = value if total is None else total + value
            strip[p, cs] = total.astype(BF16)
            return carry

        lax.fori_loop(0, 56, gather, 0)
        third = [
            new(strip.at[pl.ds(0, 16), cs], be.at[:, cs], (-1, 0)),
            new(strip.at[pl.ds(40, 16), cs], ab.at[:, cs], (1, 0)),
        ]
        start_all(third)
        thirds.append(third)
        if q == 0:
            wait_all(loads)
        if q < 3:
            for n in range(3):
                part = slice(n * C, (n + 1) * C)
                at = slice(q * 768 + n * C, q * 768 + (n + 1) * C)
                r.gfeat[:, at] = dot_nt(gfw[...], xw[part, q * TC : (q + 16) * TC])
    wait_all(wstage)
    whalo = other_side(iw[0].astype(F32), iw[1].astype(F32))
    wait_all(pstage)
    not_first, not_last = row > 0, row < NROW - 1
    p0 = own0 + only(not_last, pin[0])
    p1 = own1 + only(not_first, pin[1])
    tile_a = p0 + jnp.where(low, 0.0, rl(p1, 64, 1))
    tile_b = jnp.where(low, rl(p1, 64, 1), 0.0)
    pab[0] = tile_a.astype(BF16)
    pab[1] = tile_b.astype(BF16)
    fourth = [new(pab.at[0], pq.at[0], (-1, 0)), new(pab.at[1], pq.at[1], (1, 0))]
    start_all(fourth)

    def w_row(k):
        if k == 0 or k == TR + 1:
            return wrows[k // (TR + 1)].astype(F32)
        return gfw[:, (k - 1) * TC : k * TC].astype(F32)

    build_x3(x3, w_row, whalo, TR + 2, C)

    def last_conv(n):
        value = conv_chunk(flipped, x3, n * 512, 512)
        for j in range(4):
            wide[pl.ds(n * 4 + j, C, stride=TR), :] = value[:, j * TC : (j + 1) * TC]

    for q in range(PARTS):
        cs = part_of(q)
        wait_all(thirds[q])
        for k in range(24):
            total = strip[16 + k, cs].astype(F32)
            if k < 16:
                total = total + only(not_last, be[k, cs])
            if k >= 8:
                total = total + only(not_first, ab[k - 8, cs])
            g24[k, cs] = total.astype(BF16)
        more = [
            new(g24.at[pl.ds(0, 5), cs], g5.at[1, :, cs], (-1, 0)),
            new(g24.at[pl.ds(19, 5), cs], g5.at[0, :, cs], (1, 0)),
        ]
        start_all(more)
        fourth = fourth + more
        for n in range(q * 4 // PARTS, (q + 1) * 4 // PARTS):
            last_conv(n)
    r.out_w[...] = wide[...].astype(BF16)
    wait_all(fourth)
    tile_a = tile_a + jnp.where((lane >= 24) & (lane < 64), only(not_first, pq[1]), 0.0)
    tile_b = tile_b + jnp.where(lane < 40, only(not_last, pq[0]), 0.0)
    pack[0] = tile_a.astype(BF16)
    pack[1] = tile_b.astype(BF16)
    total = zero
    for k in range(18):
        value = g24[k + 3].astype(F32)
        if k < 5:
            value = value + only(not_first, g5[0, k])
        if k >= 13:
            value = value + only(not_last, g5[1, k - 13])
        if k == 0:
            value = only(not_first, value)
        if k == 17:
            value = only(not_last, value)
        strip[k] = value.astype(BF16)
        total = put_col(total, value, two_cols(0), k)
    pack[2] = total.astype(BF16)
    stage = [new(pack, side.at[0], (0, 1)), new(pack, side.at[1], (0, -1))]
    start_all(stage)
    source = lax.broadcasted_iota(jnp.int32, (2 * TC, TC), 0)
    target = lax.broadcasted_iota(jnp.int32, (2 * TC, TC), 1)
    take = ((target < 18) & (source == (target + 3) * 8 + 7)) | (
        (target >= 64) & (target < 82) & (source == (target - 61) * 8)
    )
    rims = dot(pack[0], take[0:TC].astype(F32).astype(BF16)) + dot(pack[1], take[TC:].astype(F32).astype(BF16))
    wait_all(stage)
    halo = other_side(side[0, 2].astype(F32), side[1, 2].astype(F32))
    halo = halo + jnp.where(low, only(col > 0, rims), only(col < NCOL - 1, rims))
    at = jnp.where(low, lane, lane - 64)
    gone = (first & (at == 0)) | (last & (at == 17))
    shalo = jnp.where(gone, 0.0, halo)
    for k in range(18):
        p, base = ((0, (k + 3) * 8) if k + 3 < 16 else (1, (k - 13) * 8))
        value = strip[k].astype(F32)
        left = rl(only(col > 0, side[0, p]), -base, 1)
        right = rl(only(col < NCOL - 1, side[1, p]), 120 - base, 1)
        extra = jnp.where(lane < 4, left, 0.0) + jnp.where(lane >= 124, right, 0.0)
        if k == 0:
            extra = only(not_first, extra)
        if k == 17:
            extra = only(not_last, extra)
        ext[:, k * TC : (k + 1) * TC] = (value + extra).astype(BF16)
    for a in range(3):
        at = slice((a + 4) * TC, (a + 20) * TC)
        for n in range(3):
            part = slice(n * C, (n + 1) * C)
            into = slice(a * 768 + n * C, a * 768 + (n + 1) * C)
            value = r.gfeat[:, into] + dot_nt(ext[:, TC : 17 * TC], xs[part, at])
            value = value.astype(BF16)
            for t in range(2):
                for g in range(16):
                    buf[(a * 6 + n * 2 + t) * 16 + g] = value[g * 16 : (g + 1) * 16, t * TC : (t + 1) * TC]
    for t in range(11):
        for g in range(4):
            buf[288 + t * 4 + g] = r.gfirst[g * 16 : (g + 1) * 16, t * TC : (t + 1) * TC].astype(BF16)
    for t in range(5):
        for g in range(2):
            buf[332 + t * 2 + g] = r.gsecond[g * 16 : (g + 1) * 16, t * TC : (t + 1) * TC].astype(BF16)
    for t in range(342, TILES):
        buf[t] = jnp.zeros((16, TC), BF16)
    partner = (row, col + 1 - 2 * core)
    pair = new(buf.at[pl.ds(HALF * (1 - core), HALF)], half_in, device=partner)
    pair.start()

    pair.wait()

    def add_half(k, carry):
        half[k] = (buf[HALF * core + k].astype(F32) + half_in[k].astype(F32)).astype(BF16)
        return carry

    lax.fori_loop(0, HALF, add_half, 0)
    chips = []
    for d in range(1, 4):
        there = lax.rem(chip + d, 4)
        chips.append(
            new(half.at[pl.ds(SHARE * there, SHARE)], y_in.at[d - 1], device=(row, 2 * there + core))
        )
    start_all(chips)
    build_x3(x3, lambda k: ext[:, k * TC : (k + 1) * TC].astype(F32), shalo, TR + 2, C)
    last_conv(0)
    last_conv(1)
    wait_all(chips)

    def add_share(k, carry):
        total = half[SHARE * chip + k].astype(F32)
        for d in range(3):
            total = total + y_in[d, k].astype(F32)
        share[k] = total.astype(BF16)
        return carry

    lax.fori_loop(0, SHARE, add_share, 0)
    rows = []
    for d in range(1, NROW):
        there = lax.rem(row + d, NROW)
        rows.append(new(share.at[pl.ds(LEAST * there, LEAST)], row_in.at[d - 1], device=(there, col)))
    start_all(rows)
    wait_all(rows)
    spot = HALF * core + SHARE * chip + LEAST * row
    for k in range(LEAST):
        total = share[LEAST * row + k].astype(F32)
        for d in range(NROW - 1):
            total = total + row_in[d, k].astype(F32)
        full[spot + k] = total.astype(BF16)
    mine = full.at[pl.ds(spot, LEAST)]
    rows = [new(mine, mine, device=(lax.rem(row + d, NROW), col)) for d in range(1, NROW)]
    start_all(rows)
    wait_all(rows)
    mine = full.at[pl.ds(HALF * core + SHARE * chip, SHARE)]
    chips = [new(mine, mine, device=(row, 2 * lax.rem(chip + d, 4) + core)) for d in range(1, 4)]
    start_all(chips)
    last_conv(2)
    last_conv(3)
    r.out_s[...] = wide[...].astype(BF16)
    wait_all(chips)
    mine = full.at[pl.ds(HALF * core, HALF)]
    pair = new(mine, mine, device=partner)
    pair.start()
    pair.wait()
    for t in range(18):
        for g in range(16):
            r.feat_out[g * 16 : (g + 1) * 16, t * TC : (t + 1) * TC] = full[t * 16 + g].astype(F32)
    for t in range(11):
        for g in range(4):
            r.first_out[g * 16 : (g + 1) * 16, t * TC : (t + 1) * TC] = full[288 + t * 4 + g].astype(F32)
    for t in range(5):
        for g in range(2):
            r.second_out[g * 16 : (g + 1) * 16, t * TC : (t + 1) * TC] = full[332 + t * 2 + g].astype(F32)


def final(offsets, fore, mid, weight):
    small = lambda *n: pltpu.VMEM(n + (16, TC), BF16)
    n = 14 + 6 * PARTS + 8 + 2 * (NROW - 1)
    scratch = dict(
        ptrio=tiles(3, 2), strip=tiles(56), be=tiles(16), ab=tiles(16), pout=tiles(2), pin=tiles(2), g24=tiles(24),
        g5=tiles(2, 5), pab=tiles(2), pq=tiles(2), pack=tiles(3), side=tiles(2, 3), rw=tiles(2), kw=tiles(), iw=tiles(2),
        wrows=tiles(2), ext=pltpu.VMEM((C, 18 * TC), BF16), flipped=pltpu.VMEM((C, 9 * C), BF16),
        gfeat=pltpu.VMEM((C, 9 * C), F32), x3=pltpu.VMEM((3 * C, 18 * TC), BF16), wide=pltpu.VMEM((C * TR, TC), F32),
        xw_here=pltpu.VMEM((3 * C, 18 * TC), BF16), xs_here=pltpu.VMEM((3 * C, 26 * TC), BF16),
        buf=small(TILES), half_in=small(HALF), half=small(HALF), y_in=small(3, SHARE), share=small(SHARE),
        row_in=small(NROW - 1, LEAST), full=small(TILES),
        lsem=dma(PARTS + 2), sems=dma(n), rsems=dma(n),
    )
    for q in range(PARTS):
        scratch[f"trio{q}"] = pltpu.VMEM((3, 25, WIDE, TC), BF16)
    return call(
        final_kernel,
        dict(
            off=(offsets, sspec()), gm=(mid.gm, vspec()), gfw=(mid.gfw, vspec()), gkw=(mid.gkw, vspec()),
            gfirst=(mid.gfirst, vspec()), gsecond=(mid.gsecond, vspec()), weight=(weight, vspec()),
            xw=(fore.xw, anyspec()), xs=(fore.xs, anyspec()),
        ),
        dict(
            out_w=(sds((C * TR, TC), BF16), vspec()), out_s=(sds((C * TR, TC), BF16), vspec()),
            feat_out=(sds((C, 9 * C), F32), vspec()), first_out=(sds((64, 1408), F32), vspec()),
            second_out=(sds((32, 640), F32), vspec()),
        ),
        scratch,
        2,
    )


def flip_weight(weight, in_channels):
    out_channels = weight.shape[0]
    return (
        weight.reshape(out_channels, 9, in_channels)[:, ::-1, :]
        .transpose(2, 1, 0)
        .reshape(in_channels, 9 * out_channels)
    )


def spread(vector):
    return jnp.pad(vector.reshape(9, 9), ((0, 0), (0, 7))).reshape(CH)


def gathered(vector):
    return vector.reshape(9, 16)[:, :9].reshape(81)


def body(winter, summer, offsets, feat_weight, bn_gain, bn_shift, w_first, w_second, cotangent):
    cot = cotangent.reshape(32 * TR, TC)
    flat = offsets.reshape(-1)
    norm = jnp.stack([jnp.broadcast_to(spread(v)[:, None], (CH, TC)) for v in (bn_gain, bn_shift)])
    w1 = jnp.pad(w_first.reshape(64, 9, 9, 9), ((0, 0), (0, 0), (0, 0), (0, 7))).reshape(64, 9 * CH)
    fore = forward(flat, summer.reshape(C * TR, TC), winter.reshape(C * TR, TC), cot, feat_weight)
    mid = middle(fore, cot, norm, w1, flip_weight(w1, CH), w_second, flip_weight(w_second, 64))
    last = final(flat, fore, mid, feat_weight)
    return (
        mid.refined.reshape(32, TR, TC),
        last.out_w.reshape(C, TR, TC),
        last.out_s.reshape(C, TR, TC),
        last.feat_out,
        last.first_out[:, : 9 * CH].reshape(64, 9, 9, 16)[:, :, :, :9].reshape(64, 729),
        last.second_out[:, :576],
        gathered(mid.gsums[1, :CH]),
        gathered(mid.gsums[0, :CH]),
    )


def solution(mesh):
    tile = P(None, "row", "col")
    return jax.shard_map(
        body,
        mesh=mesh,
        in_specs=(tile, tile, P(), P(), P(), P(), P(), P(), tile),
        out_specs=(tile, tile, tile, P(), P(), P(), P(), P()),
        check_vma=False,
    )
```

```python
import types

import jax
import jax.numpy as jnp
from jax import lax
from jax.experimental import pallas as pl
from jax.experimental.pallas import tpu as pltpu
from jax.sharding import PartitionSpec as P

MESH = pl.DeviceIdType.MESH
C = 256
TR = 16
TC = 128
CH = 144
NROW = 16
NCOL = 8
PIXELS = 262144.0
F32 = jnp.float32
BF16 = jnp.bfloat16
VMEM_LIMIT = 58 * 1024 * 1024
NT = (((1,), (1,)), ((), ()))


def vspec():
    return pl.BlockSpec(memory_space=pltpu.VMEM)


def sspec():
    return pl.BlockSpec(memory_space=pltpu.SMEM)


def sds(shape, dtype):
    return jax.ShapeDtypeStruct(shape, dtype)


def anyspec():
    return pl.BlockSpec(memory_space=pl.ANY)


def call(kernel, ins, outs, scratch, collective_id):
    names = list(ins) + list(outs) + list(scratch)

    def named(*refs):
        kernel(types.SimpleNamespace(**dict(zip(names, refs))))

    results = pl.pallas_call(
        named,
        out_shape=[shape for shape, _ in outs.values()],
        in_specs=[spec for _, spec in ins.values()],
        out_specs=[spec for _, spec in outs.values()],
        scratch_shapes=list(scratch.values()),
        compiler_params=pltpu.CompilerParams(
            vmem_limit_bytes=VMEM_LIMIT, collective_id=collective_id, has_side_effects=True
        ),
    )(*[array for array, _ in ins.values()])
    return types.SimpleNamespace(**dict(zip(outs, results)))


def tiles(*n):
    return pltpu.VMEM(n + (C, TC), BF16)


def dma(n):
    return pltpu.SemaphoreType.DMA((n,))


def numbered(sems, rsems):
    count = [0]

    def new(src, dst, step=None, device=None):
        k = count[0]
        count[0] += 1
        return pltpu.make_async_remote_copy(
            src_ref=src,
            dst_ref=dst,
            send_sem=sems.at[k],
            recv_sem=rsems.at[k],
            device_id=device_at(*step) if device is None else device,
            device_id_type=MESH,
        )

    return new


def rl(value, shift, axis):
    shift %= value.shape[axis]
    return value if shift == 0 else pltpu.roll(value, shift, axis)


def lane_of(shape):
    return lax.broadcasted_iota(jnp.int32, shape, 1)


def dot(a, b):
    return jnp.dot(a, b, preferred_element_type=F32)


def dot_nt(a, b):
    return lax.dot_general(a, b, NT, preferred_element_type=F32)


def pack_cols(row, cols, count=TR):
    total = None
    for y in range(count):
        value = row(y)
        lane = lane_of(value.shape)
        if total is None:
            total = jnp.zeros(value.shape, F32)
        for col, base in cols:
            total = jnp.where(lane == base + y, rl(value, base + y - col, 1), total)
    return total


TWO = [(0, 0), (1, 32), (126, 64), (127, 96)]


def two_cols(first_lane):
    return [(0, first_lane), (127, 64 + first_lane)]


def put_col(total, value, cols, k):
    lane = lane_of(value.shape)
    for col, base in cols:
        total = jnp.where(lane == base + k, rl(value, base + k - col, 1), total)
    return total


def other_side(left, right):
    lane = lane_of(left.shape)
    col = lax.axis_index("col")
    both = jnp.where(lane >= 64, jnp.where(col > 0, left, 0.0), jnp.where(col < NCOL - 1, right, 0.0))
    return rl(both, 64, 1)


def three_tiles(left, own, right):
    low = lane_of(own.shape) < 64
    return [
        jnp.where(low, rl(left, -64, 1), rl(own, -32, 1)),
        jnp.where(low, rl(left, -96, 1), rl(right, 64, 1)),
        jnp.where(low, own, rl(right, 32, 1)),
    ]


def device_at(drow, dcol):
    row = lax.rem(lax.axis_index("row") + drow + NROW, NROW)
    col = lax.rem(lax.axis_index("col") + dcol + NCOL, NCOL)
    return (row, col)


def greet(steps):
    both = sorted(set(steps) | {(-a, -b) for a, b in steps})
    barrier = pltpu.get_barrier_semaphore()
    for step in both:
        pl.semaphore_signal(barrier, inc=1, device_id=device_at(*step), device_id_type=MESH)
    return lambda: pl.semaphore_wait(barrier, len(both))


def start_all(copies):
    for copy in copies:
        copy.start()


def wait_all(copies):
    for copy in copies:
        copy.wait()


def strided(wide, y, channels):
    return wide[pl.ds(y, channels, stride=TR), :]


def build_x3(x3, row, halo, count, channels, first_lane=0):
    for k in range(count):
        value = row(k)
        lane = lane_of(value.shape)
        at = slice(k * TC, (k + 1) * TC)
        left = jnp.where(lane == 0, rl(halo, -(first_lane + k), 1), rl(value, 1, 1))
        right = jnp.where(lane == TC - 1, rl(halo, TC - 1 - (64 + first_lane + k), 1), rl(value, -1, 1))
        x3[0:channels, at] = left.astype(BF16)
        x3[channels : 2 * channels, at] = value.astype(BF16)
        x3[2 * channels : 3 * channels, at] = right.astype(BF16)


def conv_chunk(w_ref, x3, start, width):
    total = None
    depth = x3.shape[0]
    for a in range(3):
        term = dot(w_ref[:, a * depth : (a + 1) * depth], x3[:, start + a * TC : start + a * TC + width])
        total = term if total is None else total + term
    return total


def offset_of(off, part, row, col):
    return off[part, row, col]


PARTS = 4
WIDE = C // PARTS


def part_of(q):
    return pl.ds(q * WIDE, WIDE)


def padded_place(shape, axis):
    at = lax.broadcasted_iota(jnp.int32, shape, axis)
    tap = jnp.zeros(shape, jnp.int32)
    for t in range(1, 9):
        tap = tap + jnp.where(at >= t * CH, 1, 0)
    rest = at - tap * CH
    b = rest & 15
    return jnp.where(b < 9, tap * 81 + (rest >> 4) * 9 + b, -1)


def one_hot(mask):
    return jnp.where(mask, 1.0, 0.0).astype(BF16)


def padding_matrix():
    place = padded_place((1, 9 * CH), 1)
    return one_hot(lax.broadcasted_iota(jnp.int32, (729, 9 * CH), 0) == place)


def small_weights(r, q):
    if q == 0:
        r.w1[...] = dot(r.w_first[...], padding_matrix()).astype(BF16)
    if q == 1:
        place = padded_place((CH, 1), 0)
        source = lax.broadcasted_iota(jnp.int32, (CH, 729), 1)
        for k in range(9):
            pick = one_hot((source == place + (8 - k) * 81) & (place >= 0))
            r.w1f[:, k * 64 : (k + 1) * 64] = dot_nt(pick, r.w_first[...]).astype(BF16)
    if q == 2:
        target = lax.broadcasted_iota(jnp.int32, (64, 576), 0)
        source = lax.broadcasted_iota(jnp.int32, (64, 576), 1)
        for k in range(9):
            pick = one_hot(source == target + (8 - k) * 64)
            r.w2f[:, k * 32 : (k + 1) * 32] = dot_nt(pick, r.w_second[...]).astype(BF16)


def forward_kernel(r):
    row = lax.axis_index("row")
    col = lax.axis_index("col")
    first = row == 0
    last = row == NROW - 1
    arrived = greet([(1, 0), (0, 1), (0, 2)])
    new = numbered(r.sems, r.rsems)
    wide, wide2, cwide = r.wide, r.wide2, r.cwide

    wide[...] = r.summer[...].astype(F32)
    for k in range(5):
        r.ss[k] = strided(wide, 11 + k, C).astype(BF16)
        r.ss[5 + k] = strided(wide, k, C).astype(BF16)
    arrived()
    stage = [
        new(r.ss.at[pl.ds(0, 5)], r.rs.at[pl.ds(0, 5)], (1, 0)),
        new(r.ss.at[pl.ds(5, 5)], r.rs.at[pl.ds(5, 5)], (-1, 0)),
    ]
    start_all(stage)
    pack_s = pack_cols(lambda y: strided(wide, y, C), two_cols(5))
    wide2[...] = r.winter[...].astype(F32)
    r.sw[0] = strided(wide2, TR - 1, C).astype(BF16)
    r.sw[1] = strided(wide2, 0, C).astype(BF16)
    cwide[...] = r.cot[...].astype(F32)
    for k in range(2):
        r.sc[k] = strided(cwide, 14 + k, 32).astype(BF16)
        r.sc[2 + k] = strided(cwide, k, 32).astype(BF16)
    pack_w = pack_cols(lambda y: strided(wide2, y, C), two_cols(1))
    wait_all(stage)
    other = [
        new(r.sw.at[pl.ds(0, 1)], r.rw.at[pl.ds(0, 1)], (1, 0)),
        new(r.sw.at[pl.ds(1, 1)], r.rw.at[pl.ds(1, 1)], (-1, 0)),
        new(r.sc.at[pl.ds(0, 2)], r.rc.at[pl.ds(0, 2)], (1, 0)),
        new(r.sc.at[pl.ds(2, 2)], r.rc.at[pl.ds(2, 2)], (-1, 0)),
    ]
    start_all(other)
    for k in range(10):
        value = jnp.where(first if k < 5 else last, 0.0, r.rs[k].astype(F32))
        pack_s = put_col(pack_s, value, two_cols(0), k if k < 5 else 16 + k)
    r.ks[...] = pack_s.astype(BF16)
    stage = [new(r.ks, r.is_.at[0], (0, 1)), new(r.ks, r.is_.at[1], (0, -1))]
    start_all(stage)
    pack_c = pack_cols(lambda y: strided(cwide, y, 32), [(c, b + 2) for c, b in TWO])
    wait_all(other)
    for k in range(2):
        value = jnp.where(first if k < 1 else last, 0.0, r.rw[k].astype(F32))
        r.sw2[k] = value.astype(BF16)
        pack_w = put_col(pack_w, value, two_cols(0), 17 * k)
    r.kw[...] = pack_w.astype(BF16)
    for k in range(4):
        value = jnp.where(first if k < 2 else last, 0.0, r.rc[k].astype(F32))
        r.crows[k] = value.astype(BF16)
        pack_c = put_col(pack_c, value, TWO, k if k < 2 else 16 + k)
    r.kc[...] = pack_c.astype(BF16)
    other = [
        new(r.kw, r.iw.at[0], (0, 1)),
        new(r.kw, r.iw.at[1], (0, -1)),
        new(r.kc, r.ic.at[0], (0, 1)),
        new(r.kc, r.ic.at[1], (0, -1)),
    ]
    start_all(other)
    wait_all(stage)

    def summer_row(j):
        if j < 5:
            return jnp.where(first, 0.0, r.rs[j].astype(F32))
        if j >= 21:
            return jnp.where(last, 0.0, r.rs[j - 16].astype(F32))
        return strided(wide, j - 5, C)

    halo = other_side(r.is_[0].astype(F32), r.is_[1].astype(F32))
    build_x3(r.x3s, summer_row, halo, TR + 10, C)
    save_s = pltpu.make_async_copy(r.x3s, r.xs, r.lsem.at[PARTS])
    save_s.start()
    packs = [jnp.zeros((C, TC), F32), jnp.zeros((C, TC), F32)]
    lane = lane_of((C, TC))
    fp = r.fp
    for n in range(6):
        value = conv_chunk(r.weight, r.x3s, n * 512, 512)
        for j in range(4):
            k = n * 4 + j
            part = value[:, j * TC : (j + 1) * TC]
            if k < 4:
                part = jnp.where(first, 0.0, part)
            if k >= 20:
                part = jnp.where(last, 0.0, part)
            fp[k] = part.astype(BF16)
            for p, at in ((0, k), (1, k - 8)):
                if 0 <= at < 16:
                    low = (lane >= at * 8) & (lane < at * 8 + 4)
                    high = (lane >= at * 8 + 4) & (lane < at * 8 + 8)
                    packs[p] = jnp.where(low, rl(part, at * 8, 1), packs[p])
                    packs[p] = jnp.where(high, rl(part, at * 8 + 4 - 124, 1), packs[p])
    fp[24] = packs[0].astype(BF16)
    fp[25] = packs[1].astype(BF16)

    strips = [getattr(r, f"strip{q}") for q in range(PARTS)]
    trios = [getattr(r, f"trio{q}") for q in range(PARTS)]
    pin, cand, psend, ptrio, send_buf = r.pin, r.cand, r.psend, r.ptrio, r.send_buf
    owns = [
        pltpu.make_async_copy(fp.at[pl.ds(0, 24), part_of(q)], strips[q].at[pl.ds(16, 24)], r.lsem.at[q])
        for q in range(PARTS)
    ]
    pstage = [new(fp.at[24], pin.at[0], (1, 0)), new(fp.at[25], pin.at[1], (-1, 0))]
    start_all(pstage)
    stages = []
    for q in range(PARTS):
        cs = part_of(q)
        stages.append(
            [
                new(fp.at[pl.ds(0, 16), cs], strips[q].at[pl.ds(0, 16)], (1, 0)),
                new(fp.at[pl.ds(8, 16), cs], strips[q].at[pl.ds(40, 16)], (-1, 0)),
            ]
        )
    start_all(stages[0])
    start_all(stages[1])
    start_all(owns)
    wait_all(other)
    whalo = other_side(r.iw[0].astype(F32), r.iw[1].astype(F32))
    left = jnp.where(col > 0, r.ic[0].astype(F32), 0.0)
    right = jnp.where(col < NCOL - 1, r.ic[1].astype(F32), 0.0)
    for k, tile in enumerate(three_tiles(left, r.kc[...].astype(F32), right)):
        r.ct[k] = tile.astype(BF16)

    def winter_row(j):
        if j == 0 or j == TR + 1:
            return r.sw2[j // (TR + 1)].astype(F32)
        return strided(wide2, j - 1, C)

    build_x3(r.x3w, winter_row, whalo, TR + 2, C)
    save_w = pltpu.make_async_copy(r.x3w, r.xw, r.lsem.at[PARTS + 1])
    save_w.start()
    wait_all(owns)
    off = r.off

    def pick_of(dcol):
        return offset_of(off, 0, row, lax.rem(col + dcol + NCOL, NCOL)) + 1

    wait_all(pstage)
    low = lane < 64
    p0, p1 = fp[24].astype(F32), fp[25].astype(F32)
    above, below = pin[0].astype(F32), pin[1].astype(F32)
    cand[0, 0] = above.astype(BF16)
    cand[0, 1] = jnp.where(low, p0, 0.0).astype(BF16)
    cand[1, 0] = p0.astype(BF16)
    cand[1, 1] = jnp.where(low, rl(p1, 64, 1), 0.0).astype(BF16)
    cand[2, 0] = rl(jnp.where(low, below, p1), 64, 1).astype(BF16)
    cand[2, 1] = jnp.where(low, rl(below, 64, 1), 0.0).astype(BF16)
    second = []
    for k, dcol in enumerate((-2, -1, 1, 2)):
        pick = pick_of(dcol)
        for j in range(2):
            psend[k, j] = cand[pick, j]
        second.append(new(psend.at[k], ptrio.at[2 - dcol], (0, dcol)))
    start_all(second)
    mine = pick_of(0)
    for j in range(2):
        ptrio[2, j] = cand[mine, j]
    picks = [pick_of(-1), pick_of(1)]
    my_row = row + offset_of(off, 0, row, col)
    my_col = col + offset_of(off, 1, row, col)
    dcol = my_col - col + 1
    thirds = []
    for q in range(PARTS):
        cs = part_of(q)
        wait_all(stages[q])
        if q + 2 < PARTS:
            start_all(stages[q + 2])

        def fill(j, carry, cs=cs, q=q):
            send_buf[0, j, cs] = strips[q][16 * picks[0] + j]
            send_buf[1, j, cs] = strips[q][16 * picks[1] + j]
            return carry

        lax.fori_loop(0, 24, fill, 0)
        third = [
            new(send_buf.at[0, :, cs], trios[q].at[2], (0, -1)),
            new(send_buf.at[1, :, cs], trios[q].at[0], (0, 1)),
        ]
        start_all(third)
        thirds.append(third)

        def keep(j, carry, q=q):
            trios[q][1, j] = strips[q][16 * mine + j]
            return carry

        lax.fori_loop(0, 24, keep, 0)
        for n in range(q * 4 // PARTS, (q + 1) * 4 // PARTS):
            at = slice(n * 512, (n + 1) * 512)
            r.fw[:, at] = conv_chunk(r.weight, r.x3w, n * 512, 512).astype(BF16)
        small_weights(r, q)
    wait_all(second)
    m = r.m
    low = lax.rem(lane, 8) < 4
    for j in range(2):
        right = jnp.where(my_col == NCOL - 1, 0.0, ptrio[dcol + 2, j].astype(F32))
        left = jnp.where(my_col == 0, 0.0, ptrio[dcol, j].astype(F32))
        m[:, (24 + j) * TC : (25 + j) * TC] = jnp.where(low, right, left).astype(BF16)
    for q in range(PARTS):
        wait_all(thirds[q])
        cs = part_of(q)
        for j in range(24):
            m[cs, j * TC : (j + 1) * TC] = trios[q][dcol, j]
    correlate(r.fw, m, r.cv, r.cvpack, r.sums, r.mt, r.rt, r.grim, r.s1, r.s2)
    save_s.wait()
    save_w.wait()


def forward(offsets, summer, winter, cot, weight, w_first, w_second):
    one = lambda c: pltpu.VMEM((c, TC), BF16)
    some = lambda n, c: pltpu.VMEM((n, c, TC), BF16)
    n = 16 + 6 + 4 * PARTS
    scratch = dict(
        wide=pltpu.VMEM((C * TR, TC), F32), wide2=pltpu.VMEM((C * TR, TC), F32), cwide=pltpu.VMEM((32 * TR, TC), F32),
        ss=tiles(10), rs=tiles(10), sw=tiles(2), sw2=tiles(2), rw=tiles(2), sc=some(4, 32), rc=some(4, 32),
        ks=tiles(), kw=tiles(), kc=one(32), is_=tiles(2), iw=tiles(2), ic=some(2, 32),
        x3s=pltpu.VMEM((3 * C, 26 * TC), BF16), x3w=pltpu.VMEM((3 * C, 18 * TC), BF16), fp=tiles(26),
        pin=tiles(2), cand=tiles(3, 2), send_buf=tiles(2, 24), ptrio=tiles(5, 2), psend=tiles(4, 2),
        mt=pltpu.VMEM((24 * TC, C), BF16), rt=pltpu.VMEM((2 * TC, C), BF16), grim=pltpu.VMEM((2 * TC, TR * TC), F32),
        s1=pltpu.VMEM((CH, TC), F32), s2=pltpu.VMEM((CH, TC), F32),
        lsem=dma(PARTS + 2), sems=dma(n), rsems=dma(n),
    )
    for q in range(PARTS):
        scratch[f"strip{q}"] = pltpu.VMEM((56, WIDE, TC), BF16)
        scratch[f"trio{q}"] = pltpu.VMEM((3, 24, WIDE, TC), BF16)
    return call(
        forward_kernel,
        dict(
            off=(offsets, sspec()), summer=(summer, vspec()), winter=(winter, vspec()), cot=(cot, vspec()),
            weight=(weight, vspec()), w_first=(w_first, vspec()), w_second=(w_second, vspec()),
        ),
        dict(
            w1=(sds((64, 9 * CH), BF16), vspec()), w1f=(sds((CH, 576), BF16), vspec()),
            w2f=(sds((64, 288), BF16), vspec()),
            crows=(sds((4, 32, TC), BF16), vspec()), ct=(sds((3, 32, TC), BF16), vspec()),
            xs=(sds((3 * C, 26 * TC), BF16), anyspec()), xw=(sds((3 * C, 18 * TC), BF16), anyspec()),
            fw=(sds((C, TR * TC), BF16), vspec()), m=(sds((C, 26 * TC), BF16), vspec()),
            cv=(sds((TR, CH, TC), F32), vspec()), cvpack=(sds((CH, TC), F32), vspec()),
            sums=(sds((8, 256), F32), vspec()),
        ),
        scratch,
        0,
    )


def bit_off(lane, bit):
    return (lane & bit) == 0


def shear(main, rim):
    low = lane_of((80, TC)) < 64
    w = jnp.where(low, jnp.concatenate([rim, main[0:72]], 0), jnp.concatenate([main[56:128], rim], 0))
    w = jnp.where(bit_off(lane_of((48, TC)), 32), w[0:48], w[32:80])
    w = jnp.where(bit_off(lane_of((32, TC)), 16), w[0:32], w[16:48])
    w = jnp.where(bit_off(lane_of((24, TC)), 8), w[0:24], w[8:32])
    lane = lane_of((16, TC))
    w = jnp.where(bit_off(lane, 4), rl(w, -4, 0)[0:16], w[8:24])
    w = jnp.where(bit_off(lane, 2), w, rl(w, -2, 0))
    w = jnp.where(bit_off(lane, 1), w, rl(w, -1, 0))
    return jnp.where(lax.broadcasted_iota(jnp.int32, (16, TC), 0) < 9, w, 0.0)


def unshear(value):
    lane = lane_of((16, TC))
    w = jnp.where(bit_off(lane, 1), value, rl(value, 1, 0))
    w = jnp.where(bit_off(lane, 2), w, rl(w, 2, 0))
    zeros = lambda n: jnp.zeros((n, TC), F32)
    padded = jnp.concatenate([w, zeros(8)], 0)
    w = jnp.where(bit_off(lane_of((24, TC)), 4), rl(padded, 4, 0), jnp.concatenate([zeros(8), w], 0))
    for n, bit in ((24, 8), (32, 16), (48, 32)):
        w = jnp.where(
            bit_off(lane_of((n + bit, TC)), bit),
            jnp.concatenate([w, zeros(bit)], 0),
            jnp.concatenate([zeros(bit), w], 0),
        )
    low = lambda n: lane_of((n, TC)) < 64
    main = jnp.concatenate(
        [
            jnp.where(low(56), w[8:64], 0.0),
            jnp.where(low(16), w[64:80], w[0:16]),
            jnp.where(low(56), 0.0, w[16:72]),
        ],
        0,
    )
    return main, jnp.where(low(8), w[0:8], w[72:80])


def row_sums(first, second):
    ones = jnp.ones((8, TC), F32)
    a = lax.dot_general(ones, first, NT, precision=lax.Precision.HIGHEST, preferred_element_type=F32)
    b = lax.dot_general(ones, second, NT, precision=lax.Precision.HIGHEST, preferred_element_type=F32)
    return jnp.where(lax.broadcasted_iota(jnp.int32, a.shape, 0) == 0, a, b)


def correlate(fw, m, cv, pack, sums, mt, rt, grim, s1, s2):
    for r in range(24):
        mt[r * TC : (r + 1) * TC, :] = m[:, r * TC : (r + 1) * TC].T
    for q in range(2):
        rt[q * TC : (q + 1) * TC, :] = m[:, (24 + q) * TC : (25 + q) * TC].T
    for n in range(4):
        grim[:, n * 512 : (n + 1) * 512] = dot(rt[...], fw[:, n * 512 : (n + 1) * 512])
    s1[...] = jnp.zeros_like(s1)
    s2[...] = jnp.zeros_like(s2)

    def at_pair(pair, carry):
        feat = fw[:, pl.ds(pl.multiple_of(pair * 2 * TC, 2 * TC), 2 * TC)]
        for t in range(10):
            mains = dot(mt[pl.ds(pl.multiple_of((pair * 2 + t) * TC, TC), TC), :], feat)
            for k in range(2):
                a = t - k
                if a < 0 or a > 8:
                    continue
                y = pair * 2 + k
                lanes = pl.ds(pl.multiple_of(y * TC, TC), TC)
                rim = grim[pl.ds(pl.multiple_of((y + a) * 8, 8), 8), lanes]
                value = shear(mains[:, k * TC : (k + 1) * TC], rim) * 0.0625
                rows = slice(a * 16, (a + 1) * 16)
                cv[y, rows, :] = value
                s1[rows, :] += value
                s2[rows, :] += value * value
        return carry

    lax.fori_loop(0, TR // 2, at_pair, 0)
    pack[...] = pack_cols(lambda y: cv[y], [(c, b + 2) for c, b in TWO])
    sums[...] = jnp.zeros_like(sums)
    sums[:, 0:CH] = row_sums(s1[...], s2[...])


def reduce_one(src, dst, out, send, recv, axis, count):
    copies = []
    for d in range(1, count):
        step = (0, d) if axis == "col" else (d, 0)
        copies.append(
            pltpu.make_async_remote_copy(
                src_ref=src,
                dst_ref=dst.at[d],
                send_sem=send.at[d],
                recv_sem=recv.at[d],
                device_id=device_at(*step),
                device_id_type=MESH,
            )
        )
    start_all(copies)
    dst[0] = src[...]
    wait_all(copies)
    me = lax.axis_index(axis)
    total = None
    for d in range(count):
        value = dst[lax.rem(me - d + count, count)]
        total = value if total is None else total + value
    out[...] = total


RING = [(0, d) for d in range(1, NCOL)] + [(d, 0) for d in range(1, NROW)]


def tile_inside(b, shape):
    lane = lane_of(shape)
    row = lax.axis_index("row")
    col = lax.axis_index("col")
    local = jnp.where(lane < 64, lane, lane - 64)
    y = row * TR - 2 + local
    x = jnp.where(lane < 64, col * TC - 1 + b, col * TC + TC + b)
    return (y >= 0) & (y < NROW * TR) & (x >= 0) & (x < NCOL * TC) & (local < 20)


def rim_patches(tiles, a):
    return jnp.concatenate([rl(t, -a, 1) for t in tiles], 0).astype(BF16)


def silu_parts(value):
    sigma = jax.nn.sigmoid(value)
    return value * sigma, sigma * (1.0 + value * (1.0 - sigma))


def columns(sums):
    turned = sums.T
    return turned[0:CH, 0:1], turned[0:CH, 1:2]


def refine(r, scale, bias, inv, mid):
    row = lax.axis_index("row")
    first = row == 0
    last = row == NROW - 1
    cv, vrows, own_pack, sides, cot, crows, ct = r.cv, r.vrows, r.own_pack, r.sides, r.cot, r.crows, r.ct
    w1, w1f, w2, w2f = r.w1, r.w1f, r.w2, r.w2f
    refined, gpre, gfirst, gsecond, sums = r.refined, r.gpre, r.gfirst, r.gsecond, r.gsums0
    cwide, n3x, c3x, h3, gh3, hpre, gmain = r.cwide, r.n3x, r.c3x, r.h3, r.gh3, r.hpre, r.gmain
    s1, s2, rwide = r.s1, r.s2, r.rwide

    def normed_of(value):
        return silu_parts(value * scale + bias)[0]

    ntiles = [
        jnp.where(tile_inside(b - 1, (CH, TC)), normed_of(t), 0.0) for b, t in enumerate(three_tiles(sides[0], own_pack[...], sides[1]))
    ]

    def nrow(k):
        if k < 2:
            return jnp.where(first, 0.0, normed_of(vrows[k]))
        if k >= 18:
            return jnp.where(last, 0.0, normed_of(vrows[k - 16]))
        return normed_of(cv[k - 2])

    build_x3(n3x, nrow, ntiles[1], 20, CH)
    ctiles = [ct[k].astype(F32) for k in range(3)]
    cwide[...] = cot[...].astype(F32)

    def crow(k):
        if k < 2:
            return crows[k].astype(F32)
        if k >= 18:
            return crows[k - 16].astype(F32)
        return strided(cwide, k - 2, 32)

    build_x3(c3x, crow, ctiles[1], 20, 32)

    def both(w_ref, x3, tiles):
        depth = x3.shape[0]
        rim = None
        for a in range(3):
            term = dot(w_ref[:, a * depth : (a + 1) * depth], rim_patches(tiles, a))
            rim = term if rim is None else rim + term
        return rim

    lane = lane_of((64, TC))
    local = jnp.where(lane < 64, lane, lane - 64)
    ypos = row * TR - 1 + local
    col = lax.axis_index("col")
    xpos = jnp.where(lane < 64, col * TC - 1, col * TC + TC)
    rim_in = (ypos >= 0) & (ypos < NROW * TR) & (local < 18) & (xpos >= 0) & (xpos < NCOL * TC)
    rim_h, rim_slope = silu_parts(both(w1, n3x, ntiles))
    rim_g = both(w2f, c3x, ctiles)
    rim_h = jnp.where(rim_in, rim_h, 0.0)
    rim_g = jnp.where(rim_in, rim_g * rim_slope, 0.0)
    for n in range(6):
        hpre[:, n * 384 : (n + 1) * 384] = conv_chunk(w1, n3x, n * 384, 384)
        gmain[:, n * 384 : (n + 1) * 384] = conv_chunk(w2f, c3x, n * 384, 384)

    def edge(k):
        return first if k == 0 else (last if k == 17 else None)

    def hrow(k):
        value, slope = silu_parts(hpre[:, k * TC : (k + 1) * TC])
        grad = gmain[:, k * TC : (k + 1) * TC] * slope
        gone = edge(k)
        if gone is not None:
            value = jnp.where(gone, 0.0, value)
            grad = jnp.where(gone, 0.0, grad)
        gmain[:, k * TC : (k + 1) * TC] = grad
        return value

    build_x3(h3, hrow, rim_h, 18, 64)
    build_x3(gh3, lambda k: gmain[:, k * TC : (k + 1) * TC], rim_g, 18, 64)
    for n in range(4):
        value = conv_chunk(w2, h3, n * 512, 512)
        for j in range(4):
            rwide[pl.ds(n * 4 + j, 32, stride=TR), :] = value[:, j * TC : (j + 1) * TC]
    refined[...] = rwide[...].astype(BF16)
    own = slice(TC, 17 * TC)
    mine = slice(2 * TC, 18 * TC)
    gfirst[:, 9 * CH :] = jnp.zeros((64, 1408 - 9 * CH), F32)
    gsecond[:, 576:] = jnp.zeros((32, 64), F32)
    for a in range(3):
        gsecond[:, a * 192 : (a + 1) * 192] = dot_nt(c3x[32:64, mine], h3[:, a * TC : (a + 16) * TC])
        gfirst[:, a * 432 : (a + 1) * 432] = dot_nt(gh3[64:128, own], n3x[:, (a + 1) * TC : (a + 17) * TC])
    s1[...] = jnp.zeros_like(s1)
    s2[...] = jnp.zeros_like(s2)
    for n in range(4):
        value = conv_chunk(w1f, gh3, n * 512, 512)
        for j in range(4):
            y = n * 4 + j
            volume = cv[y]
            grad = value[:, j * TC : (j + 1) * TC] * silu_parts(volume * scale + bias)[1]
            gpre[y] = grad
            s1[...] += grad
            s2[...] += grad * (volume * inv - mid)
    sums[...] = jnp.zeros_like(sums)
    sums[:, 0:CH] = row_sums(s1[...], s2[...])


def correlate_back(cv, gpre, coef, fw, m, gfw, gm, kw, q, qrim):
    def at_row(y, carry):
        lanes = pl.ds(pl.multiple_of(y * TC, TC), TC)
        grad = coef[0] * gpre[y] + coef[1] + coef[2] * cv[y]
        grad = grad.astype(BF16).astype(F32)
        for a in range(9):
            main, rim = unshear(grad[a * 16 : (a + 1) * 16])
            q[pl.ds(pl.multiple_of((y + a) * TC, TC), TC), lanes] = main.astype(BF16)
            qrim[pl.ds(pl.multiple_of((y + a) * 8, 8), 8), lanes] = rim
        return carry

    qrim[...] = jnp.zeros_like(qrim)
    for y in range(TR):
        for p in (y - 1, y + 9):
            if 0 <= p < 24:
                q[p * TC : (p + 1) * TC, y * TC : (y + 1) * TC] = jnp.zeros((TC, TC), BF16)
    lax.fori_loop(0, TR, at_row, 0)
    for y in range(0, TR, 2):
        at = slice(y * TC, (y + 2) * TC)
        value = dot(m[:, y * TC : (y + 10) * TC], q[y * TC : (y + 10) * TC, at])
        value = value + dot(m[:, 24 * TC : 26 * TC], qrim[:, at].astype(BF16))
        gfw[:, at] = (value * 0.0625).astype(BF16)
    for p in range(0, 24, 2):
        at = slice(max(0, p - 8) * TC, (min(15, p + 1) + 1) * TC)
        value = dot_nt(fw[:, at], q[p * TC : (p + 2) * TC, at]) * 0.0625
        for k in range(2):
            gm[p + k] = value[:, k * TC : (k + 1) * TC].astype(BF16)
    kw[...] = pack_cols(lambda y: gfw[:, y * TC : (y + 1) * TC].astype(F32), two_cols(1)).astype(BF16)
    for k in range(2):
        value = dot_nt(fw[...], qrim[k * TC : (k + 1) * TC, :].astype(BF16))
        gm[24 + k] = (value * 0.0625).astype(BF16)


def middle_kernel(r):
    arrived = greet(RING)
    new = numbered(r.sems, r.rsems)
    arrived()
    rows = [
        new(r.cv.at[pl.ds(14, 2)], r.vrows.at[pl.ds(0, 2)], (1, 0)),
        new(r.cv.at[pl.ds(0, 2)], r.vrows.at[pl.ds(2, 2)], (-1, 0)),
    ]
    start_all(rows)
    reduce_one(r.sums, r.gcol, r.total, r.csend, r.crecv, "col", NCOL)
    wait_all(rows)
    pack = r.cvpack[...]
    for k in range(4):
        pack = put_col(pack, r.vrows[k], TWO, k if k < 2 else 16 + k)
    r.own_pack[...] = pack
    cols = [new(r.own_pack, r.sides.at[0], (0, 1)), new(r.own_pack, r.sides.at[1], (0, -1))]
    start_all(cols)
    reduce_one(r.total, r.grow, r.total2, r.rsend, r.rrecv, "row", NROW)
    wait_all(cols)
    sum1, sum2 = columns(r.total2[...])
    mean = sum1 / PIXELS
    inv = lax.rsqrt(sum2 / PIXELS - mean * mean + 1e-05)
    shape = (CH, TC)
    spread = jnp.where(
        lax.broadcasted_iota(jnp.int32, (CH, 81), 1) == padded_place((CH, 1), 0), 1.0, 0.0
    )
    both = lax.dot_general(spread, r.norm[...], NT, precision=lax.Precision.HIGHEST, preferred_element_type=F32)
    gain, shift = both[:, 0:1], both[:, 1:2]
    scale = jnp.broadcast_to(gain * inv, shape)
    mid = jnp.broadcast_to(mean * inv, shape)
    inv = jnp.broadcast_to(inv, shape)
    refine(r, scale, shift - mean * scale, inv, mid)
    reduce_one(r.gsums0, r.gcol2, r.total3, r.csend2, r.crecv2, "col", NCOL)
    reduce_one(r.total3, r.grow2, r.gsums, r.rsend2, r.rrecv2, "row", NROW)
    grad_shift, grad_gain = columns(r.gsums[...])
    narrow = jnp.where(
        lax.broadcasted_iota(jnp.int32, (81, CH), 0) == padded_place((1, CH), 1), 1.0, 0.0
    )
    r.gnorm[...] = lax.dot_general(
        r.gsums[:, 0:CH], narrow, NT, precision=lax.Precision.HIGHEST, preferred_element_type=F32
    )
    slope = -scale * grad_gain / PIXELS
    coef = (scale, -scale * grad_shift / PIXELS - slope * mid, slope * inv)
    correlate_back(r.cv, r.gpre, coef, r.fw, r.m, r.gfw, r.gm, r.gkw, r.q, r.qrim)


def middle(fore, cot, norm, w2):
    f32 = lambda *n: pltpu.VMEM(n, F32)
    bf16 = lambda *n: pltpu.VMEM(n, BF16)
    return call(
        middle_kernel,
        {
            name: (array, vspec())
            for name, array in dict(
                cv=fore.cv, cvpack=fore.cvpack, sums=fore.sums, crows=fore.crows, ct=fore.ct, fw=fore.fw, m=fore.m,
                cot=cot, norm=norm, w1=fore.w1, w1f=fore.w1f, w2=w2, w2f=fore.w2f,
            ).items()
        },
        {
            name: (sds(shape, kind), vspec())
            for name, shape, kind in (
                ("refined", (32 * TR, TC), BF16),
                ("gfirst", (64, 1408), F32),
                ("gsecond", (32, 640), F32),
                ("gnorm", (8, 81), F32),
                ("gfw", (C, TR * TC), BF16),
                ("gm", (26, C, TC), BF16),
                ("gkw", (C, TC), BF16),
            )
        },
        dict(
            vrows=f32(4, CH, TC), own_pack=f32(CH, TC), sides=f32(2, CH, TC),
            gcol=f32(NCOL, 8, 256), grow=f32(NROW, 8, 256), total=f32(8, 256), total2=f32(8, 256),
            gcol2=f32(NCOL, 8, 256), grow2=f32(NROW, 8, 256), gsums0=f32(8, 256), gsums=f32(8, 256), total3=f32(8, 256),
            cwide=f32(32 * TR, TC), n3x=bf16(3 * CH, 20 * TC), c3x=bf16(96, 20 * TC), h3=bf16(192, 18 * TC),
            gh3=bf16(192, 18 * TC), hpre=f32(64, 18 * TC), gmain=f32(64, 18 * TC), s1=f32(CH, TC), s2=f32(CH, TC),
            rwide=f32(32 * TR, TC), gpre=f32(TR, CH, TC), q=bf16(24 * TC, TR * TC), qrim=f32(2 * TC, TR * TC),
            sems=dma(4), rsems=dma(4),
            csend=dma(NCOL), crecv=dma(NCOL), rsend=dma(NROW), rrecv=dma(NROW),
            csend2=dma(NCOL), crecv2=dma(NCOL), rsend2=dma(NROW), rrecv2=dma(NROW),
        ),
        1,
    )


TILES = 384
HALF = TILES // 2
FIRST = 128
SHARE = FIRST // 4


def final_kernel(r):
    row = lax.axis_index("row")
    col = lax.axis_index("col")
    core = lax.rem(col, 2)
    chip = lax.div(col, 2)
    off, gm, gfw = r.off, r.gm, r.gfw
    trios = [getattr(r, f"trio{q}") for q in range(PARTS)]
    ptrio, strip, be, ab, pout, pin, g24, g5 = r.ptrio, r.strip, r.be, r.ab, r.pout, r.pin, r.g24, r.g5
    pab, pq, pack, side, rw, kw, iw, kw0 = r.pab, r.pq, r.pack, r.side, r.rw, r.kw, r.iw, r.gkw
    ext, wrows, buf, half_in, half, y_in = r.ext, r.wrows, r.buf, r.half_in, r.half, r.y_in
    share, row_in, full, x3, wide, flipped = r.share, r.row_in, r.full, r.x3, r.wide, r.flipped
    xw, xs = r.xw_here, r.xs_here
    arrived = greet(RING)
    loads = [
        pltpu.make_async_copy(r.xw, xw, r.lsem.at[PARTS]),
        pltpu.make_async_copy(r.xs, xs, r.lsem.at[PARTS + 1]),
    ]
    owns = [
        pltpu.make_async_copy(gm.at[pl.ds(0, 24), part_of(q)], trios[q].at[1, pl.ds(0, 24)], r.lsem.at[q])
        for q in range(PARTS)
    ]
    start_all(owns)
    start_all(loads)
    new = numbered(r.sems, r.rsems)
    arrived()
    pstage = [new(gm.at[pl.ds(24, 2)], ptrio.at[0], (0, 1)), new(gm.at[pl.ds(24, 2)], ptrio.at[2], (0, -1))]
    wstage = [
        new(gfw.at[:, pl.ds((TR - 1) * TC, TC)], rw.at[0], (1, 0)),
        new(gfw.at[:, pl.ds(0, TC)], rw.at[1], (-1, 0)),
    ]
    start_all(pstage + wstage)
    stages = []
    for q in range(PARTS):
        cs = part_of(q)
        stages.append(
            [
                new(gm.at[pl.ds(0, 24), cs], trios[q].at[0, pl.ds(0, 24)], (0, 1)),
                new(gm.at[pl.ds(0, 24), cs], trios[q].at[2, pl.ds(0, 24)], (0, -1)),
            ]
        )
    start_all(stages[0])
    start_all(stages[1])
    for q in range(PARTS):
        for k in range(3):
            trios[q][k, 24] = jnp.zeros((WIDE, TC), BF16)
    for k in range(9):
        flipped[:, k * C : (k + 1) * C] = r.weight[:, (8 - k) * C : (9 - k) * C].T
    wait_all(owns)
    sources = []
    for k in range(3):
        place = col + k - 1
        there = lax.rem(place + NCOL, NCOL)
        drow = offset_of(off, 0, row, there)
        dcol = offset_of(off, 1, row, there)
        good = (dcol == 1 - k) & (place >= 0) & (place < NCOL)
        sources.append((drow, good))

    first, last = row == 0, row == NROW - 1
    zero = jnp.zeros((C, TC), F32)
    lane = lane_of((C, TC))
    low = lane < 64

    def only(flag, ref):
        return jnp.where(flag, ref.astype(F32), 0.0)

    wait_all(pstage)
    to_above, own0, own1, to_below = zero, zero, zero, zero
    for k, (drow, good) in enumerate(sources):
        t0, t1 = (gm[24], gm[25]) if k == 1 else (ptrio[k, 0], ptrio[k, 1])
        t0, t1 = t0.astype(F32), jnp.where(low, t1.astype(F32), 0.0)
        up, level, down = (good & (drow == v) for v in (-1, 0, 1))
        turned0, turned1 = rl(t0, 64, 1), rl(t1, 64, 1)
        to_above += jnp.where(up, t0, 0.0)
        own0 += jnp.where(up, t1, 0.0) + jnp.where(level, t0, 0.0)
        own1 += jnp.where(level, turned1, 0.0) + jnp.where(down & jnp.logical_not(low), turned0, 0.0)
        to_below += jnp.where(down, turned1 + jnp.where(low, turned0, 0.0), 0.0)
    pout[0] = to_above.astype(BF16)
    pout[1] = to_below.astype(BF16)
    pstage = [new(pout.at[0], pin.at[0], (-1, 0)), new(pout.at[1], pin.at[1], (1, 0))]
    start_all(pstage)

    wait_all(wstage)
    kpack = kw0[...].astype(F32)
    for k in range(2):
        value = only(jnp.logical_not(first if k == 0 else last), rw[k])
        wrows[k] = value.astype(BF16)
        kpack = put_col(kpack, value, two_cols(0), 17 * k)
    kw[...] = kpack.astype(BF16)
    wstage = [new(kw, iw.at[0], (0, 1)), new(kw, iw.at[1], (0, -1))]
    start_all(wstage)

    thirds = []
    for q in range(PARTS):
        cs = part_of(q)
        wait_all(stages[q])
        if q + 2 < PARTS:
            start_all(stages[q + 2])

        def gather(p, carry, cs=cs, q=q):
            total = None
            for k, (drow, good) in enumerate(sources):
                j = p - 16 * (drow + 1)
                fits = good & (j >= 0) & (j < 24)
                value = trios[q][k, jnp.where(fits, j, 24)].astype(F32)
                total = value if total is None else total + value
            strip[p, cs] = total.astype(BF16)
            return carry

        lax.fori_loop(0, 56, gather, 0)
        third = [
            new(strip.at[pl.ds(0, 16), cs], be.at[:, cs], (-1, 0)),
            new(strip.at[pl.ds(40, 16), cs], ab.at[:, cs], (1, 0)),
        ]
        start_all(third)
        thirds.append(third)
        if q == 0:
            wait_all(loads)
        if q < 3:
            for n in range(3):
                part = slice(n * C, (n + 1) * C)
                at = slice(q * 768 + n * C, q * 768 + (n + 1) * C)
                r.gfeat[:, at] = dot_nt(gfw[...], xw[part, q * TC : (q + 16) * TC])
    wait_all(wstage)
    whalo = other_side(iw[0].astype(F32), iw[1].astype(F32))
    wait_all(pstage)
    not_first, not_last = row > 0, row < NROW - 1
    p0 = own0 + only(not_last, pin[0])
    p1 = own1 + only(not_first, pin[1])
    tile_a = p0 + jnp.where(low, 0.0, rl(p1, 64, 1))
    tile_b = jnp.where(low, rl(p1, 64, 1), 0.0)
    pab[0] = tile_a.astype(BF16)
    pab[1] = tile_b.astype(BF16)
    fourth = [new(pab.at[0], pq.at[0], (-1, 0)), new(pab.at[1], pq.at[1], (1, 0))]
    start_all(fourth)

    def w_row(k):
        if k == 0 or k == TR + 1:
            return wrows[k // (TR + 1)].astype(F32)
        return gfw[:, (k - 1) * TC : k * TC].astype(F32)

    build_x3(x3, w_row, whalo, TR + 2, C)

    def last_conv(n):
        value = conv_chunk(flipped, x3, n * 512, 512)
        for j in range(4):
            wide[pl.ds(n * 4 + j, C, stride=TR), :] = value[:, j * TC : (j + 1) * TC]

    for q in range(PARTS):
        cs = part_of(q)
        wait_all(thirds[q])
        for k in range(24):
            total = strip[16 + k, cs].astype(F32)
            if k < 16:
                total = total + only(not_last, be[k, cs])
            if k >= 8:
                total = total + only(not_first, ab[k - 8, cs])
            g24[k, cs] = total.astype(BF16)
        more = [
            new(g24.at[pl.ds(0, 5), cs], g5.at[1, :, cs], (-1, 0)),
            new(g24.at[pl.ds(19, 5), cs], g5.at[0, :, cs], (1, 0)),
        ]
        start_all(more)
        fourth = fourth + more
        for n in range(q * 4 // PARTS, (q + 1) * 4 // PARTS):
            last_conv(n)
    r.out_w[...] = wide[...].astype(BF16)
    wait_all(fourth)
    tile_a = tile_a + jnp.where((lane >= 24) & (lane < 64), only(not_first, pq[1]), 0.0)
    tile_b = tile_b + jnp.where(lane < 40, only(not_last, pq[0]), 0.0)
    pack[0] = tile_a.astype(BF16)
    pack[1] = tile_b.astype(BF16)
    total = zero
    for k in range(18):
        value = g24[k + 3].astype(F32)
        if k < 5:
            value = value + only(not_first, g5[0, k])
        if k >= 13:
            value = value + only(not_last, g5[1, k - 13])
        if k == 0:
            value = only(not_first, value)
        if k == 17:
            value = only(not_last, value)
        strip[k] = value.astype(BF16)
        total = put_col(total, value, two_cols(0), k)
    pack[2] = total.astype(BF16)
    stage = [new(pack, side.at[0], (0, 1)), new(pack, side.at[1], (0, -1))]
    start_all(stage)
    source = lax.broadcasted_iota(jnp.int32, (2 * TC, TC), 0)
    target = lax.broadcasted_iota(jnp.int32, (2 * TC, TC), 1)
    take = ((target < 18) & (source == (target + 3) * 8 + 7)) | (
        (target >= 64) & (target < 82) & (source == (target - 61) * 8)
    )
    rims = dot(pack[0], take[0:TC].astype(F32).astype(BF16)) + dot(pack[1], take[TC:].astype(F32).astype(BF16))
    wait_all(stage)
    halo = other_side(side[0, 2].astype(F32), side[1, 2].astype(F32))
    halo = halo + jnp.where(low, only(col > 0, rims), only(col < NCOL - 1, rims))
    at = jnp.where(low, lane, lane - 64)
    gone = (first & (at == 0)) | (last & (at == 17))
    shalo = jnp.where(gone, 0.0, halo)
    for k in range(18):
        p, base = ((0, (k + 3) * 8) if k + 3 < 16 else (1, (k - 13) * 8))
        value = strip[k].astype(F32)
        left = rl(only(col > 0, side[0, p]), -base, 1)
        right = rl(only(col < NCOL - 1, side[1, p]), 120 - base, 1)
        extra = jnp.where(lane < 4, left, 0.0) + jnp.where(lane >= 124, right, 0.0)
        if k == 0:
            extra = only(not_first, extra)
        if k == 17:
            extra = only(not_last, extra)
        ext[:, k * TC : (k + 1) * TC] = (value + extra).astype(BF16)
    for a in range(3):
        at = slice((a + 4) * TC, (a + 20) * TC)
        for n in range(3):
            part = slice(n * C, (n + 1) * C)
            into = slice(a * 768 + n * C, a * 768 + (n + 1) * C)
            value = r.gfeat[:, into] + dot_nt(ext[:, TC : 17 * TC], xs[part, at])
            value = value.astype(BF16)
            for t in range(2):
                for g in range(16):
                    buf[(a * 6 + n * 2 + t) * 16 + g] = value[g * 16 : (g + 1) * 16, t * TC : (t + 1) * TC]
    for t in range(11):
        for g in range(4):
            buf[288 + t * 4 + g] = r.gfirst[g * 16 : (g + 1) * 16, t * TC : (t + 1) * TC].astype(BF16)
    for t in range(5):
        for g in range(2):
            buf[332 + t * 2 + g] = r.gsecond[g * 16 : (g + 1) * 16, t * TC : (t + 1) * TC].astype(BF16)
    for t in range(342, TILES):
        buf[t] = jnp.zeros((16, TC), BF16)
    partner = (row, col + 1 - 2 * core)
    pair = new(buf.at[pl.ds(HALF * (1 - core), HALF)], half_in, device=partner)
    pair.start()

    pair.wait()

    def add_half(k, carry):
        half[k] = (buf[HALF * core + k].astype(F32) + half_in[k].astype(F32)).astype(BF16)
        return carry

    lax.fori_loop(0, HALF, add_half, 0)
    copies = []
    for d in range(1, 4):
        there = lax.rem(chip + d, 4)
        copies.append(new(half.at[pl.ds(SHARE * there, SHARE)], y_in.at[d - 1], device=(row, 2 * there + core)))
    for d in range(1, NROW):
        there = lax.rem(row + d, NROW)
        copies.append(new(half.at[pl.ds(FIRST + 4 * there, 4)], row_in.at[d - 1], device=(there, col)))
    start_all(copies)
    build_x3(x3, lambda k: ext[:, k * TC : (k + 1) * TC].astype(F32), shalo, TR + 2, C)
    last_conv(0)
    wait_all(copies)

    def add_share(k, carry):
        total = half[SHARE * chip + k].astype(F32)
        for d in range(3):
            total = total + y_in[d, k].astype(F32)
        share[k] = total.astype(BF16)
        return carry

    lax.fori_loop(0, SHARE, add_share, 0)
    for k in range(4):
        total = half[FIRST + 4 * row + k].astype(F32)
        for d in range(NROW - 1):
            total = total + row_in[d, k].astype(F32)
        r.part_b[k] = total.astype(BF16)
    copies = []
    for d in range(1, NROW):
        there = lax.rem(row + d, NROW)
        copies.append(new(share.at[pl.ds(2 * there, 2)], r.a_in.at[d - 1], device=(there, col)))
    for d in range(1, 4):
        there = lax.rem(chip + d, 4)
        copies.append(new(r.part_b.at[pl.ds(there, 1)], r.b_in.at[d - 1], device=(row, 2 * there + core)))
    start_all(copies)
    last_conv(1)
    r.padding[...] = padding_matrix()
    wait_all(copies)
    spot_a = HALF * core + SHARE * chip
    spot_b = HALF * core + FIRST + 4 * row
    for k in range(2):
        total = share[2 * row + k].astype(F32)
        for d in range(NROW - 1):
            total = total + r.a_in[d, k].astype(F32)
        full[spot_a + 2 * row + k] = total.astype(BF16)
    total = r.part_b[chip].astype(F32)
    for d in range(3):
        total = total + r.b_in[d, 0].astype(F32)
    full[spot_b + chip] = total.astype(BF16)

    def spread_along(mine, rows):
        if rows:
            return [new(mine, mine, device=(lax.rem(row + d, NROW), col)) for d in range(1, NROW)]
        return [new(mine, mine, device=(row, 2 * lax.rem(chip + d, 4) + core)) for d in range(1, 4)]

    copies = spread_along(full.at[pl.ds(spot_a + 2 * row, 2)], True)
    copies += spread_along(full.at[pl.ds(spot_b + chip, 1)], False)
    start_all(copies)
    last_conv(2)
    wait_all(copies)
    copies = spread_along(full.at[pl.ds(spot_a, SHARE)], False)
    copies += spread_along(full.at[pl.ds(spot_b, 4)], True)
    start_all(copies)
    last_conv(3)
    r.out_s[...] = wide[...].astype(BF16)
    wait_all(copies)
    mine = full.at[pl.ds(HALF * core, HALF)]
    pair = new(mine, mine, device=partner)
    pair.start()
    pair.wait()
    for t in range(18):
        for g in range(16):
            r.feat_out[g * 16 : (g + 1) * 16, t * TC : (t + 1) * TC] = full[t * 16 + g]
    for t in range(11):
        for g in range(4):
            r.firstb[g * 16 : (g + 1) * 16, t * TC : (t + 1) * TC] = full[288 + t * 4 + g]
    r.first_out[...] = dot_nt(r.firstb[:, 0 : 9 * CH], r.padding[...])
    for t in range(5):
        width = TC if t < 4 else 64
        for g in range(2):
            r.second_out[g * 16 : (g + 1) * 16, t * TC : t * TC + width] = full[332 + t * 2 + g][:, :width].astype(F32)


def final(offsets, fore, mid, weight):
    small = lambda *n: pltpu.VMEM(n + (16, TC), BF16)
    n = 14 + 6 * PARTS + 2 + 4 * (NROW - 1 + 3)
    scratch = dict(
        ptrio=tiles(3, 2), strip=tiles(56), be=tiles(16), ab=tiles(16), pout=tiles(2), pin=tiles(2), g24=tiles(24),
        g5=tiles(2, 5), pab=tiles(2), pq=tiles(2), pack=tiles(3), side=tiles(2, 3), rw=tiles(2), kw=tiles(), iw=tiles(2),
        wrows=tiles(2), ext=pltpu.VMEM((C, 18 * TC), BF16), flipped=pltpu.VMEM((C, 9 * C), BF16),
        gfeat=pltpu.VMEM((C, 9 * C), F32), x3=pltpu.VMEM((3 * C, 18 * TC), BF16), wide=pltpu.VMEM((C * TR, TC), F32),
        xw_here=pltpu.VMEM((3 * C, 18 * TC), BF16), xs_here=pltpu.VMEM((3 * C, 26 * TC), BF16),
        buf=small(TILES), half_in=small(HALF), half=small(HALF), y_in=small(3, SHARE), share=small(SHARE),
        row_in=small(NROW - 1, 4), a_in=small(NROW - 1, 2), b_in=small(3, 1), part_b=small(4), full=small(TILES),
        firstb=pltpu.VMEM((64, 1408), BF16), padding=pltpu.VMEM((729, 9 * CH), BF16),
        lsem=dma(PARTS + 2), sems=dma(n), rsems=dma(n),
    )
    for q in range(PARTS):
        scratch[f"trio{q}"] = pltpu.VMEM((3, 25, WIDE, TC), BF16)
    return call(
        final_kernel,
        dict(
            off=(offsets, sspec()), gm=(mid.gm, vspec()), gfw=(mid.gfw, vspec()), gkw=(mid.gkw, vspec()),
            gfirst=(mid.gfirst, vspec()), gsecond=(mid.gsecond, vspec()), weight=(weight, vspec()),
            xw=(fore.xw, anyspec()), xs=(fore.xs, anyspec()),
        ),
        dict(
            out_w=(sds((C * TR, TC), BF16), vspec()), out_s=(sds((C * TR, TC), BF16), vspec()),
            feat_out=(sds((C, 9 * C), BF16), vspec()), first_out=(sds((64, 729), F32), vspec()),
            second_out=(sds((32, 576), F32), vspec()),
        ),
        scratch,
        2,
    )


def body(winter, summer, offsets, feat_weight, bn_gain, bn_shift, w_first, w_second, cotangent):
    cot = cotangent.reshape(32 * TR, TC)
    norm = jnp.stack([bn_gain, bn_shift])
    fore = forward(offsets, summer.reshape(C * TR, TC), winter.reshape(C * TR, TC), cot, feat_weight, w_first, w_second)
    mid = middle(fore, cot, norm, w_second)
    last = final(offsets, fore, mid, feat_weight)
    return (
        mid.refined.reshape(32, TR, TC),
        last.out_w.reshape(C, TR, TC),
        last.out_s.reshape(C, TR, TC),
        last.feat_out.astype(F32),
        last.first_out,
        last.second_out,
        mid.gnorm[1],
        mid.gnorm[0],
    )


def solution(mesh):
    tile = P(None, "row", "col")
    return jax.shard_map(
        body,
        mesh=mesh,
        in_specs=(tile, tile, P(), P(), P(), P(), P(), P(), tile),
        out_specs=(tile, tile, tile, P(), P(), P(), P(), P()),
        check_vma=False,
    )
```

```python
import types

import jax
import jax.numpy as jnp
from jax import lax
from jax.experimental import pallas as pl
from jax.experimental.pallas import tpu as pltpu
from jax.sharding import PartitionSpec as P

MESH = pl.DeviceIdType.MESH
C = 256
TR = 16
TC = 128
CH = 144
NROW = 16
NCOL = 8
PIXELS = 262144.0
F32 = jnp.float32
BF16 = jnp.bfloat16
VMEM_LIMIT = 58 * 1024 * 1024
NT = (((1,), (1,)), ((), ()))


def vspec():
    return pl.BlockSpec(memory_space=pltpu.VMEM)


def sspec():
    return pl.BlockSpec(memory_space=pltpu.SMEM)


def sds(shape, dtype):
    return jax.ShapeDtypeStruct(shape, dtype)


def anyspec():
    return pl.BlockSpec(memory_space=pl.ANY)


def call(kernel, ins, outs, scratch, collective_id):
    names = list(ins) + list(outs) + list(scratch)

    def named(*refs):
        kernel(types.SimpleNamespace(**dict(zip(names, refs))))

    results = pl.pallas_call(
        named,
        out_shape=[shape for shape, _ in outs.values()],
        in_specs=[spec for _, spec in ins.values()],
        out_specs=[spec for _, spec in outs.values()],
        scratch_shapes=list(scratch.values()),
        compiler_params=pltpu.CompilerParams(
            vmem_limit_bytes=VMEM_LIMIT, collective_id=collective_id, has_side_effects=True
        ),
    )(*[array for array, _ in ins.values()])
    return types.SimpleNamespace(**dict(zip(outs, results)))


def tiles(*n):
    return pltpu.VMEM(n + (C, TC), BF16)


def dma(n):
    return pltpu.SemaphoreType.DMA((n,))


def numbered(sems, rsems):
    count = [0]

    def new(src, dst, step=None, device=None):
        k = count[0]
        count[0] += 1
        return pltpu.make_async_remote_copy(
            src_ref=src,
            dst_ref=dst,
            send_sem=sems.at[k],
            recv_sem=rsems.at[k],
            device_id=device_at(*step) if device is None else device,
            device_id_type=MESH,
        )

    return new


def rl(value, shift, axis):
    shift %= value.shape[axis]
    return value if shift == 0 else pltpu.roll(value, shift, axis)


def lane_of(shape):
    return lax.broadcasted_iota(jnp.int32, shape, 1)


def dot(a, b):
    return jnp.dot(a, b, preferred_element_type=F32)


def dot_nt(a, b):
    return lax.dot_general(a, b, NT, preferred_element_type=F32)


def pack_cols(row, cols, count=TR):
    total = None
    for y in range(count):
        value = row(y)
        lane = lane_of(value.shape)
        if total is None:
            total = jnp.zeros(value.shape, F32)
        for col, base in cols:
            total = jnp.where(lane == base + y, rl(value, base + y - col, 1), total)
    return total


TWO = [(0, 0), (1, 32), (126, 64), (127, 96)]


def two_cols(first_lane):
    return [(0, first_lane), (127, 64 + first_lane)]


def put_col(total, value, cols, k):
    lane = lane_of(value.shape)
    for col, base in cols:
        total = jnp.where(lane == base + k, rl(value, base + k - col, 1), total)
    return total


def other_side(left, right):
    lane = lane_of(left.shape)
    col = lax.axis_index("col")
    both = jnp.where(lane >= 64, jnp.where(col > 0, left, 0.0), jnp.where(col < NCOL - 1, right, 0.0))
    return rl(both, 64, 1)


def three_tiles(left, own, right):
    low = lane_of(own.shape) < 64
    return [
        jnp.where(low, rl(left, -64, 1), rl(own, -32, 1)),
        jnp.where(low, rl(left, -96, 1), rl(right, 64, 1)),
        jnp.where(low, own, rl(right, 32, 1)),
    ]


def device_at(drow, dcol):
    row = lax.rem(lax.axis_index("row") + drow + NROW, NROW)
    col = lax.rem(lax.axis_index("col") + dcol + NCOL, NCOL)
    return (row, col)


def greet(steps):
    both = sorted(set(steps) | {(-a, -b) for a, b in steps})
    barrier = pltpu.get_barrier_semaphore()
    for step in both:
        pl.semaphore_signal(barrier, inc=1, device_id=device_at(*step), device_id_type=MESH)
    return lambda: pl.semaphore_wait(barrier, len(both))


def start_all(copies):
    for copy in copies:
        copy.start()


def wait_all(copies):
    for copy in copies:
        copy.wait()


def strided(wide, y, channels):
    return wide[pl.ds(y, channels, stride=TR), :]


def build_x3(x3, row, halo, count, channels, first_lane=0):
    for k in range(count):
        value = row(k)
        lane = lane_of(value.shape)
        at = slice(k * TC, (k + 1) * TC)
        left = jnp.where(lane == 0, rl(halo, -(first_lane + k), 1), rl(value, 1, 1))
        right = jnp.where(lane == TC - 1, rl(halo, TC - 1 - (64 + first_lane + k), 1), rl(value, -1, 1))
        x3[0:channels, at] = left.astype(BF16)
        x3[channels : 2 * channels, at] = value.astype(BF16)
        x3[2 * channels : 3 * channels, at] = right.astype(BF16)


def conv_chunk(w_ref, x3, start, width, rows=slice(None)):
    total = None
    depth = x3.shape[0]
    for a in range(3):
        term = dot(w_ref[rows, a * depth : (a + 1) * depth], x3[:, start + a * TC : start + a * TC + width])
        total = term if total is None else total + term
    return total


def offset_of(off, part, row, col):
    return off[part, row, col]


PARTS = 4
WIDE = C // PARTS


def part_of(q):
    return pl.ds(q * WIDE, WIDE)


def padded_place(shape, axis):
    at = lax.broadcasted_iota(jnp.int32, shape, axis)
    tap = jnp.zeros(shape, jnp.int32)
    for t in range(1, 9):
        tap = tap + jnp.where(at >= t * CH, 1, 0)
    rest = at - tap * CH
    b = rest & 15
    return jnp.where(b < 9, tap * 81 + (rest >> 4) * 9 + b, -1)


def one_hot(mask):
    return jnp.where(mask, 1.0, 0.0).astype(BF16)


def padding_matrix():
    place = padded_place((1, 9 * CH), 1)
    return one_hot(lax.broadcasted_iota(jnp.int32, (729, 9 * CH), 0) == place)


def small_weights(r, q):
    if q == 0:
        r.w1[...] = dot(r.w_first[...], padding_matrix()).astype(BF16)
    if q == 1:
        place = padded_place((CH, 1), 0)
        source = lax.broadcasted_iota(jnp.int32, (CH, 729), 1)
        for k in range(9):
            pick = one_hot((source == place + (8 - k) * 81) & (place >= 0))
            r.w1f[:, k * 64 : (k + 1) * 64] = dot_nt(pick, r.w_first[...]).astype(BF16)
    if q == 2:
        target = lax.broadcasted_iota(jnp.int32, (64, 576), 0)
        source = lax.broadcasted_iota(jnp.int32, (64, 576), 1)
        for k in range(9):
            pick = one_hot(source == target + (8 - k) * 64)
            r.w2f[:, k * 32 : (k + 1) * 32] = dot_nt(pick, r.w_second[...]).astype(BF16)


def forward_kernel(r):
    row = lax.axis_index("row")
    col = lax.axis_index("col")
    first = row == 0
    last = row == NROW - 1
    arrived = greet([(1, 0), (0, 1), (0, 2)])
    new = numbered(r.sems, r.rsems)
    wide, wide2, cwide = r.wide, r.wide2, r.cwide

    wide[...] = r.summer[...].astype(F32)
    for k in range(5):
        r.ss[k] = strided(wide, 11 + k, C).astype(BF16)
        r.ss[5 + k] = strided(wide, k, C).astype(BF16)
    arrived()
    stage = [
        new(r.ss.at[pl.ds(0, 5)], r.rs.at[pl.ds(0, 5)], (1, 0)),
        new(r.ss.at[pl.ds(5, 5)], r.rs.at[pl.ds(5, 5)], (-1, 0)),
    ]
    start_all(stage)
    pack_s = pack_cols(lambda y: strided(wide, y, C), two_cols(5))
    wide2[...] = r.winter[...].astype(F32)
    r.sw[0] = strided(wide2, TR - 1, C).astype(BF16)
    r.sw[1] = strided(wide2, 0, C).astype(BF16)
    cwide[...] = r.cot[...].astype(F32)
    for k in range(2):
        r.sc[k] = strided(cwide, 14 + k, 32).astype(BF16)
        r.sc[2 + k] = strided(cwide, k, 32).astype(BF16)
    pack_w = pack_cols(lambda y: strided(wide2, y, C), two_cols(1))
    wait_all(stage)
    other = [
        new(r.sw.at[pl.ds(0, 1)], r.rw.at[pl.ds(0, 1)], (1, 0)),
        new(r.sw.at[pl.ds(1, 1)], r.rw.at[pl.ds(1, 1)], (-1, 0)),
        new(r.sc.at[pl.ds(0, 2)], r.rc.at[pl.ds(0, 2)], (1, 0)),
        new(r.sc.at[pl.ds(2, 2)], r.rc.at[pl.ds(2, 2)], (-1, 0)),
    ]
    start_all(other)
    for k in range(10):
        value = jnp.where(first if k < 5 else last, 0.0, r.rs[k].astype(F32))
        pack_s = put_col(pack_s, value, two_cols(0), k if k < 5 else 16 + k)
    r.ks[...] = pack_s.astype(BF16)
    stage = [new(r.ks, r.is_.at[0], (0, 1)), new(r.ks, r.is_.at[1], (0, -1))]
    start_all(stage)
    pack_c = pack_cols(lambda y: strided(cwide, y, 32), [(c, b + 2) for c, b in TWO])
    wait_all(other)
    for k in range(2):
        value = jnp.where(first if k < 1 else last, 0.0, r.rw[k].astype(F32))
        r.sw2[k] = value.astype(BF16)
        pack_w = put_col(pack_w, value, two_cols(0), 17 * k)
    r.kw[...] = pack_w.astype(BF16)
    for k in range(4):
        value = jnp.where(first if k < 2 else last, 0.0, r.rc[k].astype(F32))
        r.crows[k] = value.astype(BF16)
        pack_c = put_col(pack_c, value, TWO, k if k < 2 else 16 + k)
    r.kc[...] = pack_c.astype(BF16)
    other = [
        new(r.kw, r.iw.at[0], (0, 1)),
        new(r.kw, r.iw.at[1], (0, -1)),
        new(r.kc, r.ic.at[0], (0, 1)),
        new(r.kc, r.ic.at[1], (0, -1)),
    ]
    start_all(other)
    wait_all(stage)

    def summer_row(j):
        if j < 5:
            return jnp.where(first, 0.0, r.rs[j].astype(F32))
        if j >= 21:
            return jnp.where(last, 0.0, r.rs[j - 16].astype(F32))
        return strided(wide, j - 5, C)

    halo = other_side(r.is_[0].astype(F32), r.is_[1].astype(F32))
    build_x3(r.x3s, summer_row, halo, TR + 10, C)
    save_s = pltpu.make_async_copy(r.x3s, r.xs, r.lsem.at[PARTS])
    save_s.start()
    fp = r.fp
    strips = [getattr(r, f"strip{q}") for q in range(PARTS)]
    trios = [getattr(r, f"trio{q}") for q in range(PARTS)]
    pin, cand, psend, ptrio, send_buf = r.pin, r.cand, r.psend, r.ptrio, r.send_buf
    owns = [
        pltpu.make_async_copy(fp.at[pl.ds(0, 24), part_of(q)], strips[q].at[pl.ds(16, 24)], r.lsem.at[q])
        for q in range(PARTS)
    ]
    pstage = [new(fp.at[24], pin.at[0], (1, 0)), new(fp.at[25], pin.at[1], (-1, 0))]
    stages = []
    for q in range(PARTS):
        cs = part_of(q)
        stages.append(
            [
                new(fp.at[pl.ds(0, 16), cs], strips[q].at[pl.ds(0, 16)], (1, 0)),
                new(fp.at[pl.ds(8, 16), cs], strips[q].at[pl.ds(40, 16)], (-1, 0)),
            ]
        )
    for h in range(2):
        channels = slice(h * C // 2, (h + 1) * C // 2)
        packs = [jnp.zeros((C // 2, TC), F32), jnp.zeros((C // 2, TC), F32)]
        lane = lane_of((C // 2, TC))
        for n in range(6):
            value = conv_chunk(r.weight, r.x3s, n * 512, 512, channels)
            for j in range(4):
                k = n * 4 + j
                part = value[:, j * TC : (j + 1) * TC]
                if k < 4:
                    part = jnp.where(first, 0.0, part)
                if k >= 20:
                    part = jnp.where(last, 0.0, part)
                fp[k, channels] = part.astype(BF16)
                for p, at in ((0, k), (1, k - 8)):
                    if 0 <= at < 16:
                        low = (lane >= at * 8) & (lane < at * 8 + 4)
                        high = (lane >= at * 8 + 4) & (lane < at * 8 + 8)
                        packs[p] = jnp.where(low, rl(part, at * 8, 1), packs[p])
                        packs[p] = jnp.where(high, rl(part, at * 8 + 4 - 124, 1), packs[p])
        fp[24, channels] = packs[0].astype(BF16)
        fp[25, channels] = packs[1].astype(BF16)
        if h == 0:
            start_all(stages[0])
            start_all(stages[1])
        start_all(owns[h * PARTS // 2 : (h + 1) * PARTS // 2])
    start_all(pstage)
    lane = lane_of((C, TC))
    wait_all(other)
    whalo = other_side(r.iw[0].astype(F32), r.iw[1].astype(F32))
    left = jnp.where(col > 0, r.ic[0].astype(F32), 0.0)
    right = jnp.where(col < NCOL - 1, r.ic[1].astype(F32), 0.0)
    for k, tile in enumerate(three_tiles(left, r.kc[...].astype(F32), right)):
        r.ct[k] = tile.astype(BF16)

    def winter_row(j):
        if j == 0 or j == TR + 1:
            return r.sw2[j // (TR + 1)].astype(F32)
        return strided(wide2, j - 1, C)

    build_x3(r.x3w, winter_row, whalo, TR + 2, C)
    save_w = pltpu.make_async_copy(r.x3w, r.xw, r.lsem.at[PARTS + 1])
    save_w.start()
    wait_all(owns)
    off = r.off

    def pick_of(dcol):
        return offset_of(off, 0, row, lax.rem(col + dcol + NCOL, NCOL)) + 1

    wait_all(pstage)
    low = lane < 64
    p0, p1 = fp[24].astype(F32), fp[25].astype(F32)
    above, below = pin[0].astype(F32), pin[1].astype(F32)
    cand[0, 0] = above.astype(BF16)
    cand[0, 1] = jnp.where(low, p0, 0.0).astype(BF16)
    cand[1, 0] = p0.astype(BF16)
    cand[1, 1] = jnp.where(low, rl(p1, 64, 1), 0.0).astype(BF16)
    cand[2, 0] = rl(jnp.where(low, below, p1), 64, 1).astype(BF16)
    cand[2, 1] = jnp.where(low, rl(below, 64, 1), 0.0).astype(BF16)
    second = []
    for k, dcol in enumerate((-2, -1, 1, 2)):
        pick = pick_of(dcol)
        for j in range(2):
            psend[k, j] = cand[pick, j]
        second.append(new(psend.at[k], ptrio.at[2 - dcol], (0, dcol)))
    start_all(second)
    mine = pick_of(0)
    for j in range(2):
        ptrio[2, j] = cand[mine, j]
    picks = [pick_of(-1), pick_of(1)]
    my_row = row + offset_of(off, 0, row, col)
    my_col = col + offset_of(off, 1, row, col)
    dcol = my_col - col + 1
    thirds = []
    for q in range(PARTS):
        cs = part_of(q)
        wait_all(stages[q])
        if q + 2 < PARTS:
            start_all(stages[q + 2])

        def fill(j, carry, cs=cs, q=q):
            send_buf[0, j, cs] = strips[q][16 * picks[0] + j]
            send_buf[1, j, cs] = strips[q][16 * picks[1] + j]
            return carry

        lax.fori_loop(0, 24, fill, 0)
        third = [
            new(send_buf.at[0, :, cs], trios[q].at[2], (0, -1)),
            new(send_buf.at[1, :, cs], trios[q].at[0], (0, 1)),
        ]
        start_all(third)
        thirds.append(third)

        def keep(j, carry, q=q):
            trios[q][1, j] = strips[q][16 * mine + j]
            return carry

        lax.fori_loop(0, 24, keep, 0)
        for n in range(q * 4 // PARTS, (q + 1) * 4 // PARTS):
            at = slice(n * 512, (n + 1) * 512)
            r.fw[:, at] = conv_chunk(r.weight, r.x3w, n * 512, 512).astype(BF16)
        small_weights(r, q)
    wait_all(second)
    m = r.m
    low = lax.rem(lane, 8) < 4
    for j in range(2):
        right = jnp.where(my_col == NCOL - 1, 0.0, ptrio[dcol + 2, j].astype(F32))
        left = jnp.where(my_col == 0, 0.0, ptrio[dcol, j].astype(F32))
        m[:, (24 + j) * TC : (25 + j) * TC] = jnp.where(low, right, left).astype(BF16)
    for q in range(PARTS):
        wait_all(thirds[q])
        cs = part_of(q)
        for j in range(24):
            m[cs, j * TC : (j + 1) * TC] = trios[q][dcol, j]
    correlate(r.fw, m, r.cv, r.cvpack, r.sums, r.mt, r.rt, r.grim, r.s1, r.s2)
    save_s.wait()
    save_w.wait()


def forward(offsets, summer, winter, cot, weight, w_first, w_second):
    one = lambda c: pltpu.VMEM((c, TC), BF16)
    some = lambda n, c: pltpu.VMEM((n, c, TC), BF16)
    n = 16 + 6 + 4 * PARTS
    scratch = dict(
        wide=pltpu.VMEM((C * TR, TC), F32), wide2=pltpu.VMEM((C * TR, TC), F32), cwide=pltpu.VMEM((32 * TR, TC), F32),
        ss=tiles(10), rs=tiles(10), sw=tiles(2), sw2=tiles(2), rw=tiles(2), sc=some(4, 32), rc=some(4, 32),
        ks=tiles(), kw=tiles(), kc=one(32), is_=tiles(2), iw=tiles(2), ic=some(2, 32),
        x3s=pltpu.VMEM((3 * C, 26 * TC), BF16), x3w=pltpu.VMEM((3 * C, 18 * TC), BF16), fp=tiles(26),
        pin=tiles(2), cand=tiles(3, 2), send_buf=tiles(2, 24), ptrio=tiles(5, 2), psend=tiles(4, 2),
        mt=pltpu.VMEM((24 * TC, C), BF16), rt=pltpu.VMEM((2 * TC, C), BF16), grim=pltpu.VMEM((2 * TC, TR * TC), F32),
        s1=pltpu.VMEM((CH, TC), F32), s2=pltpu.VMEM((CH, TC), F32),
        lsem=dma(PARTS + 2), sems=dma(n), rsems=dma(n),
    )
    for q in range(PARTS):
        scratch[f"strip{q}"] = pltpu.VMEM((56, WIDE, TC), BF16)
        scratch[f"trio{q}"] = pltpu.VMEM((3, 24, WIDE, TC), BF16)
    return call(
        forward_kernel,
        dict(
            off=(offsets, sspec()), summer=(summer, vspec()), winter=(winter, vspec()), cot=(cot, vspec()),
            weight=(weight, vspec()), w_first=(w_first, vspec()), w_second=(w_second, vspec()),
        ),
        dict(
            w1=(sds((64, 9 * CH), BF16), vspec()), w1f=(sds((CH, 576), BF16), vspec()),
            w2f=(sds((64, 288), BF16), vspec()),
            crows=(sds((4, 32, TC), BF16), vspec()), ct=(sds((3, 32, TC), BF16), vspec()),
            xs=(sds((3 * C, 26 * TC), BF16), anyspec()), xw=(sds((3 * C, 18 * TC), BF16), anyspec()),
            fw=(sds((C, TR * TC), BF16), vspec()), m=(sds((C, 26 * TC), BF16), vspec()),
            cv=(sds((TR, CH, TC), F32), vspec()), cvpack=(sds((CH, TC), F32), vspec()),
            sums=(sds((8, 256), F32), vspec()),
        ),
        scratch,
        0,
    )


def bit_off(lane, bit):
    return (lane & bit) == 0


def shear(main, rim):
    low = lane_of((80, TC)) < 64
    w = jnp.where(low, jnp.concatenate([rim, main[0:72]], 0), jnp.concatenate([main[56:128], rim], 0))
    w = jnp.where(bit_off(lane_of((48, TC)), 32), w[0:48], w[32:80])
    w = jnp.where(bit_off(lane_of((32, TC)), 16), w[0:32], w[16:48])
    w = jnp.where(bit_off(lane_of((24, TC)), 8), w[0:24], w[8:32])
    lane = lane_of((16, TC))
    w = jnp.where(bit_off(lane, 4), rl(w, -4, 0)[0:16], w[8:24])
    w = jnp.where(bit_off(lane, 2), w, rl(w, -2, 0))
    w = jnp.where(bit_off(lane, 1), w, rl(w, -1, 0))
    return jnp.where(lax.broadcasted_iota(jnp.int32, (16, TC), 0) < 9, w, 0.0)


def unshear(value):
    lane = lane_of((16, TC))
    w = jnp.where(bit_off(lane, 1), value, rl(value, 1, 0))
    w = jnp.where(bit_off(lane, 2), w, rl(w, 2, 0))
    zeros = lambda n: jnp.zeros((n, TC), F32)
    padded = jnp.concatenate([w, zeros(8)], 0)
    w = jnp.where(bit_off(lane_of((24, TC)), 4), rl(padded, 4, 0), jnp.concatenate([zeros(8), w], 0))
    for n, bit in ((24, 8), (32, 16), (48, 32)):
        w = jnp.where(
            bit_off(lane_of((n + bit, TC)), bit),
            jnp.concatenate([w, zeros(bit)], 0),
            jnp.concatenate([zeros(bit), w], 0),
        )
    low = lambda n: lane_of((n, TC)) < 64
    main = jnp.concatenate(
        [
            jnp.where(low(56), w[8:64], 0.0),
            jnp.where(low(16), w[64:80], w[0:16]),
            jnp.where(low(56), 0.0, w[16:72]),
        ],
        0,
    )
    return main, jnp.where(low(8), w[0:8], w[72:80])


def row_sums(first, second):
    ones = jnp.ones((8, TC), F32)
    a = lax.dot_general(ones, first, NT, precision=lax.Precision.HIGHEST, preferred_element_type=F32)
    b = lax.dot_general(ones, second, NT, precision=lax.Precision.HIGHEST, preferred_element_type=F32)
    return jnp.where(lax.broadcasted_iota(jnp.int32, a.shape, 0) == 0, a, b)


def correlate(fw, m, cv, pack, sums, mt, rt, grim, s1, s2):
    for r in range(24):
        mt[r * TC : (r + 1) * TC, :] = m[:, r * TC : (r + 1) * TC].T
    for q in range(2):
        rt[q * TC : (q + 1) * TC, :] = m[:, (24 + q) * TC : (25 + q) * TC].T
    for n in range(4):
        grim[:, n * 512 : (n + 1) * 512] = dot(rt[...], fw[:, n * 512 : (n + 1) * 512])
    s1[...] = jnp.zeros_like(s1)
    s2[...] = jnp.zeros_like(s2)

    def at_pair(pair, carry):
        feat = fw[:, pl.ds(pl.multiple_of(pair * 2 * TC, 2 * TC), 2 * TC)]
        for t in range(10):
            mains = dot(mt[pl.ds(pl.multiple_of((pair * 2 + t) * TC, TC), TC), :], feat)
            for k in range(2):
                a = t - k
                if a < 0 or a > 8:
                    continue
                y = pair * 2 + k
                lanes = pl.ds(pl.multiple_of(y * TC, TC), TC)
                rim = grim[pl.ds(pl.multiple_of((y + a) * 8, 8), 8), lanes]
                value = shear(mains[:, k * TC : (k + 1) * TC], rim) * 0.0625
                rows = slice(a * 16, (a + 1) * 16)
                cv[y, rows, :] = value
                s1[rows, :] += value
                s2[rows, :] += value * value
        return carry

    lax.fori_loop(0, TR // 2, at_pair, 0)
    pack[...] = pack_cols(lambda y: cv[y], [(c, b + 2) for c, b in TWO])
    sums[...] = jnp.zeros_like(sums)
    sums[:, 0:CH] = row_sums(s1[...], s2[...])


def reduce_one(src, dst, out, send, recv, axis, count):
    copies = []
    for d in range(1, count):
        step = (0, d) if axis == "col" else (d, 0)
        copies.append(
            pltpu.make_async_remote_copy(
                src_ref=src,
                dst_ref=dst.at[d],
                send_sem=send.at[d],
                recv_sem=recv.at[d],
                device_id=device_at(*step),
                device_id_type=MESH,
            )
        )
    start_all(copies)
    dst[0] = src[...]
    wait_all(copies)
    me = lax.axis_index(axis)
    total = None
    for d in range(count):
        value = dst[lax.rem(me - d + count, count)]
        total = value if total is None else total + value
    out[...] = total


RING = [(0, d) for d in range(1, NCOL)] + [(d, 0) for d in range(1, NROW)]


def tile_inside(b, shape):
    lane = lane_of(shape)
    row = lax.axis_index("row")
    col = lax.axis_index("col")
    local = jnp.where(lane < 64, lane, lane - 64)
    y = row * TR - 2 + local
    x = jnp.where(lane < 64, col * TC - 1 + b, col * TC + TC + b)
    return (y >= 0) & (y < NROW * TR) & (x >= 0) & (x < NCOL * TC) & (local < 20)


def rim_patches(tiles, a):
    return jnp.concatenate([rl(t, -a, 1) for t in tiles], 0).astype(BF16)


def silu_parts(value):
    sigma = jax.nn.sigmoid(value)
    return value * sigma, sigma * (1.0 + value * (1.0 - sigma))


def columns(sums):
    turned = sums.T
    return turned[0:CH, 0:1], turned[0:CH, 1:2]


def refine(r, scale, bias, inv, mid):
    row = lax.axis_index("row")
    first = row == 0
    last = row == NROW - 1
    cv, vrows, own_pack, sides, cot, crows, ct = r.cv, r.vrows, r.own_pack, r.sides, r.cot, r.crows, r.ct
    w1, w1f, w2, w2f = r.w1, r.w1f, r.w2, r.w2f
    refined, gpre, gfirst, gsecond, sums = r.refined, r.gpre, r.gfirst, r.gsecond, r.gsums0
    cwide, n3x, c3x, h3, gh3, hpre, gmain = r.cwide, r.n3x, r.c3x, r.h3, r.gh3, r.hpre, r.gmain
    s1, s2, rwide = r.s1, r.s2, r.rwide

    def normed_of(value):
        return silu_parts(value * scale + bias)[0]

    ntiles = [
        jnp.where(tile_inside(b - 1, (CH, TC)), normed_of(t), 0.0) for b, t in enumerate(three_tiles(sides[0], own_pack[...], sides[1]))
    ]

    def nrow(k):
        if k < 2:
            return jnp.where(first, 0.0, normed_of(vrows[k]))
        if k >= 18:
            return jnp.where(last, 0.0, normed_of(vrows[k - 16]))
        return normed_of(cv[k - 2])

    build_x3(n3x, nrow, ntiles[1], 20, CH)
    ctiles = [ct[k].astype(F32) for k in range(3)]
    cwide[...] = cot[...].astype(F32)

    def crow(k):
        if k < 2:
            return crows[k].astype(F32)
        if k >= 18:
            return crows[k - 16].astype(F32)
        return strided(cwide, k - 2, 32)

    build_x3(c3x, crow, ctiles[1], 20, 32)

    def both(w_ref, x3, tiles):
        depth = x3.shape[0]
        rim = None
        for a in range(3):
            term = dot(w_ref[:, a * depth : (a + 1) * depth], rim_patches(tiles, a))
            rim = term if rim is None else rim + term
        return rim

    lane = lane_of((64, TC))
    local = jnp.where(lane < 64, lane, lane - 64)
    ypos = row * TR - 1 + local
    col = lax.axis_index("col")
    xpos = jnp.where(lane < 64, col * TC - 1, col * TC + TC)
    rim_in = (ypos >= 0) & (ypos < NROW * TR) & (local < 18) & (xpos >= 0) & (xpos < NCOL * TC)
    rim_h, rim_slope = silu_parts(both(w1, n3x, ntiles))
    rim_g = both(w2f, c3x, ctiles)
    rim_h = jnp.where(rim_in, rim_h, 0.0)
    rim_g = jnp.where(rim_in, rim_g * rim_slope, 0.0)
    for n in range(6):
        hpre[:, n * 384 : (n + 1) * 384] = conv_chunk(w1, n3x, n * 384, 384)
        gmain[:, n * 384 : (n + 1) * 384] = conv_chunk(w2f, c3x, n * 384, 384)

    def edge(k):
        return first if k == 0 else (last if k == 17 else None)

    def hrow(k):
        value, slope = silu_parts(hpre[:, k * TC : (k + 1) * TC])
        grad = gmain[:, k * TC : (k + 1) * TC] * slope
        gone = edge(k)
        if gone is not None:
            value = jnp.where(gone, 0.0, value)
            grad = jnp.where(gone, 0.0, grad)
        gmain[:, k * TC : (k + 1) * TC] = grad
        return value

    build_x3(h3, hrow, rim_h, 18, 64)
    build_x3(gh3, lambda k: gmain[:, k * TC : (k + 1) * TC], rim_g, 18, 64)
    for n in range(4):
        value = conv_chunk(w2, h3, n * 512, 512)
        for j in range(4):
            rwide[pl.ds(n * 4 + j, 32, stride=TR), :] = value[:, j * TC : (j + 1) * TC]
    refined[...] = rwide[...].astype(BF16)
    own = slice(TC, 17 * TC)
    mine = slice(2 * TC, 18 * TC)
    gfirst[:, 9 * CH :] = jnp.zeros((64, 1408 - 9 * CH), F32)
    gsecond[:, 576:] = jnp.zeros((32, 64), F32)
    for a in range(3):
        gsecond[:, a * 192 : (a + 1) * 192] = dot_nt(c3x[32:64, mine], h3[:, a * TC : (a + 16) * TC])
        gfirst[:, a * 432 : (a + 1) * 432] = dot_nt(gh3[64:128, own], n3x[:, (a + 1) * TC : (a + 17) * TC])
    s1[...] = jnp.zeros_like(s1)
    s2[...] = jnp.zeros_like(s2)
    for n in range(4):
        value = conv_chunk(w1f, gh3, n * 512, 512)
        for j in range(4):
            y = n * 4 + j
            volume = cv[y]
            grad = value[:, j * TC : (j + 1) * TC] * silu_parts(volume * scale + bias)[1]
            gpre[y] = grad
            s1[...] += grad
            s2[...] += grad * (volume * inv - mid)
    sums[...] = jnp.zeros_like(sums)
    sums[:, 0:CH] = row_sums(s1[...], s2[...])


def correlate_back(cv, gpre, coef, fw, m, gfw, gm, kw, q, qrim):
    def at_row(y, carry):
        lanes = pl.ds(pl.multiple_of(y * TC, TC), TC)
        grad = coef[0] * gpre[y] + coef[1] + coef[2] * cv[y]
        grad = grad.astype(BF16).astype(F32)
        for a in range(9):
            main, rim = unshear(grad[a * 16 : (a + 1) * 16])
            q[pl.ds(pl.multiple_of((y + a) * TC, TC), TC), lanes] = main.astype(BF16)
            qrim[pl.ds(pl.multiple_of((y + a) * 8, 8), 8), lanes] = rim
        return carry

    qrim[...] = jnp.zeros_like(qrim)
    for y in range(TR):
        for p in (y - 1, y + 9):
            if 0 <= p < 24:
                q[p * TC : (p + 1) * TC, y * TC : (y + 1) * TC] = jnp.zeros((TC, TC), BF16)
    lax.fori_loop(0, TR, at_row, 0)
    for y in range(0, TR, 2):
        at = slice(y * TC, (y + 2) * TC)
        value = dot(m[:, y * TC : (y + 10) * TC], q[y * TC : (y + 10) * TC, at])
        value = value + dot(m[:, 24 * TC : 26 * TC], qrim[:, at].astype(BF16))
        gfw[:, at] = (value * 0.0625).astype(BF16)
    for p in range(0, 24, 2):
        at = slice(max(0, p - 8) * TC, (min(15, p + 1) + 1) * TC)
        value = dot_nt(fw[:, at], q[p * TC : (p + 2) * TC, at]) * 0.0625
        for k in range(2):
            gm[p + k] = value[:, k * TC : (k + 1) * TC].astype(BF16)
    kw[...] = pack_cols(lambda y: gfw[:, y * TC : (y + 1) * TC].astype(F32), two_cols(1)).astype(BF16)
    for k in range(2):
        value = dot_nt(fw[...], qrim[k * TC : (k + 1) * TC, :].astype(BF16))
        gm[24 + k] = (value * 0.0625).astype(BF16)


def middle_kernel(r):
    arrived = greet(RING)
    new = numbered(r.sems, r.rsems)
    arrived()
    rows = [
        new(r.cv.at[pl.ds(14, 2)], r.vrows.at[pl.ds(0, 2)], (1, 0)),
        new(r.cv.at[pl.ds(0, 2)], r.vrows.at[pl.ds(2, 2)], (-1, 0)),
    ]
    start_all(rows)
    reduce_one(r.sums, r.gcol, r.total, r.csend, r.crecv, "col", NCOL)
    wait_all(rows)
    pack = r.cvpack[...]
    for k in range(4):
        pack = put_col(pack, r.vrows[k], TWO, k if k < 2 else 16 + k)
    r.own_pack[...] = pack
    cols = [new(r.own_pack, r.sides.at[0], (0, 1)), new(r.own_pack, r.sides.at[1], (0, -1))]
    start_all(cols)
    reduce_one(r.total, r.grow, r.total2, r.rsend, r.rrecv, "row", NROW)
    wait_all(cols)
    sum1, sum2 = columns(r.total2[...])
    mean = sum1 / PIXELS
    inv = lax.rsqrt(sum2 / PIXELS - mean * mean + 1e-05)
    shape = (CH, TC)
    spread = jnp.where(
        lax.broadcasted_iota(jnp.int32, (CH, 81), 1) == padded_place((CH, 1), 0), 1.0, 0.0
    )
    gain, shift = (jnp.sum(spread * ref[...].reshape(1, 81), axis=1, keepdims=True) for ref in (r.gain, r.shift))
    scale = jnp.broadcast_to(gain * inv, shape)
    mid = jnp.broadcast_to(mean * inv, shape)
    inv = jnp.broadcast_to(inv, shape)
    refine(r, scale, shift - mean * scale, inv, mid)
    reduce_one(r.gsums0, r.gcol2, r.total3, r.csend2, r.crecv2, "col", NCOL)
    reduce_one(r.total3, r.grow2, r.gsums, r.rsend2, r.rrecv2, "row", NROW)
    grad_shift, grad_gain = columns(r.gsums[...])
    narrow = jnp.where(
        lax.broadcasted_iota(jnp.int32, (81, CH), 0) == padded_place((1, CH), 1), 1.0, 0.0
    )
    r.gnorm[...] = lax.dot_general(
        r.gsums[:, 0:CH], narrow, NT, precision=lax.Precision.HIGHEST, preferred_element_type=F32
    )
    slope = -scale * grad_gain / PIXELS
    coef = (scale, -scale * grad_shift / PIXELS - slope * mid, slope * inv)
    correlate_back(r.cv, r.gpre, coef, r.fw, r.m, r.gfw, r.gm, r.gkw, r.q, r.qrim)


def middle(fore, cot, gain, shift, w2):
    f32 = lambda *n: pltpu.VMEM(n, F32)
    bf16 = lambda *n: pltpu.VMEM(n, BF16)
    return call(
        middle_kernel,
        {
            name: (array, vspec())
            for name, array in dict(
                cv=fore.cv, cvpack=fore.cvpack, sums=fore.sums, crows=fore.crows, ct=fore.ct, fw=fore.fw, m=fore.m,
                cot=cot, gain=gain, shift=shift, w1=fore.w1, w1f=fore.w1f, w2=w2, w2f=fore.w2f,
            ).items()
        },
        {
            name: (sds(shape, kind), vspec())
            for name, shape, kind in (
                ("refined", (32 * TR, TC), BF16),
                ("gfirst", (64, 1408), F32),
                ("gsecond", (32, 640), F32),
                ("gnorm", (8, 81), F32),
                ("gfw", (C, TR * TC), BF16),
                ("gm", (26, C, TC), BF16),
                ("gkw", (C, TC), BF16),
            )
        },
        dict(
            vrows=f32(4, CH, TC), own_pack=f32(CH, TC), sides=f32(2, CH, TC),
            gcol=f32(NCOL, 8, 256), grow=f32(NROW, 8, 256), total=f32(8, 256), total2=f32(8, 256),
            gcol2=f32(NCOL, 8, 256), grow2=f32(NROW, 8, 256), gsums0=f32(8, 256), gsums=f32(8, 256), total3=f32(8, 256),
            cwide=f32(32 * TR, TC), n3x=bf16(3 * CH, 20 * TC), c3x=bf16(96, 20 * TC), h3=bf16(192, 18 * TC),
            gh3=bf16(192, 18 * TC), hpre=f32(64, 18 * TC), gmain=f32(64, 18 * TC), s1=f32(CH, TC), s2=f32(CH, TC),
            rwide=f32(32 * TR, TC), gpre=f32(TR, CH, TC), q=bf16(24 * TC, TR * TC), qrim=f32(2 * TC, TR * TC),
            sems=dma(4), rsems=dma(4),
            csend=dma(NCOL), crecv=dma(NCOL), rsend=dma(NROW), rrecv=dma(NROW),
            csend2=dma(NCOL), crecv2=dma(NCOL), rsend2=dma(NROW), rrecv2=dma(NROW),
        ),
        1,
    )


TILES = 384
HALF = TILES // 2
FIRST = 128
SHARE = FIRST // 4


def feat_tile(t, g):
    return (g // 8) * HALF + t * 8 + g % 8


def first_tile(t, g):
    return (g // 2) * HALF + 144 + t * 2 + g % 2


def second_tile(t, g):
    return g * HALF + 166 + t


def final_kernel(r):
    row = lax.axis_index("row")
    col = lax.axis_index("col")
    core = lax.rem(col, 2)
    chip = lax.div(col, 2)
    off, gm, gfw = r.off, r.gm, r.gfw
    trios = [getattr(r, f"trio{q}") for q in range(PARTS)]
    ptrio, strip, be, ab, pout, pin, g24, g5 = r.ptrio, r.strip, r.be, r.ab, r.pout, r.pin, r.g24, r.g5
    pab, pq, pack, side, rw, kw, iw, kw0 = r.pab, r.pq, r.pack, r.side, r.rw, r.kw, r.iw, r.gkw
    ext, wrows, buf, half_in, half, y_in = r.ext, r.wrows, r.buf, r.half_in, r.half, r.y_in
    share, row_in, full, x3, wide, flipped = r.share, r.row_in, r.full, r.x3, r.wide, r.flipped
    xw, xs = r.xw_here, r.xs_here
    arrived = greet(RING)
    loads = [
        pltpu.make_async_copy(r.xw, xw, r.lsem.at[PARTS]),
        pltpu.make_async_copy(r.xs, xs, r.lsem.at[PARTS + 1]),
    ]
    owns = [
        pltpu.make_async_copy(gm.at[pl.ds(0, 24), part_of(q)], trios[q].at[1, pl.ds(0, 24)], r.lsem.at[q])
        for q in range(PARTS)
    ]
    start_all(owns)
    start_all(loads)
    new = numbered(r.sems, r.rsems)
    for t in range(11):
        for g in range(4):
            buf[first_tile(t, g)] = r.gfirst[g * 16 : (g + 1) * 16, t * TC : (t + 1) * TC].astype(BF16)
    for t in range(5):
        for g in range(2):
            buf[second_tile(t, g)] = r.gsecond[g * 16 : (g + 1) * 16, t * TC : (t + 1) * TC].astype(BF16)
    for h in range(2):
        for t in range(171, HALF):
            buf[h * HALF + t] = jnp.zeros((16, TC), BF16)
    partner = (row, col + 1 - 2 * core)
    pairs = [
        new(buf.at[pl.ds(HALF * (1 - core) + 48 * p, 48)], half_in.at[pl.ds(48 * p, 48)], device=partner)
        for p in range(4)
    ]
    arrived()
    pstage = [new(gm.at[pl.ds(24, 2)], ptrio.at[0], (0, 1)), new(gm.at[pl.ds(24, 2)], ptrio.at[2], (0, -1))]
    wstage = [
        new(gfw.at[:, pl.ds((TR - 1) * TC, TC)], rw.at[0], (1, 0)),
        new(gfw.at[:, pl.ds(0, TC)], rw.at[1], (-1, 0)),
    ]
    start_all(pstage + wstage)
    start_all(pairs[3:])
    stages = []
    for q in range(PARTS):
        cs = part_of(q)
        stages.append(
            [
                new(gm.at[pl.ds(0, 24), cs], trios[q].at[0, pl.ds(0, 24)], (0, 1)),
                new(gm.at[pl.ds(0, 24), cs], trios[q].at[2, pl.ds(0, 24)], (0, -1)),
            ]
        )
    start_all(stages[0])
    start_all(stages[1])
    for q in range(PARTS):
        for k in range(3):
            trios[q][k, 24] = jnp.zeros((WIDE, TC), BF16)
    for k in range(9):
        flipped[:, k * C : (k + 1) * C] = r.weight[:, (8 - k) * C : (9 - k) * C].T
    wait_all(owns)
    sources = []
    for k in range(3):
        place = col + k - 1
        there = lax.rem(place + NCOL, NCOL)
        drow = offset_of(off, 0, row, there)
        dcol = offset_of(off, 1, row, there)
        good = (dcol == 1 - k) & (place >= 0) & (place < NCOL)
        sources.append((drow, good))

    first, last = row == 0, row == NROW - 1
    zero = jnp.zeros((C, TC), F32)
    lane = lane_of((C, TC))
    low = lane < 64

    def only(flag, ref):
        return jnp.where(flag, ref.astype(F32), 0.0)

    wait_all(pstage)
    to_above, own0, own1, to_below = zero, zero, zero, zero
    for k, (drow, good) in enumerate(sources):
        t0, t1 = (gm[24], gm[25]) if k == 1 else (ptrio[k, 0], ptrio[k, 1])
        t0, t1 = t0.astype(F32), jnp.where(low, t1.astype(F32), 0.0)
        up, level, down = (good & (drow == v) for v in (-1, 0, 1))
        turned0, turned1 = rl(t0, 64, 1), rl(t1, 64, 1)
        to_above += jnp.where(up, t0, 0.0)
        own0 += jnp.where(up, t1, 0.0) + jnp.where(level, t0, 0.0)
        own1 += jnp.where(level, turned1, 0.0) + jnp.where(down & jnp.logical_not(low), turned0, 0.0)
        to_below += jnp.where(down, turned1 + jnp.where(low, turned0, 0.0), 0.0)
    pout[0] = to_above.astype(BF16)
    pout[1] = to_below.astype(BF16)
    pstage = [new(pout.at[0], pin.at[0], (-1, 0)), new(pout.at[1], pin.at[1], (1, 0))]
    start_all(pstage)

    wait_all(wstage)
    kpack = kw0[...].astype(F32)
    for k in range(2):
        value = only(jnp.logical_not(first if k == 0 else last), rw[k])
        wrows[k] = value.astype(BF16)
        kpack = put_col(kpack, value, two_cols(0), 17 * k)
    kw[...] = kpack.astype(BF16)
    wstage = [new(kw, iw.at[0], (0, 1)), new(kw, iw.at[1], (0, -1))]
    start_all(wstage)

    thirds = []
    for q in range(PARTS):
        cs = part_of(q)
        wait_all(stages[q])
        if q + 2 < PARTS:
            start_all(stages[q + 2])

        def gather(p, carry, cs=cs, q=q):
            total = None
            for k, (drow, good) in enumerate(sources):
                j = p - 16 * (drow + 1)
                fits = good & (j >= 0) & (j < 24)
                value = trios[q][k, jnp.where(fits, j, 24)].astype(F32)
                total = value if total is None else total + value
            strip[p, cs] = total.astype(BF16)
            return carry

        lax.fori_loop(0, 56, gather, 0)
        third = [
            new(strip.at[pl.ds(0, 16), cs], be.at[:, cs], (-1, 0)),
            new(strip.at[pl.ds(40, 16), cs], ab.at[:, cs], (1, 0)),
        ]
        start_all(third)
        thirds.append(third)
        if q == 0:
            wait_all(loads)
        if q < 3:
            for n in range(3):
                part = slice(n * C, (n + 1) * C)
                at = slice(q * 768 + n * C, q * 768 + (n + 1) * C)
                r.gfeat[:, at] = dot_nt(gfw[...], xw[part, q * TC : (q + 16) * TC])
    wait_all(wstage)
    whalo = other_side(iw[0].astype(F32), iw[1].astype(F32))
    wait_all(pstage)
    not_first, not_last = row > 0, row < NROW - 1
    p0 = own0 + only(not_last, pin[0])
    p1 = own1 + only(not_first, pin[1])
    tile_a = p0 + jnp.where(low, 0.0, rl(p1, 64, 1))
    tile_b = jnp.where(low, rl(p1, 64, 1), 0.0)
    pab[0] = tile_a.astype(BF16)
    pab[1] = tile_b.astype(BF16)
    fourth = [new(pab.at[0], pq.at[0], (-1, 0)), new(pab.at[1], pq.at[1], (1, 0))]
    start_all(fourth)

    def w_row(k):
        if k == 0 or k == TR + 1:
            return wrows[k // (TR + 1)].astype(F32)
        return gfw[:, (k - 1) * TC : k * TC].astype(F32)

    build_x3(x3, w_row, whalo, TR + 2, C)

    def last_conv(n):
        value = conv_chunk(flipped, x3, n * 512, 512)
        for j in range(4):
            wide[pl.ds(n * 4 + j, C, stride=TR), :] = value[:, j * TC : (j + 1) * TC]

    for q in range(PARTS):
        cs = part_of(q)
        wait_all(thirds[q])
        for k in range(24):
            total = strip[16 + k, cs].astype(F32)
            if k < 16:
                total = total + only(not_last, be[k, cs])
            if k >= 8:
                total = total + only(not_first, ab[k - 8, cs])
            g24[k, cs] = total.astype(BF16)
        more = [
            new(g24.at[pl.ds(0, 5), cs], g5.at[1, :, cs], (-1, 0)),
            new(g24.at[pl.ds(19, 5), cs], g5.at[0, :, cs], (1, 0)),
        ]
        start_all(more)
        fourth = fourth + more
        for n in range(q * 4 // PARTS, (q + 1) * 4 // PARTS):
            last_conv(n)
    r.out_w[...] = wide[...].astype(BF16)
    wait_all(fourth)
    tile_a = tile_a + jnp.where((lane >= 24) & (lane < 64), only(not_first, pq[1]), 0.0)
    tile_b = tile_b + jnp.where(lane < 40, only(not_last, pq[0]), 0.0)
    pack[0] = tile_a.astype(BF16)
    pack[1] = tile_b.astype(BF16)
    total = zero
    for k in range(18):
        value = g24[k + 3].astype(F32)
        if k < 5:
            value = value + only(not_first, g5[0, k])
        if k >= 13:
            value = value + only(not_last, g5[1, k - 13])
        if k == 0:
            value = only(not_first, value)
        if k == 17:
            value = only(not_last, value)
        strip[k] = value.astype(BF16)
        total = put_col(total, value, two_cols(0), k)
    pack[2] = total.astype(BF16)
    stage = [new(pack, side.at[0], (0, 1)), new(pack, side.at[1], (0, -1))]
    start_all(stage)
    source = lax.broadcasted_iota(jnp.int32, (2 * TC, TC), 0)
    target = lax.broadcasted_iota(jnp.int32, (2 * TC, TC), 1)
    take = ((target < 18) & (source == (target + 3) * 8 + 7)) | (
        (target >= 64) & (target < 82) & (source == (target - 61) * 8)
    )
    rims = dot(pack[0], take[0:TC].astype(F32).astype(BF16)) + dot(pack[1], take[TC:].astype(F32).astype(BF16))
    wait_all(stage)
    halo = other_side(side[0, 2].astype(F32), side[1, 2].astype(F32))
    halo = halo + jnp.where(low, only(col > 0, rims), only(col < NCOL - 1, rims))
    at = jnp.where(low, lane, lane - 64)
    gone = (first & (at == 0)) | (last & (at == 17))
    shalo = jnp.where(gone, 0.0, halo)
    for k in range(18):
        p, base = ((0, (k + 3) * 8) if k + 3 < 16 else (1, (k - 13) * 8))
        value = strip[k].astype(F32)
        left = rl(only(col > 0, side[0, p]), -base, 1)
        right = rl(only(col < NCOL - 1, side[1, p]), 120 - base, 1)
        extra = jnp.where(lane < 4, left, 0.0) + jnp.where(lane >= 124, right, 0.0)
        if k == 0:
            extra = only(not_first, extra)
        if k == 17:
            extra = only(not_last, extra)
        ext[:, k * TC : (k + 1) * TC] = (value + extra).astype(BF16)
    for a in range(3):
        at = slice((a + 4) * TC, (a + 20) * TC)
        for n in range(3):
            part = slice(n * C, (n + 1) * C)
            into = slice(a * 768 + n * C, a * 768 + (n + 1) * C)
            value = r.gfeat[:, into] + dot_nt(ext[:, TC : 17 * TC], xs[part, at])
            value = value.astype(BF16)
            for t in range(2):
                for g in range(16):
                    buf[feat_tile(a * 6 + n * 2 + t, g)] = value[g * 16 : (g + 1) * 16, t * TC : (t + 1) * TC]
        start_all(pairs[a : a + 1])
    wait_all(pairs)

    def add_half(k, carry):
        half[k] = (buf[HALF * core + k].astype(F32) + half_in[k].astype(F32)).astype(BF16)
        return carry

    lax.fori_loop(0, HALF, add_half, 0)
    copies = []
    for d in range(1, 4):
        there = lax.rem(chip + d, 4)
        copies.append(new(half.at[pl.ds(SHARE * there, SHARE)], y_in.at[d - 1], device=(row, 2 * there + core)))
    for d in range(1, NROW):
        there = lax.rem(row + d, NROW)
        copies.append(new(half.at[pl.ds(FIRST + 4 * there, 4)], row_in.at[d - 1], device=(there, col)))
    start_all(copies)
    build_x3(x3, lambda k: ext[:, k * TC : (k + 1) * TC].astype(F32), shalo, TR + 2, C)
    last_conv(0)
    wait_all(copies)

    def add_share(k, carry):
        total = half[SHARE * chip + k].astype(F32)
        for d in range(3):
            total = total + y_in[d, k].astype(F32)
        share[k] = total.astype(BF16)
        return carry

    lax.fori_loop(0, SHARE, add_share, 0)
    for k in range(4):
        total = half[FIRST + 4 * row + k].astype(F32)
        for d in range(NROW - 1):
            total = total + row_in[d, k].astype(F32)
        r.part_b[k] = total.astype(BF16)
    copies = []
    for d in range(1, NROW):
        there = lax.rem(row + d, NROW)
        copies.append(new(share.at[pl.ds(2 * there, 2)], r.a_in.at[d - 1], device=(there, col)))
    for d in range(1, 4):
        there = lax.rem(chip + d, 4)
        copies.append(new(r.part_b.at[pl.ds(there, 1)], r.b_in.at[d - 1], device=(row, 2 * there + core)))
    start_all(copies)
    last_conv(1)
    r.padding[...] = padding_matrix()
    wait_all(copies)
    spot_a = HALF * core + SHARE * chip
    spot_b = HALF * core + FIRST + 4 * row
    for k in range(2):
        total = share[2 * row + k].astype(F32)
        for d in range(NROW - 1):
            total = total + r.a_in[d, k].astype(F32)
        full[spot_a + 2 * row + k] = total.astype(BF16)
    total = r.part_b[chip].astype(F32)
    for d in range(3):
        total = total + r.b_in[d, 0].astype(F32)
    full[spot_b + chip] = total.astype(BF16)

    def spread_along(mine, rows):
        if rows:
            return [new(mine, mine, device=(lax.rem(row + d, NROW), col)) for d in range(1, NROW)]
        return [new(mine, mine, device=(row, 2 * lax.rem(chip + d, 4) + core)) for d in range(1, 4)]

    copies = spread_along(full.at[pl.ds(spot_a + 2 * row, 2)], True)
    copies += spread_along(full.at[pl.ds(spot_b + chip, 1)], False)
    start_all(copies)
    last_conv(2)
    wait_all(copies)
    copies = spread_along(full.at[pl.ds(spot_a, SHARE)], False)
    copies += spread_along(full.at[pl.ds(spot_b, 4)], True)
    start_all(copies)
    last_conv(3)
    r.out_s[...] = wide[...].astype(BF16)
    wait_all(copies)
    mine = full.at[pl.ds(HALF * core, HALF)]
    pair = new(mine, mine, device=partner)
    pair.start()
    pair.wait()
    for t in range(18):
        for g in range(16):
            r.feat_out[g * 16 : (g + 1) * 16, t * TC : (t + 1) * TC] = full[feat_tile(t, g)].astype(F32)
    for t in range(11):
        for g in range(4):
            r.firstb[g * 16 : (g + 1) * 16, t * TC : (t + 1) * TC] = full[first_tile(t, g)]
    r.first_out[...] = dot_nt(r.firstb[:, 0 : 9 * CH], r.padding[...])
    for t in range(5):
        width = TC if t < 4 else 64
        for g in range(2):
            r.second_out[g * 16 : (g + 1) * 16, t * TC : t * TC + width] = full[second_tile(t, g)][:, :width].astype(F32)


def final(offsets, fore, mid, weight):
    small = lambda *n: pltpu.VMEM(n + (16, TC), BF16)
    n = 14 + 6 * PARTS + 5 + 4 * (NROW - 1 + 3)
    scratch = dict(
        ptrio=tiles(3, 2), strip=tiles(56), be=tiles(16), ab=tiles(16), pout=tiles(2), pin=tiles(2), g24=tiles(24),
        g5=tiles(2, 5), pab=tiles(2), pq=tiles(2), pack=tiles(3), side=tiles(2, 3), rw=tiles(2), kw=tiles(), iw=tiles(2),
        wrows=tiles(2), ext=pltpu.VMEM((C, 18 * TC), BF16), flipped=pltpu.VMEM((C, 9 * C), BF16),
        gfeat=pltpu.VMEM((C, 9 * C), F32), x3=pltpu.VMEM((3 * C, 18 * TC), BF16), wide=pltpu.VMEM((C * TR, TC), F32),
        xw_here=pltpu.VMEM((3 * C, 18 * TC), BF16), xs_here=pltpu.VMEM((3 * C, 26 * TC), BF16),
        buf=small(TILES), half_in=small(HALF), half=small(HALF), y_in=small(3, SHARE), share=small(SHARE),
        row_in=small(NROW - 1, 4), a_in=small(NROW - 1, 2), b_in=small(3, 1), part_b=small(4), full=small(TILES),
        firstb=pltpu.VMEM((64, 1408), BF16), padding=pltpu.VMEM((729, 9 * CH), BF16),
        lsem=dma(PARTS + 2), sems=dma(n), rsems=dma(n),
    )
    for q in range(PARTS):
        scratch[f"trio{q}"] = pltpu.VMEM((3, 25, WIDE, TC), BF16)
    return call(
        final_kernel,
        dict(
            off=(offsets, sspec()), gm=(mid.gm, vspec()), gfw=(mid.gfw, vspec()), gkw=(mid.gkw, vspec()),
            gfirst=(mid.gfirst, vspec()), gsecond=(mid.gsecond, vspec()), weight=(weight, vspec()),
            xw=(fore.xw, anyspec()), xs=(fore.xs, anyspec()),
        ),
        dict(
            out_w=(sds((C * TR, TC), BF16), vspec()), out_s=(sds((C * TR, TC), BF16), vspec()),
            feat_out=(sds((C, 9 * C), F32), vspec()), first_out=(sds((64, 729), F32), vspec()),
            second_out=(sds((32, 576), F32), vspec()),
        ),
        scratch,
        2,
    )


def body(winter, summer, offsets, feat_weight, bn_gain, bn_shift, w_first, w_second, cotangent):
    cot = cotangent.reshape(32 * TR, TC)
    fore = forward(offsets, summer.reshape(C * TR, TC), winter.reshape(C * TR, TC), cot, feat_weight, w_first, w_second)
    mid = middle(fore, cot, bn_gain, bn_shift, w_second)
    last = final(offsets, fore, mid, feat_weight)
    return (
        mid.refined.reshape(32, TR, TC),
        last.out_w.reshape(C, TR, TC),
        last.out_s.reshape(C, TR, TC),
        last.feat_out,
        last.first_out,
        last.second_out,
        mid.gnorm[1],
        mid.gnorm[0],
    )


def solution(mesh):
    tile = P(None, "row", "col")
    return jax.shard_map(
        body,
        mesh=mesh,
        in_specs=(tile, tile, P(), P(), P(), P(), P(), P(), tile),
        out_specs=(tile, tile, tile, P(), P(), P(), P(), P()),
        check_vma=False,
    )
```

```python
import types

import jax
import jax.numpy as jnp
from jax import lax
from jax.experimental import pallas as pl
from jax.experimental.pallas import tpu as pltpu
from jax.sharding import PartitionSpec as P

MESH = pl.DeviceIdType.MESH
C = 256
TR = 16
TC = 128
CH = 144
NROW = 16
NCOL = 8
PIXELS = 262144.0
F32 = jnp.float32
BF16 = jnp.bfloat16
VMEM_LIMIT = 58 * 1024 * 1024
NT = (((1,), (1,)), ((), ()))


def vspec():
    return pl.BlockSpec(memory_space=pltpu.VMEM)


def sspec():
    return pl.BlockSpec(memory_space=pltpu.SMEM)


def sds(shape, dtype):
    return jax.ShapeDtypeStruct(shape, dtype)


def anyspec():
    return pl.BlockSpec(memory_space=pl.ANY)


def call(kernel, ins, outs, scratch, collective_id):
    names = list(ins) + list(outs) + list(scratch)

    def named(*refs):
        kernel(types.SimpleNamespace(**dict(zip(names, refs))))

    results = pl.pallas_call(
        named,
        out_shape=[shape for shape, _ in outs.values()],
        in_specs=[spec for _, spec in ins.values()],
        out_specs=[spec for _, spec in outs.values()],
        scratch_shapes=list(scratch.values()),
        compiler_params=pltpu.CompilerParams(
            vmem_limit_bytes=VMEM_LIMIT, collective_id=collective_id, has_side_effects=True
        ),
    )(*[array for array, _ in ins.values()])
    return types.SimpleNamespace(**dict(zip(outs, results)))


def tiles(*n):
    return pltpu.VMEM(n + (C, TC), BF16)


def dma(n):
    return pltpu.SemaphoreType.DMA((n,))


def numbered(sems, rsems):
    count = [0]

    def new(src, dst, step=None, device=None):
        k = count[0]
        count[0] += 1
        return pltpu.make_async_remote_copy(
            src_ref=src,
            dst_ref=dst,
            send_sem=sems.at[k],
            recv_sem=rsems.at[k],
            device_id=device_at(*step) if device is None else device,
            device_id_type=MESH,
        )

    return new


def rl(value, shift, axis):
    shift %= value.shape[axis]
    return value if shift == 0 else pltpu.roll(value, shift, axis)


def lane_of(shape):
    return lax.broadcasted_iota(jnp.int32, shape, 1)


def dot(a, b):
    return jnp.dot(a, b, preferred_element_type=F32)


def dot_nt(a, b):
    return lax.dot_general(a, b, NT, preferred_element_type=F32)


def pack_cols(row, cols, count=TR):
    total = None
    for y in range(count):
        value = row(y)
        lane = lane_of(value.shape)
        if total is None:
            total = jnp.zeros(value.shape, F32)
        for col, base in cols:
            total = jnp.where(lane == base + y, rl(value, base + y - col, 1), total)
    return total


TWO = [(0, 0), (1, 32), (126, 64), (127, 96)]


def two_cols(first_lane):
    return [(0, first_lane), (127, 64 + first_lane)]


def put_col(total, value, cols, k):
    lane = lane_of(value.shape)
    for col, base in cols:
        total = jnp.where(lane == base + k, rl(value, base + k - col, 1), total)
    return total


def other_side(left, right):
    lane = lane_of(left.shape)
    col = lax.axis_index("col")
    both = jnp.where(lane >= 64, jnp.where(col > 0, left, 0.0), jnp.where(col < NCOL - 1, right, 0.0))
    return rl(both, 64, 1)


def three_tiles(left, own, right):
    low = lane_of(own.shape) < 64
    return [
        jnp.where(low, rl(left, -64, 1), rl(own, -32, 1)),
        jnp.where(low, rl(left, -96, 1), rl(right, 64, 1)),
        jnp.where(low, own, rl(right, 32, 1)),
    ]


def device_at(drow, dcol):
    row = lax.rem(lax.axis_index("row") + drow + NROW, NROW)
    col = lax.rem(lax.axis_index("col") + dcol + NCOL, NCOL)
    return (row, col)


def greet(steps):
    both = sorted(set(steps) | {(-a, -b) for a, b in steps})
    barrier = pltpu.get_barrier_semaphore()
    for step in both:
        pl.semaphore_signal(barrier, inc=1, device_id=device_at(*step), device_id_type=MESH)
    return lambda: pl.semaphore_wait(barrier, len(both))


def start_all(copies):
    for copy in copies:
        copy.start()


def wait_all(copies):
    for copy in copies:
        copy.wait()


def strided(wide, y, channels):
    return wide[pl.ds(y, channels, stride=TR), :]


def build_x3(x3, row, halo, count, channels, first_lane=0):
    for k in range(count):
        value = row(k)
        lane = lane_of(value.shape)
        at = slice(k * TC, (k + 1) * TC)
        left = jnp.where(lane == 0, rl(halo, -(first_lane + k), 1), rl(value, 1, 1))
        right = jnp.where(lane == TC - 1, rl(halo, TC - 1 - (64 + first_lane + k), 1), rl(value, -1, 1))
        x3[0:channels, at] = left.astype(BF16)
        x3[channels : 2 * channels, at] = value.astype(BF16)
        x3[2 * channels : 3 * channels, at] = right.astype(BF16)


def conv_chunk(w_ref, x3, start, width, rows=slice(None)):
    total = None
    depth = x3.shape[0]
    for a in range(3):
        term = dot(w_ref[rows, a * depth : (a + 1) * depth], x3[:, start + a * TC : start + a * TC + width])
        total = term if total is None else total + term
    return total


def offset_of(off, part, row, col):
    return off[part, row, col]


PARTS = 4
WIDE = C // PARTS


def part_of(q):
    return pl.ds(q * WIDE, WIDE)


def padded_place(shape, axis):
    at = lax.broadcasted_iota(jnp.int32, shape, axis)
    tap = jnp.zeros(shape, jnp.int32)
    for t in range(1, 9):
        tap = tap + jnp.where(at >= t * CH, 1, 0)
    rest = at - tap * CH
    b = rest & 15
    return jnp.where(b < 9, tap * 81 + (rest >> 4) * 9 + b, -1)


def one_hot(mask):
    return jnp.where(mask, 1.0, 0.0).astype(BF16)


def padding_matrix():
    place = padded_place((1, 9 * CH), 1)
    return one_hot(lax.broadcasted_iota(jnp.int32, (729, 9 * CH), 0) == place)


def small_weights(r, q):
    if q == 0:
        r.w1[...] = dot(r.w_first[...], padding_matrix()).astype(BF16)
    if q == 1:
        place = padded_place((CH, 1), 0)
        source = lax.broadcasted_iota(jnp.int32, (CH, 729), 1)
        for k in range(9):
            pick = one_hot((source == place + (8 - k) * 81) & (place >= 0))
            r.w1f[:, k * 64 : (k + 1) * 64] = dot_nt(pick, r.w_first[...]).astype(BF16)
    if q == 2:
        target = lax.broadcasted_iota(jnp.int32, (64, 576), 0)
        source = lax.broadcasted_iota(jnp.int32, (64, 576), 1)
        for k in range(9):
            pick = one_hot(source == target + (8 - k) * 64)
            r.w2f[:, k * 32 : (k + 1) * 32] = dot_nt(pick, r.w_second[...]).astype(BF16)


def forward_kernel(r):
    row = lax.axis_index("row")
    col = lax.axis_index("col")
    first = row == 0
    last = row == NROW - 1
    arrived = greet([(1, 0), (0, 1), (0, 2)])
    new = numbered(r.sems, r.rsems)
    wide, wide2, cwide = r.wide, r.wide2, r.cwide

    wide[...] = r.summer[...].astype(F32)
    for k in range(5):
        r.ss[k] = strided(wide, 11 + k, C).astype(BF16)
        r.ss[5 + k] = strided(wide, k, C).astype(BF16)
    arrived()
    stage = [
        new(r.ss.at[pl.ds(0, 5)], r.rs.at[pl.ds(0, 5)], (1, 0)),
        new(r.ss.at[pl.ds(5, 5)], r.rs.at[pl.ds(5, 5)], (-1, 0)),
    ]
    start_all(stage)
    pack_s = pack_cols(lambda y: strided(wide, y, C), two_cols(5))
    wide2[...] = r.winter[...].astype(F32)
    r.sw[0] = strided(wide2, TR - 1, C).astype(BF16)
    r.sw[1] = strided(wide2, 0, C).astype(BF16)
    cwide[...] = r.cot[...].astype(F32)
    for k in range(2):
        r.sc[k] = strided(cwide, 14 + k, 32).astype(BF16)
        r.sc[2 + k] = strided(cwide, k, 32).astype(BF16)
    pack_w = pack_cols(lambda y: strided(wide2, y, C), two_cols(1))
    wait_all(stage)
    other = [
        new(r.sw.at[pl.ds(0, 1)], r.rw.at[pl.ds(0, 1)], (1, 0)),
        new(r.sw.at[pl.ds(1, 1)], r.rw.at[pl.ds(1, 1)], (-1, 0)),
        new(r.sc.at[pl.ds(0, 2)], r.rc.at[pl.ds(0, 2)], (1, 0)),
        new(r.sc.at[pl.ds(2, 2)], r.rc.at[pl.ds(2, 2)], (-1, 0)),
    ]
    start_all(other)
    for k in range(10):
        value = jnp.where(first if k < 5 else last, 0.0, r.rs[k].astype(F32))
        pack_s = put_col(pack_s, value, two_cols(0), k if k < 5 else 16 + k)
    r.ks[...] = pack_s.astype(BF16)
    stage = [new(r.ks, r.is_.at[0], (0, 1)), new(r.ks, r.is_.at[1], (0, -1))]
    start_all(stage)
    pack_c = pack_cols(lambda y: strided(cwide, y, 32), [(c, b + 2) for c, b in TWO])
    wait_all(other)
    for k in range(2):
        value = jnp.where(first if k < 1 else last, 0.0, r.rw[k].astype(F32))
        r.sw2[k] = value.astype(BF16)
        pack_w = put_col(pack_w, value, two_cols(0), 17 * k)
    r.kw[...] = pack_w.astype(BF16)
    for k in range(4):
        value = jnp.where(first if k < 2 else last, 0.0, r.rc[k].astype(F32))
        r.crows[k] = value.astype(BF16)
        pack_c = put_col(pack_c, value, TWO, k if k < 2 else 16 + k)
    r.kc[...] = pack_c.astype(BF16)
    other = [
        new(r.kw, r.iw.at[0], (0, 1)),
        new(r.kw, r.iw.at[1], (0, -1)),
        new(r.kc, r.ic.at[0], (0, 1)),
        new(r.kc, r.ic.at[1], (0, -1)),
    ]
    start_all(other)
    wait_all(stage)

    def summer_row(j):
        if j < 5:
            return jnp.where(first, 0.0, r.rs[j].astype(F32))
        if j >= 21:
            return jnp.where(last, 0.0, r.rs[j - 16].astype(F32))
        return strided(wide, j - 5, C)

    halo = other_side(r.is_[0].astype(F32), r.is_[1].astype(F32))
    build_x3(r.x3s, summer_row, halo, TR + 10, C)
    save_s = pltpu.make_async_copy(r.x3s, r.xs, r.lsem.at[PARTS])
    save_s.start()
    packs = [jnp.zeros((C, TC), F32), jnp.zeros((C, TC), F32)]
    lane = lane_of((C, TC))
    fp = r.fp
    for n in range(6):
        value = conv_chunk(r.weight, r.x3s, n * 512, 512)
        for j in range(4):
            k = n * 4 + j
            part = value[:, j * TC : (j + 1) * TC]
            if k < 4:
                part = jnp.where(first, 0.0, part)
            if k >= 20:
                part = jnp.where(last, 0.0, part)
            fp[k] = part.astype(BF16)
            for p, at in ((0, k), (1, k - 8)):
                if 0 <= at < 16:
                    low = (lane >= at * 8) & (lane < at * 8 + 4)
                    high = (lane >= at * 8 + 4) & (lane < at * 8 + 8)
                    packs[p] = jnp.where(low, rl(part, at * 8, 1), packs[p])
                    packs[p] = jnp.where(high, rl(part, at * 8 + 4 - 124, 1), packs[p])
    fp[24] = packs[0].astype(BF16)
    fp[25] = packs[1].astype(BF16)

    strips = [getattr(r, f"strip{q}") for q in range(PARTS)]
    trios = [getattr(r, f"trio{q}") for q in range(PARTS)]
    pin, cand, psend, ptrio, send_buf = r.pin, r.cand, r.psend, r.ptrio, r.send_buf
    owns = [
        pltpu.make_async_copy(fp.at[pl.ds(0, 24), part_of(q)], strips[q].at[pl.ds(16, 24)], r.lsem.at[q])
        for q in range(PARTS)
    ]
    pstage = [new(fp.at[24], pin.at[0], (1, 0)), new(fp.at[25], pin.at[1], (-1, 0))]
    start_all(pstage)
    stages = []
    for q in range(PARTS):
        cs = part_of(q)
        stages.append(
            [
                new(fp.at[pl.ds(0, 16), cs], strips[q].at[pl.ds(0, 16)], (1, 0)),
                new(fp.at[pl.ds(8, 16), cs], strips[q].at[pl.ds(40, 16)], (-1, 0)),
            ]
        )
    start_all(stages[0])
    start_all(stages[1])
    start_all(owns)
    wait_all(other)
    whalo = other_side(r.iw[0].astype(F32), r.iw[1].astype(F32))
    left = jnp.where(col > 0, r.ic[0].astype(F32), 0.0)
    right = jnp.where(col < NCOL - 1, r.ic[1].astype(F32), 0.0)
    for k, tile in enumerate(three_tiles(left, r.kc[...].astype(F32), right)):
        r.ct[k] = tile.astype(BF16)

    def winter_row(j):
        if j == 0 or j == TR + 1:
            return r.sw2[j // (TR + 1)].astype(F32)
        return strided(wide2, j - 1, C)

    build_x3(r.x3w, winter_row, whalo, TR + 2, C)
    save_w = pltpu.make_async_copy(r.x3w, r.xw, r.lsem.at[PARTS + 1])
    save_w.start()
    wait_all(owns)
    off = r.off

    def pick_of(dcol):
        return offset_of(off, 0, row, lax.rem(col + dcol + NCOL, NCOL)) + 1

    wait_all(pstage)
    low = lane < 64
    p0, p1 = fp[24].astype(F32), fp[25].astype(F32)
    above, below = pin[0].astype(F32), pin[1].astype(F32)
    cand[0, 0] = above.astype(BF16)
    cand[0, 1] = jnp.where(low, p0, 0.0).astype(BF16)
    cand[1, 0] = p0.astype(BF16)
    cand[1, 1] = jnp.where(low, rl(p1, 64, 1), 0.0).astype(BF16)
    cand[2, 0] = rl(jnp.where(low, below, p1), 64, 1).astype(BF16)
    cand[2, 1] = jnp.where(low, rl(below, 64, 1), 0.0).astype(BF16)
    second = []
    for k, dcol in enumerate((-2, -1, 1, 2)):
        pick = pick_of(dcol)
        for j in range(2):
            psend[k, j] = cand[pick, j]
        second.append(new(psend.at[k], ptrio.at[2 - dcol], (0, dcol)))
    start_all(second)
    mine = pick_of(0)
    for j in range(2):
        ptrio[2, j] = cand[mine, j]
    picks = [pick_of(-1), pick_of(1)]
    my_row = row + offset_of(off, 0, row, col)
    my_col = col + offset_of(off, 1, row, col)
    dcol = my_col - col + 1
    thirds = []
    for q in range(PARTS):
        cs = part_of(q)
        wait_all(stages[q])
        if q + 2 < PARTS:
            start_all(stages[q + 2])

        def fill(j, carry, cs=cs, q=q):
            send_buf[0, j, cs] = strips[q][16 * picks[0] + j]
            send_buf[1, j, cs] = strips[q][16 * picks[1] + j]
            return carry

        lax.fori_loop(0, 24, fill, 0)
        third = [
            new(send_buf.at[0, :, cs], trios[q].at[2], (0, -1)),
            new(send_buf.at[1, :, cs], trios[q].at[0], (0, 1)),
        ]
        start_all(third)
        thirds.append(third)

        def keep(j, carry, q=q):
            trios[q][1, j] = strips[q][16 * mine + j]
            return carry

        lax.fori_loop(0, 24, keep, 0)
        for n in range(q * 4 // PARTS, (q + 1) * 4 // PARTS):
            at = slice(n * 512, (n + 1) * 512)
            r.fw[:, at] = conv_chunk(r.weight, r.x3w, n * 512, 512).astype(BF16)
        small_weights(r, q)
    wait_all(second)
    m = r.m
    low = lax.rem(lane, 8) < 4
    for j in range(2):
        right = jnp.where(my_col == NCOL - 1, 0.0, ptrio[dcol + 2, j].astype(F32))
        left = jnp.where(my_col == 0, 0.0, ptrio[dcol, j].astype(F32))
        m[:, (24 + j) * TC : (25 + j) * TC] = jnp.where(low, right, left).astype(BF16)
    for q in range(PARTS):
        wait_all(thirds[q])
        cs = part_of(q)
        for j in range(24):
            m[cs, j * TC : (j + 1) * TC] = trios[q][dcol, j]
    correlate(r.fw, m, r.cv, r.cvpack, r.sums, r.mt, r.rt, r.grim, r.s1, r.s2)
    save_s.wait()
    save_w.wait()


def forward(offsets, summer, winter, cot, weight, w_first, w_second):
    one = lambda c: pltpu.VMEM((c, TC), BF16)
    some = lambda n, c: pltpu.VMEM((n, c, TC), BF16)
    n = 16 + 6 + 4 * PARTS
    scratch = dict(
        wide=pltpu.VMEM((C * TR, TC), F32), wide2=pltpu.VMEM((C * TR, TC), F32), cwide=pltpu.VMEM((32 * TR, TC), F32),
        ss=tiles(10), rs=tiles(10), sw=tiles(2), sw2=tiles(2), rw=tiles(2), sc=some(4, 32), rc=some(4, 32),
        ks=tiles(), kw=tiles(), kc=one(32), is_=tiles(2), iw=tiles(2), ic=some(2, 32),
        x3s=pltpu.VMEM((3 * C, 26 * TC), BF16), x3w=pltpu.VMEM((3 * C, 18 * TC), BF16), fp=tiles(26),
        pin=tiles(2), cand=tiles(3, 2), send_buf=tiles(2, 24), ptrio=tiles(5, 2), psend=tiles(4, 2),
        mt=pltpu.VMEM((24 * TC, C), BF16), rt=pltpu.VMEM((2 * TC, C), BF16), grim=pltpu.VMEM((2 * TC, TR * TC), F32),
        s1=pltpu.VMEM((CH, TC), F32), s2=pltpu.VMEM((CH, TC), F32),
        lsem=dma(PARTS + 2), sems=dma(n), rsems=dma(n),
    )
    for q in range(PARTS):
        scratch[f"strip{q}"] = pltpu.VMEM((56, WIDE, TC), BF16)
        scratch[f"trio{q}"] = pltpu.VMEM((3, 24, WIDE, TC), BF16)
    return call(
        forward_kernel,
        dict(
            off=(offsets, sspec()), summer=(summer, vspec()), winter=(winter, vspec()), cot=(cot, vspec()),
            weight=(weight, vspec()), w_first=(w_first, vspec()), w_second=(w_second, vspec()),
        ),
        dict(
            w1=(sds((64, 9 * CH), BF16), vspec()), w1f=(sds((CH, 576), BF16), vspec()),
            w2f=(sds((64, 288), BF16), vspec()),
            crows=(sds((4, 32, TC), BF16), vspec()), ct=(sds((3, 32, TC), BF16), vspec()),
            xs=(sds((3 * C, 26 * TC), BF16), anyspec()), xw=(sds((3 * C, 18 * TC), BF16), anyspec()),
            fw=(sds((C, TR * TC), BF16), vspec()), m=(sds((C, 26 * TC), BF16), vspec()),
            cv=(sds((TR, CH, TC), F32), vspec()), cvpack=(sds((CH, TC), F32), vspec()),
            sums=(sds((8, 256), F32), vspec()),
        ),
        scratch,
        0,
    )


def bit_off(lane, bit):
    return (lane & bit) == 0


def shear(main, rim):
    low = lane_of((80, TC)) < 64
    w = jnp.where(low, jnp.concatenate([rim, main[0:72]], 0), jnp.concatenate([main[56:128], rim], 0))
    w = jnp.where(bit_off(lane_of((48, TC)), 32), w[0:48], w[32:80])
    w = jnp.where(bit_off(lane_of((32, TC)), 16), w[0:32], w[16:48])
    w = jnp.where(bit_off(lane_of((24, TC)), 8), w[0:24], w[8:32])
    lane = lane_of((16, TC))
    w = jnp.where(bit_off(lane, 4), rl(w, -4, 0)[0:16], w[8:24])
    w = jnp.where(bit_off(lane, 2), w, rl(w, -2, 0))
    w = jnp.where(bit_off(lane, 1), w, rl(w, -1, 0))
    return jnp.where(lax.broadcasted_iota(jnp.int32, (16, TC), 0) < 9, w, 0.0)


def unshear(value):
    lane = lane_of((16, TC))
    w = jnp.where(bit_off(lane, 1), value, rl(value, 1, 0))
    w = jnp.where(bit_off(lane, 2), w, rl(w, 2, 0))
    zeros = lambda n: jnp.zeros((n, TC), F32)
    padded = jnp.concatenate([w, zeros(8)], 0)
    w = jnp.where(bit_off(lane_of((24, TC)), 4), rl(padded, 4, 0), jnp.concatenate([zeros(8), w], 0))
    for n, bit in ((24, 8), (32, 16), (48, 32)):
        w = jnp.where(
            bit_off(lane_of((n + bit, TC)), bit),
            jnp.concatenate([w, zeros(bit)], 0),
            jnp.concatenate([zeros(bit), w], 0),
        )
    low = lambda n: lane_of((n, TC)) < 64
    main = jnp.concatenate(
        [
            jnp.where(low(56), w[8:64], 0.0),
            jnp.where(low(16), w[64:80], w[0:16]),
            jnp.where(low(56), 0.0, w[16:72]),
        ],
        0,
    )
    return main, jnp.where(low(8), w[0:8], w[72:80])


def row_sums(first, second):
    ones = jnp.ones((8, TC), F32)
    a = lax.dot_general(ones, first, NT, precision=lax.Precision.HIGHEST, preferred_element_type=F32)
    b = lax.dot_general(ones, second, NT, precision=lax.Precision.HIGHEST, preferred_element_type=F32)
    return jnp.where(lax.broadcasted_iota(jnp.int32, a.shape, 0) == 0, a, b)


def correlate(fw, m, cv, pack, sums, mt, rt, grim, s1, s2):
    for r in range(24):
        mt[r * TC : (r + 1) * TC, :] = m[:, r * TC : (r + 1) * TC].T
    for q in range(2):
        rt[q * TC : (q + 1) * TC, :] = m[:, (24 + q) * TC : (25 + q) * TC].T
    for n in range(4):
        grim[:, n * 512 : (n + 1) * 512] = dot(rt[...], fw[:, n * 512 : (n + 1) * 512])
    s1[...] = jnp.zeros_like(s1)
    s2[...] = jnp.zeros_like(s2)

    def at_pair(pair, carry):
        feat = fw[:, pl.ds(pl.multiple_of(pair * 2 * TC, 2 * TC), 2 * TC)]
        for t in range(10):
            mains = dot(mt[pl.ds(pl.multiple_of((pair * 2 + t) * TC, TC), TC), :], feat)
            for k in range(2):
                a = t - k
                if a < 0 or a > 8:
                    continue
                y = pair * 2 + k
                lanes = pl.ds(pl.multiple_of(y * TC, TC), TC)
                rim = grim[pl.ds(pl.multiple_of((y + a) * 8, 8), 8), lanes]
                value = shear(mains[:, k * TC : (k + 1) * TC], rim) * 0.0625
                rows = slice(a * 16, (a + 1) * 16)
                cv[y, rows, :] = value
                s1[rows, :] += value
                s2[rows, :] += value * value
        return carry

    lax.fori_loop(0, TR // 2, at_pair, 0)
    pack[...] = pack_cols(lambda y: cv[y], [(c, b + 2) for c, b in TWO])
    sums[...] = jnp.zeros_like(sums)
    sums[:, 0:CH] = row_sums(s1[...], s2[...])


def reduce_one(src, dst, out, send, recv, axis, count):
    copies = []
    for d in range(1, count):
        step = (0, d) if axis == "col" else (d, 0)
        copies.append(
            pltpu.make_async_remote_copy(
                src_ref=src,
                dst_ref=dst.at[d],
                send_sem=send.at[d],
                recv_sem=recv.at[d],
                device_id=device_at(*step),
                device_id_type=MESH,
            )
        )
    start_all(copies)
    dst[0] = src[...]
    wait_all(copies)
    me = lax.axis_index(axis)
    total = None
    for d in range(count):
        value = dst[lax.rem(me - d + count, count)]
        total = value if total is None else total + value
    out[...] = total


RING = [(0, d) for d in range(1, NCOL)] + [(d, 0) for d in range(1, NROW)]


def tile_inside(b, shape):
    lane = lane_of(shape)
    row = lax.axis_index("row")
    col = lax.axis_index("col")
    local = jnp.where(lane < 64, lane, lane - 64)
    y = row * TR - 2 + local
    x = jnp.where(lane < 64, col * TC - 1 + b, col * TC + TC + b)
    return (y >= 0) & (y < NROW * TR) & (x >= 0) & (x < NCOL * TC) & (local < 20)


def rim_patches(tiles, a):
    return jnp.concatenate([rl(t, -a, 1) for t in tiles], 0).astype(BF16)


def silu_parts(value):
    sigma = jax.nn.sigmoid(value)
    return value * sigma, sigma * (1.0 + value * (1.0 - sigma))


def columns(sums):
    turned = sums.T
    return turned[0:CH, 0:1], turned[0:CH, 1:2]


def refine(r, scale, bias, inv, mid):
    row = lax.axis_index("row")
    first = row == 0
    last = row == NROW - 1
    cv, vrows, own_pack, sides, cot, crows, ct = r.cv, r.vrows, r.own_pack, r.sides, r.cot, r.crows, r.ct
    w1, w1f, w2, w2f = r.w1, r.w1f, r.w2, r.w2f
    refined, gpre, gfirst, gsecond, sums = r.refined, r.gpre, r.gfirst, r.gsecond, r.gsums0
    cwide, n3x, c3x, h3, gh3, hpre, gmain = r.cwide, r.n3x, r.c3x, r.h3, r.gh3, r.hpre, r.gmain
    s1, s2, rwide = r.s1, r.s2, r.rwide

    def normed_of(value):
        return silu_parts(value * scale + bias)[0]

    ntiles = [
        jnp.where(tile_inside(b - 1, (CH, TC)), normed_of(t), 0.0) for b, t in enumerate(three_tiles(sides[0], own_pack[...], sides[1]))
    ]

    def nrow(k):
        if k < 2:
            return jnp.where(first, 0.0, normed_of(vrows[k]))
        if k >= 18:
            return jnp.where(last, 0.0, normed_of(vrows[k - 16]))
        return normed_of(cv[k - 2])

    build_x3(n3x, nrow, ntiles[1], 20, CH)
    ctiles = [ct[k].astype(F32) for k in range(3)]
    cwide[...] = cot[...].astype(F32)

    def crow(k):
        if k < 2:
            return crows[k].astype(F32)
        if k >= 18:
            return crows[k - 16].astype(F32)
        return strided(cwide, k - 2, 32)

    build_x3(c3x, crow, ctiles[1], 20, 32)

    def both(w_ref, x3, tiles):
        depth = x3.shape[0]
        rim = None
        for a in range(3):
            term = dot(w_ref[:, a * depth : (a + 1) * depth], rim_patches(tiles, a))
            rim = term if rim is None else rim + term
        return rim

    lane = lane_of((64, TC))
    local = jnp.where(lane < 64, lane, lane - 64)
    ypos = row * TR - 1 + local
    col = lax.axis_index("col")
    xpos = jnp.where(lane < 64, col * TC - 1, col * TC + TC)
    rim_in = (ypos >= 0) & (ypos < NROW * TR) & (local < 18) & (xpos >= 0) & (xpos < NCOL * TC)
    rim_h, rim_slope = silu_parts(both(w1, n3x, ntiles))
    rim_g = both(w2f, c3x, ctiles)
    rim_h = jnp.where(rim_in, rim_h, 0.0)
    rim_g = jnp.where(rim_in, rim_g * rim_slope, 0.0)
    for n in range(6):
        hpre[:, n * 384 : (n + 1) * 384] = conv_chunk(w1, n3x, n * 384, 384)
        gmain[:, n * 384 : (n + 1) * 384] = conv_chunk(w2f, c3x, n * 384, 384)

    def edge(k):
        return first if k == 0 else (last if k == 17 else None)

    def hrow(k):
        value, slope = silu_parts(hpre[:, k * TC : (k + 1) * TC])
        grad = gmain[:, k * TC : (k + 1) * TC] * slope
        gone = edge(k)
        if gone is not None:
            value = jnp.where(gone, 0.0, value)
            grad = jnp.where(gone, 0.0, grad)
        gmain[:, k * TC : (k + 1) * TC] = grad
        return value

    build_x3(h3, hrow, rim_h, 18, 64)
    build_x3(gh3, lambda k: gmain[:, k * TC : (k + 1) * TC], rim_g, 18, 64)
    for n in range(4):
        value = conv_chunk(w2, h3, n * 512, 512)
        for j in range(4):
            rwide[pl.ds(n * 4 + j, 32, stride=TR), :] = value[:, j * TC : (j + 1) * TC]
    refined[...] = rwide[...].astype(BF16)
    own = slice(TC, 17 * TC)
    mine = slice(2 * TC, 18 * TC)
    gfirst[:, 9 * CH :] = jnp.zeros((64, 1408 - 9 * CH), F32)
    gsecond[:, 576:] = jnp.zeros((32, 64), F32)
    for a in range(3):
        gsecond[:, a * 192 : (a + 1) * 192] = dot_nt(c3x[32:64, mine], h3[:, a * TC : (a + 16) * TC])
        gfirst[:, a * 432 : (a + 1) * 432] = dot_nt(gh3[64:128, own], n3x[:, (a + 1) * TC : (a + 17) * TC])
    s1[...] = jnp.zeros_like(s1)
    s2[...] = jnp.zeros_like(s2)
    for n in range(4):
        value = conv_chunk(w1f, gh3, n * 512, 512)
        for j in range(4):
            y = n * 4 + j
            volume = cv[y]
            grad = value[:, j * TC : (j + 1) * TC] * silu_parts(volume * scale + bias)[1]
            gpre[y] = grad
            s1[...] += grad
            s2[...] += grad * (volume * inv - mid)
    sums[...] = jnp.zeros_like(sums)
    sums[:, 0:CH] = row_sums(s1[...], s2[...])


def correlate_back(cv, gpre, coef, fw, m, gfw, gm, kw, q, qrim):
    def at_row(y, carry):
        lanes = pl.ds(pl.multiple_of(y * TC, TC), TC)
        grad = coef[0] * gpre[y] + coef[1] + coef[2] * cv[y]
        grad = grad.astype(BF16).astype(F32)
        for a in range(9):
            main, rim = unshear(grad[a * 16 : (a + 1) * 16])
            q[pl.ds(pl.multiple_of((y + a) * TC, TC), TC), lanes] = main.astype(BF16)
            qrim[pl.ds(pl.multiple_of((y + a) * 8, 8), 8), lanes] = rim
        return carry

    qrim[...] = jnp.zeros_like(qrim)
    for y in range(TR):
        for p in (y - 1, y + 9):
            if 0 <= p < 24:
                q[p * TC : (p + 1) * TC, y * TC : (y + 1) * TC] = jnp.zeros((TC, TC), BF16)
    lax.fori_loop(0, TR, at_row, 0)
    for y in range(0, TR, 2):
        at = slice(y * TC, (y + 2) * TC)
        value = dot(m[:, y * TC : (y + 10) * TC], q[y * TC : (y + 10) * TC, at])
        value = value + dot(m[:, 24 * TC : 26 * TC], qrim[:, at].astype(BF16))
        gfw[:, at] = (value * 0.0625).astype(BF16)
    for p in range(0, 24, 2):
        at = slice(max(0, p - 8) * TC, (min(15, p + 1) + 1) * TC)
        value = dot_nt(fw[:, at], q[p * TC : (p + 2) * TC, at]) * 0.0625
        for k in range(2):
            gm[p + k] = value[:, k * TC : (k + 1) * TC].astype(BF16)
    kw[...] = pack_cols(lambda y: gfw[:, y * TC : (y + 1) * TC].astype(F32), two_cols(1)).astype(BF16)
    for k in range(2):
        value = dot_nt(fw[...], qrim[k * TC : (k + 1) * TC, :].astype(BF16))
        gm[24 + k] = (value * 0.0625).astype(BF16)


def middle_kernel(r):
    arrived = greet(RING)
    new = numbered(r.sems, r.rsems)
    arrived()
    rows = [
        new(r.cv.at[pl.ds(14, 2)], r.vrows.at[pl.ds(0, 2)], (1, 0)),
        new(r.cv.at[pl.ds(0, 2)], r.vrows.at[pl.ds(2, 2)], (-1, 0)),
    ]
    start_all(rows)
    reduce_one(r.sums, r.gcol, r.total, r.csend, r.crecv, "col", NCOL)
    wait_all(rows)
    pack = r.cvpack[...]
    for k in range(4):
        pack = put_col(pack, r.vrows[k], TWO, k if k < 2 else 16 + k)
    r.own_pack[...] = pack
    cols = [new(r.own_pack, r.sides.at[0], (0, 1)), new(r.own_pack, r.sides.at[1], (0, -1))]
    start_all(cols)
    reduce_one(r.total, r.grow, r.total2, r.rsend, r.rrecv, "row", NROW)
    wait_all(cols)
    sum1, sum2 = columns(r.total2[...])
    mean = sum1 / PIXELS
    inv = lax.rsqrt(sum2 / PIXELS - mean * mean + 1e-05)
    shape = (CH, TC)
    spread = jnp.where(
        lax.broadcasted_iota(jnp.int32, (CH, 81), 1) == padded_place((CH, 1), 0), 1.0, 0.0
    )
    gain, shift = (jnp.sum(spread * ref[...].reshape(1, 81), axis=1, keepdims=True) for ref in (r.gain, r.shift))
    scale = jnp.broadcast_to(gain * inv, shape)
    mid = jnp.broadcast_to(mean * inv, shape)
    inv = jnp.broadcast_to(inv, shape)
    refine(r, scale, shift - mean * scale, inv, mid)
    reduce_one(r.gsums0, r.gcol2, r.total3, r.csend2, r.crecv2, "col", NCOL)
    reduce_one(r.total3, r.grow2, r.gsums, r.rsend2, r.rrecv2, "row", NROW)
    grad_shift, grad_gain = columns(r.gsums[...])
    narrow = jnp.where(
        lax.broadcasted_iota(jnp.int32, (81, CH), 0) == padded_place((1, CH), 1), 1.0, 0.0
    )
    r.gnorm[...] = lax.dot_general(
        r.gsums[:, 0:CH], narrow, NT, precision=lax.Precision.HIGHEST, preferred_element_type=F32
    )
    slope = -scale * grad_gain / PIXELS
    coef = (scale, -scale * grad_shift / PIXELS - slope * mid, slope * inv)
    correlate_back(r.cv, r.gpre, coef, r.fw, r.m, r.gfw, r.gm, r.gkw, r.q, r.qrim)


def middle(fore, cot, gain, shift, w2):
    f32 = lambda *n: pltpu.VMEM(n, F32)
    bf16 = lambda *n: pltpu.VMEM(n, BF16)
    return call(
        middle_kernel,
        {
            name: (array, vspec())
            for name, array in dict(
                cv=fore.cv, cvpack=fore.cvpack, sums=fore.sums, crows=fore.crows, ct=fore.ct, fw=fore.fw, m=fore.m,
                cot=cot, gain=gain, shift=shift, w1=fore.w1, w1f=fore.w1f, w2=w2, w2f=fore.w2f,
            ).items()
        },
        {
            name: (sds(shape, kind), vspec())
            for name, shape, kind in (
                ("refined", (32 * TR, TC), BF16),
                ("gfirst", (64, 1408), F32),
                ("gsecond", (32, 640), F32),
                ("gnorm", (8, 81), F32),
                ("gfw", (C, TR * TC), BF16),
                ("gm", (26, C, TC), BF16),
                ("gkw", (C, TC), BF16),
            )
        },
        dict(
            vrows=f32(4, CH, TC), own_pack=f32(CH, TC), sides=f32(2, CH, TC),
            gcol=f32(NCOL, 8, 256), grow=f32(NROW, 8, 256), total=f32(8, 256), total2=f32(8, 256),
            gcol2=f32(NCOL, 8, 256), grow2=f32(NROW, 8, 256), gsums0=f32(8, 256), gsums=f32(8, 256), total3=f32(8, 256),
            cwide=f32(32 * TR, TC), n3x=bf16(3 * CH, 20 * TC), c3x=bf16(96, 20 * TC), h3=bf16(192, 18 * TC),
            gh3=bf16(192, 18 * TC), hpre=f32(64, 18 * TC), gmain=f32(64, 18 * TC), s1=f32(CH, TC), s2=f32(CH, TC),
            rwide=f32(32 * TR, TC), gpre=f32(TR, CH, TC), q=bf16(24 * TC, TR * TC), qrim=f32(2 * TC, TR * TC),
            sems=dma(4), rsems=dma(4),
            csend=dma(NCOL), crecv=dma(NCOL), rsend=dma(NROW), rrecv=dma(NROW),
            csend2=dma(NCOL), crecv2=dma(NCOL), rsend2=dma(NROW), rrecv2=dma(NROW),
        ),
        1,
    )


TILES = 384
HALF = TILES // 2
FIRST = 128
SHARE = FIRST // 4


def feat_tile(t, g):
    return (g // 8) * HALF + t * 8 + g % 8


def first_tile(t, g):
    return (g // 2) * HALF + 144 + t * 2 + g % 2


def second_tile(t, g):
    return g * HALF + 166 + t


def final_kernel(r):
    row = lax.axis_index("row")
    col = lax.axis_index("col")
    core = lax.rem(col, 2)
    chip = lax.div(col, 2)
    off, gm, gfw = r.off, r.gm, r.gfw
    trios = [getattr(r, f"trio{q}") for q in range(PARTS)]
    ptrio, strip, be, ab, pout, pin, g24, g5 = r.ptrio, r.strip, r.be, r.ab, r.pout, r.pin, r.g24, r.g5
    pab, pq, pack, side, rw, kw, iw, kw0 = r.pab, r.pq, r.pack, r.side, r.rw, r.kw, r.iw, r.gkw
    ext, wrows, buf, half_in, half, y_in = r.ext, r.wrows, r.buf, r.half_in, r.half, r.y_in
    share, row_in, full, x3, wide, flipped = r.share, r.row_in, r.full, r.x3, r.wide, r.flipped
    xw, xs = r.xw_here, r.xs_here
    arrived = greet(RING)
    loads = [
        pltpu.make_async_copy(r.xw, xw, r.lsem.at[PARTS]),
        pltpu.make_async_copy(r.xs, xs, r.lsem.at[PARTS + 1]),
    ]
    owns = [
        pltpu.make_async_copy(gm.at[pl.ds(0, 24), part_of(q)], trios[q].at[1, pl.ds(0, 24)], r.lsem.at[q])
        for q in range(PARTS)
    ]
    start_all(owns)
    start_all(loads)
    new = numbered(r.sems, r.rsems)
    for t in range(11):
        for g in range(4):
            buf[first_tile(t, g)] = r.gfirst[g * 16 : (g + 1) * 16, t * TC : (t + 1) * TC].astype(BF16)
    for t in range(5):
        for g in range(2):
            buf[second_tile(t, g)] = r.gsecond[g * 16 : (g + 1) * 16, t * TC : (t + 1) * TC].astype(BF16)
    for h in range(2):
        for t in range(171, HALF):
            buf[h * HALF + t] = jnp.zeros((16, TC), BF16)
    partner = (row, col + 1 - 2 * core)
    pairs = [
        new(buf.at[pl.ds(HALF * (1 - core) + 48 * p, 48)], half_in.at[pl.ds(48 * p, 48)], device=partner)
        for p in range(4)
    ]
    arrived()
    pstage = [new(gm.at[pl.ds(24, 2)], ptrio.at[0], (0, 1)), new(gm.at[pl.ds(24, 2)], ptrio.at[2], (0, -1))]
    wstage = [
        new(gfw.at[:, pl.ds((TR - 1) * TC, TC)], rw.at[0], (1, 0)),
        new(gfw.at[:, pl.ds(0, TC)], rw.at[1], (-1, 0)),
    ]
    start_all(pstage + wstage)
    start_all(pairs[3:])
    stages = []
    for q in range(PARTS):
        cs = part_of(q)
        stages.append(
            [
                new(gm.at[pl.ds(0, 24), cs], trios[q].at[0, pl.ds(0, 24)], (0, 1)),
                new(gm.at[pl.ds(0, 24), cs], trios[q].at[2, pl.ds(0, 24)], (0, -1)),
            ]
        )
    start_all(stages[0])
    start_all(stages[1])
    for q in range(PARTS):
        for k in range(3):
            trios[q][k, 24] = jnp.zeros((WIDE, TC), BF16)
    for k in range(9):
        flipped[:, k * C : (k + 1) * C] = r.weight[:, (8 - k) * C : (9 - k) * C].T
    wait_all(owns)
    sources = []
    for k in range(3):
        place = col + k - 1
        there = lax.rem(place + NCOL, NCOL)
        drow = offset_of(off, 0, row, there)
        dcol = offset_of(off, 1, row, there)
        good = (dcol == 1 - k) & (place >= 0) & (place < NCOL)
        sources.append((drow, good))

    first, last = row == 0, row == NROW - 1
    zero = jnp.zeros((C, TC), F32)
    lane = lane_of((C, TC))
    low = lane < 64

    def only(flag, ref):
        return jnp.where(flag, ref.astype(F32), 0.0)

    wait_all(pstage)
    to_above, own0, own1, to_below = zero, zero, zero, zero
    for k, (drow, good) in enumerate(sources):
        t0, t1 = (gm[24], gm[25]) if k == 1 else (ptrio[k, 0], ptrio[k, 1])
        t0, t1 = t0.astype(F32), jnp.where(low, t1.astype(F32), 0.0)
        up, level, down = (good & (drow == v) for v in (-1, 0, 1))
        turned0, turned1 = rl(t0, 64, 1), rl(t1, 64, 1)
        to_above += jnp.where(up, t0, 0.0)
        own0 += jnp.where(up, t1, 0.0) + jnp.where(level, t0, 0.0)
        own1 += jnp.where(level, turned1, 0.0) + jnp.where(down & jnp.logical_not(low), turned0, 0.0)
        to_below += jnp.where(down, turned1 + jnp.where(low, turned0, 0.0), 0.0)
    pout[0] = to_above.astype(BF16)
    pout[1] = to_below.astype(BF16)
    pstage = [new(pout.at[0], pin.at[0], (-1, 0)), new(pout.at[1], pin.at[1], (1, 0))]
    start_all(pstage)

    wait_all(wstage)
    kpack = kw0[...].astype(F32)
    for k in range(2):
        value = only(jnp.logical_not(first if k == 0 else last), rw[k])
        wrows[k] = value.astype(BF16)
        kpack = put_col(kpack, value, two_cols(0), 17 * k)
    kw[...] = kpack.astype(BF16)
    wstage = [new(kw, iw.at[0], (0, 1)), new(kw, iw.at[1], (0, -1))]
    start_all(wstage)

    thirds = []
    for q in range(PARTS):
        cs = part_of(q)
        wait_all(stages[q])
        if q + 2 < PARTS:
            start_all(stages[q + 2])

        def gather(p, carry, cs=cs, q=q):
            total = None
            for k, (drow, good) in enumerate(sources):
                j = p - 16 * (drow + 1)
                fits = good & (j >= 0) & (j < 24)
                value = trios[q][k, jnp.where(fits, j, 24)].astype(F32)
                total = value if total is None else total + value
            strip[p, cs] = total.astype(BF16)
            return carry

        lax.fori_loop(0, 56, gather, 0)
        third = [
            new(strip.at[pl.ds(0, 16), cs], be.at[:, cs], (-1, 0)),
            new(strip.at[pl.ds(40, 16), cs], ab.at[:, cs], (1, 0)),
        ]
        start_all(third)
        thirds.append(third)
        if q == 0:
            wait_all(loads)
        if q < 3:
            for n in range(3):
                part = slice(n * C, (n + 1) * C)
                at = slice(q * 768 + n * C, q * 768 + (n + 1) * C)
                r.gfeat[:, at] = dot_nt(gfw[...], xw[part, q * TC : (q + 16) * TC])
    wait_all(wstage)
    whalo = other_side(iw[0].astype(F32), iw[1].astype(F32))
    wait_all(pstage)
    not_first, not_last = row > 0, row < NROW - 1
    p0 = own0 + only(not_last, pin[0])
    p1 = own1 + only(not_first, pin[1])
    tile_a = p0 + jnp.where(low, 0.0, rl(p1, 64, 1))
    tile_b = jnp.where(low, rl(p1, 64, 1), 0.0)
    pab[0] = tile_a.astype(BF16)
    pab[1] = tile_b.astype(BF16)
    fourth = [new(pab.at[0], pq.at[0], (-1, 0)), new(pab.at[1], pq.at[1], (1, 0))]
    start_all(fourth)

    def w_row(k):
        if k == 0 or k == TR + 1:
            return wrows[k // (TR + 1)].astype(F32)
        return gfw[:, (k - 1) * TC : k * TC].astype(F32)

    build_x3(x3, w_row, whalo, TR + 2, C)

    def last_conv(n):
        value = conv_chunk(flipped, x3, n * 512, 512)
        for j in range(4):
            wide[pl.ds(n * 4 + j, C, stride=TR), :] = value[:, j * TC : (j + 1) * TC]

    for q in range(PARTS):
        cs = part_of(q)
        wait_all(thirds[q])
        for k in range(24):
            total = strip[16 + k, cs].astype(F32)
            if k < 16:
                total = total + only(not_last, be[k, cs])
            if k >= 8:
                total = total + only(not_first, ab[k - 8, cs])
            g24[k, cs] = total.astype(BF16)
        more = [
            new(g24.at[pl.ds(0, 5), cs], g5.at[1, :, cs], (-1, 0)),
            new(g24.at[pl.ds(19, 5), cs], g5.at[0, :, cs], (1, 0)),
        ]
        start_all(more)
        fourth = fourth + more
        for n in range(q * 4 // PARTS, (q + 1) * 4 // PARTS):
            last_conv(n)
    r.out_w[...] = wide[...].astype(BF16)
    wait_all(fourth)
    tile_a = tile_a + jnp.where((lane >= 24) & (lane < 64), only(not_first, pq[1]), 0.0)
    tile_b = tile_b + jnp.where(lane < 40, only(not_last, pq[0]), 0.0)
    pack[0] = tile_a.astype(BF16)
    pack[1] = tile_b.astype(BF16)
    total = zero
    for k in range(18):
        value = g24[k + 3].astype(F32)
        if k < 5:
            value = value + only(not_first, g5[0, k])
        if k >= 13:
            value = value + only(not_last, g5[1, k - 13])
        if k == 0:
            value = only(not_first, value)
        if k == 17:
            value = only(not_last, value)
        strip[k] = value.astype(BF16)
        total = put_col(total, value, two_cols(0), k)
    pack[2] = total.astype(BF16)
    stage = [new(pack, side.at[0], (0, 1)), new(pack, side.at[1], (0, -1))]
    start_all(stage)
    source = lax.broadcasted_iota(jnp.int32, (2 * TC, TC), 0)
    target = lax.broadcasted_iota(jnp.int32, (2 * TC, TC), 1)
    take = ((target < 18) & (source == (target + 3) * 8 + 7)) | (
        (target >= 64) & (target < 82) & (source == (target - 61) * 8)
    )
    rims = dot(pack[0], take[0:TC].astype(F32).astype(BF16)) + dot(pack[1], take[TC:].astype(F32).astype(BF16))
    wait_all(stage)
    halo = other_side(side[0, 2].astype(F32), side[1, 2].astype(F32))
    halo = halo + jnp.where(low, only(col > 0, rims), only(col < NCOL - 1, rims))
    at = jnp.where(low, lane, lane - 64)
    gone = (first & (at == 0)) | (last & (at == 17))
    shalo = jnp.where(gone, 0.0, halo)
    for k in range(18):
        p, base = ((0, (k + 3) * 8) if k + 3 < 16 else (1, (k - 13) * 8))
        value = strip[k].astype(F32)
        left = rl(only(col > 0, side[0, p]), -base, 1)
        right = rl(only(col < NCOL - 1, side[1, p]), 120 - base, 1)
        extra = jnp.where(lane < 4, left, 0.0) + jnp.where(lane >= 124, right, 0.0)
        if k == 0:
            extra = only(not_first, extra)
        if k == 17:
            extra = only(not_last, extra)
        ext[:, k * TC : (k + 1) * TC] = (value + extra).astype(BF16)
    for a in range(3):
        at = slice((a + 4) * TC, (a + 20) * TC)
        for n in range(3):
            part = slice(n * C, (n + 1) * C)
            into = slice(a * 768 + n * C, a * 768 + (n + 1) * C)
            value = r.gfeat[:, into] + dot_nt(ext[:, TC : 17 * TC], xs[part, at])
            value = value.astype(BF16)
            for t in range(2):
                for g in range(16):
                    buf[feat_tile(a * 6 + n * 2 + t, g)] = value[g * 16 : (g + 1) * 16, t * TC : (t + 1) * TC]
        start_all(pairs[a : a + 1])
    wait_all(pairs)

    def add_half(k, carry):
        half[k] = (buf[HALF * core + k].astype(F32) + half_in[k].astype(F32)).astype(BF16)
        return carry

    lax.fori_loop(0, HALF, add_half, 0)
    copies = []
    for d in range(1, 4):
        there = lax.rem(chip + d, 4)
        copies.append(new(half.at[pl.ds(SHARE * there, SHARE)], y_in.at[d - 1], device=(row, 2 * there + core)))
    for d in range(1, NROW):
        there = lax.rem(row + d, NROW)
        copies.append(new(half.at[pl.ds(FIRST + 4 * there, 4)], row_in.at[d - 1], device=(there, col)))
    start_all(copies)
    build_x3(x3, lambda k: ext[:, k * TC : (k + 1) * TC].astype(F32), shalo, TR + 2, C)
    last_conv(0)
    wait_all(copies)

    def add_share(k, carry):
        total = half[SHARE * chip + k].astype(F32)
        for d in range(3):
            total = total + y_in[d, k].astype(F32)
        share[k] = total.astype(BF16)
        return carry

    lax.fori_loop(0, SHARE, add_share, 0)
    for k in range(4):
        total = half[FIRST + 4 * row + k].astype(F32)
        for d in range(NROW - 1):
            total = total + row_in[d, k].astype(F32)
        r.part_b[k] = total.astype(BF16)
    copies = []
    for d in range(1, NROW):
        there = lax.rem(row + d, NROW)
        copies.append(new(share.at[pl.ds(2 * there, 2)], r.a_in.at[d - 1], device=(there, col)))
    for d in range(1, 4):
        there = lax.rem(chip + d, 4)
        copies.append(new(r.part_b.at[pl.ds(there, 1)], r.b_in.at[d - 1], device=(row, 2 * there + core)))
    start_all(copies)
    last_conv(1)
    r.padding[...] = padding_matrix()
    wait_all(copies)
    spot_a = HALF * core + SHARE * chip
    spot_b = HALF * core + FIRST + 4 * row
    for k in range(2):
        total = share[2 * row + k].astype(F32)
        for d in range(NROW - 1):
            total = total + r.a_in[d, k].astype(F32)
        full[spot_a + 2 * row + k] = total.astype(BF16)
    total = r.part_b[chip].astype(F32)
    for d in range(3):
        total = total + r.b_in[d, 0].astype(F32)
    full[spot_b + chip] = total.astype(BF16)

    def spread_along(mine, rows):
        if rows:
            return [new(mine, mine, device=(lax.rem(row + d, NROW), col)) for d in range(1, NROW)]
        return [new(mine, mine, device=(row, 2 * lax.rem(chip + d, 4) + core)) for d in range(1, 4)]

    copies = spread_along(full.at[pl.ds(spot_a + 2 * row, 2)], True)
    copies += spread_along(full.at[pl.ds(spot_b + chip, 1)], False)
    start_all(copies)
    last_conv(2)
    wait_all(copies)
    copies = spread_along(full.at[pl.ds(spot_a, SHARE)], False)
    copies += spread_along(full.at[pl.ds(spot_b, 4)], True)
    start_all(copies)
    last_conv(3)
    r.out_s[...] = wide[...].astype(BF16)
    wait_all(copies)
    mine = full.at[pl.ds(HALF * core, HALF)]
    pair = new(mine, mine, device=partner)
    pair.start()
    pair.wait()
    for t in range(18):
        for g in range(16):
            r.feat_out[g * 16 : (g + 1) * 16, t * TC : (t + 1) * TC] = full[feat_tile(t, g)]
    for t in range(11):
        for g in range(4):
            r.firstb[g * 16 : (g + 1) * 16, t * TC : (t + 1) * TC] = full[first_tile(t, g)]
    r.first_out[...] = dot_nt(r.firstb[:, 0 : 9 * CH], r.padding[...])
    for t in range(5):
        width = TC if t < 4 else 64
        for g in range(2):
            r.second_out[g * 16 : (g + 1) * 16, t * TC : t * TC + width] = full[second_tile(t, g)][:, :width].astype(F32)


def final(offsets, fore, mid, weight):
    small = lambda *n: pltpu.VMEM(n + (16, TC), BF16)
    n = 14 + 6 * PARTS + 5 + 4 * (NROW - 1 + 3)
    scratch = dict(
        ptrio=tiles(3, 2), strip=tiles(56), be=tiles(16), ab=tiles(16), pout=tiles(2), pin=tiles(2), g24=tiles(24),
        g5=tiles(2, 5), pab=tiles(2), pq=tiles(2), pack=tiles(3), side=tiles(2, 3), rw=tiles(2), kw=tiles(), iw=tiles(2),
        wrows=tiles(2), ext=pltpu.VMEM((C, 18 * TC), BF16), flipped=pltpu.VMEM((C, 9 * C), BF16),
        gfeat=pltpu.VMEM((C, 9 * C), F32), x3=pltpu.VMEM((3 * C, 18 * TC), BF16), wide=pltpu.VMEM((C * TR, TC), F32),
        xw_here=pltpu.VMEM((3 * C, 18 * TC), BF16), xs_here=pltpu.VMEM((3 * C, 26 * TC), BF16),
        buf=small(TILES), half_in=small(HALF), half=small(HALF), y_in=small(3, SHARE), share=small(SHARE),
        row_in=small(NROW - 1, 4), a_in=small(NROW - 1, 2), b_in=small(3, 1), part_b=small(4), full=small(TILES),
        firstb=pltpu.VMEM((64, 1408), BF16), padding=pltpu.VMEM((729, 9 * CH), BF16),
        lsem=dma(PARTS + 2), sems=dma(n), rsems=dma(n),
    )
    for q in range(PARTS):
        scratch[f"trio{q}"] = pltpu.VMEM((3, 25, WIDE, TC), BF16)
    return call(
        final_kernel,
        dict(
            off=(offsets, sspec()), gm=(mid.gm, vspec()), gfw=(mid.gfw, vspec()), gkw=(mid.gkw, vspec()),
            gfirst=(mid.gfirst, vspec()), gsecond=(mid.gsecond, vspec()), weight=(weight, vspec()),
            xw=(fore.xw, anyspec()), xs=(fore.xs, anyspec()),
        ),
        dict(
            out_w=(sds((C * TR, TC), BF16), vspec()), out_s=(sds((C * TR, TC), BF16), vspec()),
            feat_out=(sds((C, 9 * C), BF16), vspec()), first_out=(sds((64, 729), F32), vspec()),
            second_out=(sds((32, 576), F32), vspec()),
        ),
        scratch,
        2,
    )


def body(winter, summer, offsets, feat_weight, bn_gain, bn_shift, w_first, w_second, cotangent):
    cot = cotangent.reshape(32 * TR, TC)
    fore = forward(offsets, summer.reshape(C * TR, TC), winter.reshape(C * TR, TC), cot, feat_weight, w_first, w_second)
    mid = middle(fore, cot, bn_gain, bn_shift, w_second)
    last = final(offsets, fore, mid, feat_weight)
    return (
        mid.refined.reshape(32, TR, TC),
        last.out_w.reshape(C, TR, TC),
        last.out_s.reshape(C, TR, TC),
        last.feat_out.astype(F32),
        last.first_out,
        last.second_out,
        mid.gnorm[1],
        mid.gnorm[0],
    )


def solution(mesh):
    tile = P(None, "row", "col")
    return jax.shard_map(
        body,
        mesh=mesh,
        in_specs=(tile, tile, P(), P(), P(), P(), P(), P(), tile),
        out_specs=(tile, tile, tile, P(), P(), P(), P(), P()),
        check_vma=False,
    )
```
